32 devices in a mesh: group: 2 (over x), patch: 8 (over z, y), expert: 2 (over core).
Axes of the slice: x: 2, y: 2, z: 4, core: 2. Of those that a mesh axis runs over, the one named last changes fastest.
Arguments:
- queries: bfloat16 [2048, 1792], P(('group', 'patch'), 'expert'), parts along dimension 0, may hold values from -8 to 8
- fresh_keys: bfloat16 [2048, 1792], P(('group', 'patch'), 'expert'), parts along dimension 0, may hold values from -6 to 6
- fresh_values: bfloat16 [2048, 1792], P(('group', 'patch'), 'expert'), parts along dimension 0, may hold values from -6 to 6
- stale_keys: bfloat16 [2048, 1792], P(('group', 'patch'), 'expert'), parts along dimension 0, may hold values from -8 to 8
- stale_values: bfloat16 [2048, 1792], P(('group', 'patch'), 'expert'), parts along dimension 0, may hold values from -6 to 6
- residual: bfloat16 [2048, 1792], P(('group', 'patch', 'expert')), parts along dimension 0, may hold values from -40 to 40
- out_weight: bfloat16 [1792, 1792], P('expert'), may hold values from -0.125 to 0.125
- modulation: float32 [4, 1792], P('group'), parts along dimension 0, may hold values from -3 to 3
- up_weight: bfloat16 [16, 1792, 3584], P(('patch', 'expert')), may hold values from -0.125 to 0.125
- down_weight: bfloat16 [16, 3584, 1792], P(('patch', 'expert')), may hold values from -0.09375 to 0.09375
- routes: int32 [2048, 2], P(('group', 'patch', 'expert')), parts along dimension 0, may hold values from 0 to 15, all different within a row; in each aligned block of 64 rows (0 to 63, 64 to 127, ...) at most 16 rows name the same one
- gates: float32 [2048, 2], P(('group', 'patch', 'expert')), parts along dimension 0, may hold values from 0.2 to 1
Outputs:
- mixed: bfloat16 [2048, 1792], P(('group', 'patch', 'expert')), parts along dimension 0
The draws below stay inside these ranges and needn't reach their ends.
There are 2 independent parts, one for each index of `group`. The reference program is written for one: setup_inputs(seed, part) draws one part's arguments, and reference() takes and returns one part's arrays. A program takes and returns all parts, laid end to end along the dimension named above; an argument that names none is the same for every part. Nothing has to cross between parts.
Inputs may be any that keep to these rules, and one draw needn't show every extreme that they name: `routes`: each row names 2 different experts; within an aligned block of 64 rows (the rows of one device) no expert is named by more than 16 rows, and in some blocks one is named by exactly 16.
All inputs are finite; a program needn't handle non-finite values.
Results may differ from the reference program's by a relative error of at most 0.0045.
Values may be sent and summed in bfloat16 or wider, within the bound.
No kernel may reach another device: no remote copies, remote signals or barrier semaphores. Data moves between devices by JAX's collectives and lax.ppermute only.
A program may use at most 128 MiB of HBM per device.

```python
import math
import jax
import jax.numpy as jnp
import numpy as np
from jax import lax

D = 1792
HEADS = 16
HEAD_DIM = 112
FF = 3584
EXPERTS = 16
TOPK = 2
TOK_DEV = 128
SEQ = 1024
ROWS = 64
CAP = 16
WSPLIT = 1
FW = 3584
N_PATCH = 8
N_EXPERT = 2


def draw_queries(key, part):
    key = jax.random.fold_in(key, 1)
    entries = jnp.clip(jax.random.normal(key, (SEQ, D), jnp.float32), -6.0, 6.0)
    return entries.astype(jnp.bfloat16)


def draw_stale_keys(key, part):
    key = jax.random.fold_in(key, 2)
    entries = jnp.clip(jax.random.normal(key, (SEQ, D), jnp.float32), -6.0, 6.0)
    return entries.astype(jnp.bfloat16)


def draw_residual(key, part):
    key = jax.random.fold_in(key, 3)
    base_key, row_key, column_key = jax.random.split(key, 3)
    row_scale = jnp.exp(jax.random.uniform(row_key, (SEQ, 1), jnp.float32, jnp.log(0.3), jnp.log(3.0)))
    column_scale = jnp.exp(jax.random.uniform(column_key, (1, D), jnp.float32, jnp.log(0.3), jnp.log(3.0)))
    entries = jnp.clip(jax.random.normal(base_key, (SEQ, D), jnp.float32), -4.0, 4.0) * row_scale * column_scale
    return entries.astype(jnp.bfloat16)


def steps_of(rng, shape, shards, smallest, high):
    def one(dim, shards_of):
        steps = jax.random.uniform(jax.random.fold_in(jax.random.fold_in(rng, 6), dim), (shards_of,), jnp.float32, smallest / len(shards), high / len(shards))
        return jnp.repeat(jnp.exp(steps), shape[dim] // shards_of).reshape((-1,) + (1,) * (len(shape) - dim - 1))

    gain = one(*shards[0])
    for cut in shards[1:]:
        gain = gain * one(*cut)
    return gain


def routed_block(key, own, number, rows, amount, top, limit, slope):
    order = jax.random.permutation(key, amount)
    heavy_load, ordinary = portions_of(amount, rows * top, limit, slope, True), portions_of(amount, rows * top, limit, slope, False)
    places = jnp.arange(amount)

    def named(tallies, offset_by):
        used = int((tallies > 0).sum())
        fixed = max(1, used // 4)
        shifted = fixed + (places - fixed + offset_by * (used - fixed)) % max(1, amount - fixed)
        return jnp.zeros((amount,), jnp.int32).at[order[jnp.where(places < fixed, places, shifted)]].set(jnp.asarray(tallies, jnp.int32))

    tallies = jnp.where(number % 4 == 0, named(heavy_load, number // 4), named(ordinary, number - number // 4 - 1))
    mixed = jax.random.permutation(jax.random.fold_in(own, 3), amount)
    source_of, taker = mixed[0:amount // 2 * 2:2], mixed[1:amount // 2 * 2:2]
    room = jnp.minimum(tallies[source_of] - 1, limit - tallies[taker]) // 2
    room = jnp.where((source_of == order[0]) | (taker == order[0]) | (tallies[taker] == 0), 0, jnp.maximum(room, 0))
    shifted = jax.random.randint(jax.random.fold_in(own, 4), (amount // 2,), 0, 1 << 20) % (room + 1)
    tallies = tallies.at[source_of].add(-shifted).at[taker].add(shifted)
    items = jnp.searchsorted(jnp.cumsum(tallies), jnp.arange(rows * top), side="right").astype(jnp.int32)
    table = items.reshape(top, rows).T
    table = table[jax.random.permutation(jax.random.fold_in(own, 1), rows)]
    offset_by = jax.random.randint(jax.random.fold_in(own, 2), (rows, 1), 0, top)
    return jnp.take_along_axis(table, (jnp.arange(top)[None, :] + offset_by) % top, axis=1)


def portions_of(number_of, total, most, lean, full):
    portions = [(1 << 20) // math.isqrt(rank ** lean) + 1 for rank in range(1, number_of + 1)]
    largest = most if full else min(most, max(-(-total // number_of), total * portions[0] // sum(portions)))
    least = 1 if total - largest >= number_of - 1 else 0
    given, surplus = [largest] + [least] * (number_of - 1), total - largest - least * (number_of - 1)
    while surplus > 0:
        movable = [i for i in range(1, number_of) if given[i] < largest] or [i for i in range(1, number_of) if given[i] < most]
        pool, left = sum([portions[i] for i in movable]), surplus
        for i in movable:
            addition = min(most - given[i], max(1, left * portions[i] // pool), surplus)
            given[i] = given[i] + addition
            surplus = surplus - addition
    return np.array(given)


def scatter_about(key, shape, width, reach, cuts=(), kind=jnp.bfloat16):
    result = width * jax.random.normal(key, shape, jnp.float32)
    if cuts:
        result = result * steps_of(key, shape, cuts, -0.22, 0.18)
    return jnp.clip(result, -reach, reach).astype(kind)


def setup_inputs(seed: int = 0, part: int = 0) -> dict:
    arg_keys = jax.random.split(jax.random.key(seed), 13)
    part_keys = jax.random.split(jax.random.fold_in(arg_keys[12], part), 13)
    queries = draw_queries(jax.random.fold_in(jax.random.fold_in(arg_keys[12], part), 71), part)
    fresh_keys = scatter_about(part_keys[1], (SEQ, D), 1.0, 6.0, ((0, 8), (1, 2)))
    fresh_values = scatter_about(part_keys[2], (SEQ, D), 1.0, 6.0, ((0, 8), (1, 2)))
    stale_keys = draw_stale_keys(jax.random.fold_in(jax.random.fold_in(arg_keys[12], part), 71), part)
    stale_values = scatter_about(part_keys[4], (SEQ, D), 1.0, 6.0, ((0, 8), (1, 2)))
    residual = draw_residual(jax.random.fold_in(jax.random.fold_in(arg_keys[12], part), 71), part)
    out_weight = scatter_about(arg_keys[6], (D, D), D ** -0.5, 0.125, ((0, 2),))
    modulation = scatter_about(part_keys[7], (2, D), 0.5, 3.0, (), jnp.float32)
    up_weight = scatter_about(arg_keys[8], (N_PATCH * N_EXPERT, D, FW), D ** -0.5, 0.125, ((0, 16),))
    down_weight = scatter_about(arg_keys[9], (N_PATCH * N_EXPERT, FW, D), FF ** -0.5, 0.09375, ((0, 16),))
    routes_keys = jax.random.split(jax.random.fold_in(part_keys[10], 1), SEQ // ROWS)
    routes_turns = jax.random.permutation(jax.random.fold_in(part_keys[10], 3), SEQ // ROWS)
    routes = jax.vmap(lambda own, number: routed_block(jax.random.fold_in(part_keys[10], 2), own, number, ROWS, EXPERTS, TOPK, CAP, 2))(routes_keys, routes_turns).reshape((SEQ, TOPK))
    gates = jnp.clip(0.2 + 0.8 * jax.random.uniform(part_keys[11], (SEQ, TOPK), jnp.float32) ** steps_of(part_keys[11], (SEQ, TOPK), ((0, 16),), -0.2, 0.2), 0.2, 1.0)
    return {"queries": queries, "fresh_keys": fresh_keys, "fresh_values": fresh_values, "stale_keys": stale_keys, "stale_values": stale_values, "residual": residual, "out_weight": out_weight, "modulation": modulation, "up_weight": up_weight, "down_weight": down_weight, "routes": routes, "gates": gates}


def reference(queries, fresh_keys, fresh_values, stale_keys, stale_values, residual, out_weight, modulation, up_weight, down_weight, routes, gates):
    inverse_root = 1.0 / math.sqrt(HEAD_DIM)
    highest = lax.Precision.HIGHEST

    def one_patch(patch_index):
        first_row = (patch_index * TOK_DEV).astype(jnp.int32)
        anchor = jnp.zeros((), jnp.int32)
        key_block = lax.dynamic_update_slice(stale_keys, lax.dynamic_slice_in_dim(fresh_keys, first_row, TOK_DEV, 0), (first_row, anchor))
        value_block = lax.dynamic_update_slice(stale_values, lax.dynamic_slice_in_dim(fresh_values, first_row, TOK_DEV, 0), (first_row, anchor))
        query_heads = lax.dynamic_slice_in_dim(queries, first_row, TOK_DEV, 0).astype(jnp.float32).reshape(TOK_DEV, HEADS, HEAD_DIM)
        key_heads = key_block.astype(jnp.float32).reshape(SEQ, HEADS, HEAD_DIM)
        value_heads = value_block.astype(jnp.float32).reshape(SEQ, HEADS, HEAD_DIM)
        scores = jnp.einsum('qhd,khd->qhk', query_heads, key_heads, precision=highest) * inverse_root
        row_max = scores.max(-1, keepdims=True)
        weights = jnp.exp(scores - row_max)
        denominator = weights.sum(-1)
        rounded = lax.optimization_barrier(weights.astype(jnp.bfloat16)).astype(jnp.float32)
        numerator = jnp.einsum('qhk,khd->qhd', rounded, value_heads, precision=highest)
        return (numerator / denominator[..., None]).reshape(TOK_DEV, D).astype(jnp.bfloat16)
    attended = lax.map(one_patch, jnp.arange(N_PATCH, dtype=jnp.int32)).reshape(SEQ, D)
    hidden_state = residual.astype(jnp.float32) + jnp.dot(attended, out_weight, preferred_element_type=jnp.float32)
    row_mean = hidden_state.mean(-1, keepdims=True)
    centered = hidden_state - row_mean
    variance = (centered * centered).mean(-1, keepdims=True)
    normed = (centered / jnp.sqrt(variance + 1e-06) * (1.0 + modulation[1]) + modulation[0]).astype(jnp.bfloat16)
    blocks = SEQ // ROWS
    per_block = routes.reshape(blocks, ROWS * TOPK)
    one_hot = (per_block[..., None] == jnp.arange(EXPERTS, dtype=jnp.int32)).astype(jnp.int32)
    position = (jnp.cumsum(one_hot, axis=1) * one_hot).sum(-1) - 1
    block_ids = jnp.arange(blocks, dtype=jnp.int32)[:, None]
    expert_rows = blocks * CAP
    slot_index = (per_block * expert_rows + block_ids * CAP + position).reshape(-1).astype(jnp.int32)
    token_ids = jnp.arange(SEQ * TOPK, dtype=jnp.int32) // TOPK
    slot_tokens = jnp.zeros((EXPERTS * expert_rows,), jnp.int32).at[slot_index].set(token_ids)
    up_slices = up_weight.reshape(EXPERTS, WSPLIT, D, FW)
    down_slices = down_weight.reshape(EXPERTS, WSPLIT, FW, D)

    def one_expert(expert_id):
        tokens = lax.dynamic_slice_in_dim(slot_tokens, (expert_id * expert_rows).astype(jnp.int32), expert_rows, 0)
        inputs = jnp.take(normed, tokens, axis=0)
        outputs = jnp.zeros((expert_rows, D), jnp.float32)
        for slice_id in range(WSPLIT):
            hidden_units = jax.nn.gelu(jnp.dot(inputs, up_slices[expert_id, slice_id], preferred_element_type=jnp.float32), approximate=True).astype(jnp.bfloat16)
            slice_out = jnp.dot(hidden_units, down_slices[expert_id, slice_id], preferred_element_type=jnp.float32).astype(jnp.bfloat16)
            outputs = outputs + lax.optimization_barrier(slice_out).astype(jnp.float32)
        return outputs
    expert_out = lax.map(one_expert, jnp.arange(EXPERTS, dtype=jnp.int32)).reshape(-1, D)
    picked = jnp.take(expert_out, slot_index, axis=0).reshape(SEQ, TOPK, D)
    mixed = hidden_state + (picked * gates[..., None]).sum(1)
    return mixed.astype(jnp.bfloat16)
```

```python
import functools
import math

import jax
import jax.numpy as jnp
from jax import lax
from jax.experimental import pallas as pl
from jax.experimental.pallas import tpu as pltpu
from jax.sharding import PartitionSpec as P

HEAD_DIM = 112
EXPERTS = 16
TOPK = 2
LANES = 128
SCALE = 1.0 / math.sqrt(HEAD_DIM)
BF16 = jnp.bfloat16
F32 = jnp.float32
VMEM = pl.BlockSpec(memory_space=pltpu.VMEM)
SMEM = pl.BlockSpec(memory_space=pltpu.SMEM)


def contract(a, b, dim_a, dim_b):
    return lax.dot_general(a, b, (((dim_a,), (dim_b,)), ((), ())), preferred_element_type=F32)


def pack_kernel(q_ref, k_ref, v_ref, out_ref):
    for i, ref in enumerate((q_ref, k_ref, v_ref)):
        turned = ref[...].T
        for h in range(out_ref.shape[0]):
            out_ref[h, i * HEAD_DIM : (i + 1) * HEAD_DIM, :] = turned[
                h * HEAD_DIM : (h + 1) * HEAD_DIM
            ]


def with_ones(values):
    return jnp.concatenate([values, jnp.ones((LANES - HEAD_DIM, values.shape[1]), BF16)], axis=0)


def partial_softmax(query, keys, values):
    scores = contract(query, keys, 0, 0)
    top = scores.max(-1, keepdims=True)
    weights = jnp.exp((scores - top) * SCALE).astype(BF16)
    return contract(weights, with_ones(values), 1, 1), top * SCALE


def fresh_kernel(core_ref, q_ref, k_ref, v_ref, own_ref, other_ref):
    q, k, v = q_ref[...].T, k_ref[...].T, v_ref[...].T
    half = q.shape[1] // 2
    first = core_ref[0] == 0
    lane = lax.broadcasted_iota(jnp.int32, (2 * half, LANES), 1)
    for h in range(q.shape[0] // HEAD_DIM):
        rows = slice(h * HEAD_DIM, (h + 1) * HEAD_DIM)
        sums, top = partial_softmax(q[rows], k[rows], v[rows])
        sums = jnp.where(lane == HEAD_DIM + 1, top, sums)
        lanes = slice(h * LANES, (h + 1) * LANES)
        own_ref[:, lanes] = jnp.where(first, sums[:half], sums[half:])
        other_ref[:, lanes] = jnp.where(first, sums[half:], sums[:half])


def attend_kernel(in_ref, out_ref):
    patches, tokens = in_ref.shape[0], in_ref.shape[2]
    half = tokens // 2
    lane = lax.broadcasted_iota(jnp.int32, (tokens, LANES), 1)
    for p in range(patches):
        others = [j for j in range(patches) if j != p]
        keys = jnp.concatenate([in_ref[j, HEAD_DIM : 2 * HEAD_DIM] for j in others], axis=1)
        values = jnp.concatenate([in_ref[j, 2 * HEAD_DIM :] for j in others], axis=1)
        sums, top = partial_softmax(in_ref[p, :HEAD_DIM], keys, values)
        total = sums[:, HEAD_DIM : HEAD_DIM + 1]
        log_total = top + jnp.log(total)
        high = log_total.astype(BF16).astype(F32)
        rest = log_total - high
        middle = rest.astype(BF16).astype(F32)
        result = sums / total
        result = jnp.where(lane == HEAD_DIM, high, result)
        result = jnp.where(lane == HEAD_DIM + 1, middle, result)
        result = jnp.where(lane == HEAD_DIM + 2, rest - middle, result)
        result = result.astype(BF16)
        out_ref[2 * p] = result[:half]
        out_ref[2 * p + 1] = result[half:]


def slots_of(routes, capacity):
    rows = routes.shape[0]
    expert = lax.broadcasted_iota(jnp.int32, (rows, EXPERTS), 1)
    names = [expert == routes[:, k : k + 1] for k in range(TOPK)]
    named = sum(n.astype(F32) for n in names).astype(BF16)
    earlier = (
        lax.broadcasted_iota(jnp.int32, (rows, rows), 1)
        < lax.broadcasted_iota(jnp.int32, (rows, rows), 0)
    ).astype(F32).astype(BF16)
    count = jnp.dot(earlier, named, preferred_element_type=F32)
    return [
        routes[:, k : k + 1] * capacity
        + jnp.where(names[k], count, 0.0).sum(-1, keepdims=True).astype(jnp.int32)
        for k in range(TOPK)
    ]


def chosen(slot, slots):
    return (
        (lax.broadcasted_iota(jnp.int32, (slot.shape[0], slots), 1) == slot).astype(F32).astype(BF16)
    )


def home_kernel(
    core_ref, far_ref, own_ref, other_ref, w_own_ref, w_other_ref, residual_ref, modulation_ref,
    routes_ref, hidden_ref, buffer_ref, attended_ref,
):
    heads = far_ref.shape[0]
    core = core_ref[0]
    projected = None
    for side, (near_ref, w_ref) in enumerate(((own_ref, w_own_ref), (other_ref, w_other_ref))):
        which = core if side == 0 else 1 - core
        for h in range(heads):
            far = far_ref[h, which].astype(F32)
            near = near_ref[:, h * LANES : (h + 1) * LANES]
            far_log = (
                far[:, HEAD_DIM : HEAD_DIM + 1]
                + far[:, HEAD_DIM + 1 : HEAD_DIM + 2]
                + far[:, HEAD_DIM + 2 : HEAD_DIM + 3]
            )
            near_total = near[:, HEAD_DIM : HEAD_DIM + 1]
            near_top = near[:, HEAD_DIM + 1 : HEAD_DIM + 2]
            top = jnp.maximum(far_log, near_top)
            far_weight = jnp.exp(far_log - top)
            near_weight = jnp.exp(near_top - top)
            scale = 1.0 / (far_weight + near_total * near_weight)
            merged = far * (far_weight * scale) + near * (near_weight * scale)
            attended_ref[side, :, h * HEAD_DIM : (h + 1) * HEAD_DIM] = merged[:, :HEAD_DIM].astype(BF16)
        part = jnp.dot(attended_ref[side], w_ref[...], preferred_element_type=F32)
        projected = part if projected is None else projected + part
    hidden = residual_ref[...].astype(F32) + projected
    hidden_ref[...] = hidden
    centered = hidden - hidden.mean(-1, keepdims=True)
    variance = (centered * centered).mean(-1, keepdims=True)
    normed = (
        centered / jnp.sqrt(variance + 1e-06) * (1.0 + modulation_ref[1:2]) + modulation_ref[0:1]
    ).astype(BF16)
    slots = buffer_ref.shape[0]
    picks = [chosen(slot, slots) for slot in slots_of(routes_ref[...], slots // EXPERTS)]
    buffer_ref[...] = contract(picks[0] + picks[1], normed, 0, 0).astype(BF16)


def attention_by_heads(queries, fresh_keys, fresh_values, stale_keys, stale_values, out_weight, residual, modulation, routes):
    tokens, width = queries.shape
    heads = width // HEAD_DIM
    rows, features = residual.shape
    core = lax.axis_index("expert").astype(jnp.int32).reshape(1)
    swap = [(0, 1), (1, 0)]
    packed = pl.pallas_call(
        pack_kernel,
        out_shape=jax.ShapeDtypeStruct((heads, 3 * HEAD_DIM, tokens), BF16),
        in_specs=[VMEM] * 3,
        out_specs=VMEM,
        name="pack",
    )(queries, stale_keys, stale_values)
    w_other = lax.ppermute(out_weight, "expert", swap)
    gathered = lax.all_to_all(packed, "patch", split_axis=0, concat_axis=0, tiled=True)
    fresh_shape = jax.ShapeDtypeStruct((tokens // 2, heads * LANES), F32)
    fresh_own, fresh_away = pl.pallas_call(
        fresh_kernel,
        out_shape=(fresh_shape, fresh_shape),
        in_specs=[SMEM] + [VMEM] * 3,
        out_specs=(VMEM, VMEM),
        cost_estimate=pl.CostEstimate(flops=60_000_000, bytes_accessed=2_000_000, transcendentals=200_000),
        name="fresh",
    )(core, queries, fresh_keys, fresh_values)
    fresh_other = lax.ppermute(fresh_away, "expert", swap)
    stale = pl.pallas_call(
        attend_kernel,
        out_shape=jax.ShapeDtypeStruct((2 * heads, tokens // 2, LANES), BF16),
        in_specs=[VMEM],
        out_specs=VMEM,
        compiler_params=pltpu.CompilerParams(vmem_limit_bytes=32 << 20),
        name="attend",
    )(gathered)
    far = lax.all_to_all(stale, ("patch", "expert"), split_axis=0, concat_axis=0, tiled=True)
    return pl.pallas_call(
        home_kernel,
        out_shape=(
            jax.ShapeDtypeStruct((rows, features), F32),
            jax.ShapeDtypeStruct((EXPERTS * (rows // 4), features), BF16),
        ),
        in_specs=[SMEM] + [VMEM] * 8,
        out_specs=(VMEM, VMEM),
        scratch_shapes=[pltpu.VMEM((2, rows, width), BF16)],
        compiler_params=pltpu.CompilerParams(vmem_limit_bytes=40 << 20),
        name="home",
    )(core, far.reshape(heads, 2, rows, LANES), fresh_own, fresh_other, out_weight, w_other, residual, modulation, routes)


def split_heads(block_rows):
    return block_rows.reshape(block_rows.shape[0], block_rows.shape[1] // HEAD_DIM, HEAD_DIM)


def head_scores(query_heads, key_rows):
    products = jnp.einsum("qhd,khd->qhk", query_heads, split_heads(key_rows), preferred_element_type=F32)
    return products * SCALE


def weighted_values(weights, value_rows):
    return jnp.einsum(
        "qhk,khd->qhd", weights.astype(BF16), split_heads(value_rows), preferred_element_type=F32
    )


def attention_by_gather(queries, fresh_keys, fresh_values, stale_keys, stale_values, out_weight, residual, modulation, routes):
    row_count = queries.shape[0]
    own_start = lax.axis_index("patch") * row_count
    query_heads = split_heads(queries)
    scores = head_scores(query_heads, fresh_keys)
    running_max = scores.max(-1)
    weights = jnp.exp(scores - running_max[..., None])
    denominator, numerator = weights.sum(-1), weighted_values(weights, fresh_values)
    piece_keys = lax.all_gather(stale_keys, "patch", axis=0, tiled=True)
    piece_values = lax.all_gather(stale_values, "patch", axis=0, tiled=True)
    scores = head_scores(query_heads, piece_keys)
    positions = jnp.arange(piece_keys.shape[0], dtype=jnp.int32)
    own_rows = (positions >= own_start) & (positions < own_start + row_count)
    scores = jnp.where(own_rows[None, None, :], -1e30, scores)
    newest = jnp.maximum(running_max, scores.max(-1))
    rescale = jnp.exp(running_max - newest)
    weights = jnp.where(own_rows[None, None, :], 0.0, jnp.exp(scores - newest[..., None]))
    denominator = denominator * rescale + weights.sum(-1)
    numerator = numerator * rescale[..., None] + weighted_values(weights, piece_values)
    attended = (numerator / denominator[..., None]).reshape(queries.shape).astype(BF16)
    hidden = residual.astype(F32) + lax.psum_scatter(
        jnp.dot(attended, out_weight, preferred_element_type=F32).astype(BF16),
        "expert",
        scatter_dimension=0,
        tiled=True,
    ).astype(F32)
    centered = hidden - hidden.mean(-1, keepdims=True)
    variance = (centered * centered).mean(-1, keepdims=True)
    normed = (centered / jnp.sqrt(variance + 1e-06) * (1.0 + modulation[1]) + modulation[0]).astype(BF16)
    capacity = residual.shape[0] // 4
    picks = [chosen(slot, EXPERTS * capacity) for slot in slots_of(routes, capacity)]
    return hidden, contract(picks[0] + picks[1], normed, 0, 0).astype(BF16)


def expert_kernel(x_ref, up_ref, down_ref, out_ref, total_ref):
    step = pl.program_id(0)
    units = jax.nn.gelu(
        jnp.dot(x_ref[...], up_ref[0], preferred_element_type=F32), approximate=True
    ).astype(BF16)
    part = jnp.dot(units, down_ref[0], preferred_element_type=F32)

    @pl.when(step == 0)
    def _():
        total_ref[...] = part

    @pl.when(step > 0)
    def _():
        total_ref[...] += part

    @pl.when(step == pl.num_programs(0) - 1)
    def _():
        out_ref[...] = total_ref[...].astype(BF16)


def expert_slice(inputs, up_weight, down_weight):
    rows, features = inputs.shape
    units = up_weight.shape[2]
    chunk = next(c for c in (512, 256, 128) if units % c == 0)
    return pl.pallas_call(
        expert_kernel,
        grid=(units // chunk,),
        out_shape=jax.ShapeDtypeStruct((rows, features), BF16),
        in_specs=[
            pl.BlockSpec((rows, features), lambda j: (0, 0)),
            pl.BlockSpec((1, features, chunk), lambda j: (0, 0, j)),
            pl.BlockSpec((1, chunk, features), lambda j: (0, j, 0)),
        ],
        out_specs=pl.BlockSpec((rows, features), lambda j: (0, 0)),
        scratch_shapes=[pltpu.VMEM((rows, features), F32)],
        compiler_params=pltpu.CompilerParams(vmem_limit_bytes=40 << 20),
        name="experts",
    )(inputs, up_weight, down_weight)


def combine_kernel(hidden_ref, routes_ref, gates_ref, returned_ref, out_ref):
    slices = returned_ref.shape[1]
    slots = returned_ref.shape[0] * returned_ref.shape[2]
    mixed = hidden_ref[...]
    picks = [chosen(slot, slots) for slot in slots_of(routes_ref[...], slots // EXPERTS)]
    for s in range(slices):
        rows = returned_ref[:, s].reshape(slots, returned_ref.shape[3])
        for k in range(TOPK):
            mixed += gates_ref[:, k : k + 1] * jnp.dot(picks[k], rows, preferred_element_type=F32)
    out_ref[...] = mixed.astype(BF16)


def body(
    queries, fresh_keys, fresh_values, stale_keys, stale_values, residual, out_weight, modulation,
    up_weight, down_weight, routes, gates,
):
    rows, features = residual.shape
    patch_count = lax.axis_size("patch")
    device_count = patch_count * lax.axis_size("expert")
    by_heads = queries.shape[1] // HEAD_DIM == patch_count and lax.axis_size("expert") == 2
    attention = attention_by_heads if by_heads else attention_by_gather
    hidden, buffer = attention(
        queries, fresh_keys, fresh_values, stale_keys, stale_values, out_weight, residual, modulation, routes
    )
    capacity = rows // 4
    slice_count = device_count // EXPERTS
    outgoing = jnp.broadcast_to(
        buffer.reshape(EXPERTS, 1, capacity, features), (EXPERTS, slice_count, capacity, features)
    ).reshape(device_count, capacity, features)
    arrived = lax.all_to_all(outgoing, ("patch", "expert"), split_axis=0, concat_axis=0, tiled=True)
    outputs = expert_slice(arrived.reshape(device_count * capacity, features), up_weight, down_weight)
    returned = lax.all_to_all(
        outputs.reshape(device_count, capacity, features),
        ("patch", "expert"),
        split_axis=0,
        concat_axis=0,
        tiled=True,
    )
    return pl.pallas_call(
        combine_kernel,
        out_shape=jax.ShapeDtypeStruct((rows, features), BF16),
        in_specs=[VMEM] * 4,
        out_specs=VMEM,
        compiler_params=pltpu.CompilerParams(vmem_limit_bytes=32 << 20),
        name="combine",
    )(hidden, routes, gates, returned.reshape(EXPERTS, slice_count, capacity, features))


def solution(mesh):
    tokens = P(("group", "patch"), "expert")
    rows = P(("group", "patch", "expert"), None)
    weight = P(("patch", "expert"), None, None)
    placed = (
        tokens, tokens, tokens, tokens, tokens, rows, P("expert", None), P("group", None), weight, weight, rows, rows,
    )
    return jax.shard_map(body, mesh=mesh, in_specs=placed, out_specs=rows, check_vma=False)
```

```python
import functools
import math

import jax
import jax.numpy as jnp
from jax import lax
from jax.experimental import pallas as pl
from jax.experimental.pallas import tpu as pltpu
from jax.sharding import PartitionSpec as P

HEAD_DIM = 112
EXPERTS = 16
TOPK = 2
LANES = 128
SCALE = 1.0 / math.sqrt(HEAD_DIM)
BF16 = jnp.bfloat16
F32 = jnp.float32
VMEM = pl.BlockSpec(memory_space=pltpu.VMEM)
SMEM = pl.BlockSpec(memory_space=pltpu.SMEM)
ANY = pl.BlockSpec(memory_space=pl.ANY)


def contract(a, b, dim_a, dim_b):
    return lax.dot_general(a, b, (((dim_a,), (dim_b,)), ((), ())), preferred_element_type=F32)


def pack_kernel(q_ref, k_ref, v_ref, out_ref):
    for i, ref in enumerate((q_ref, k_ref, v_ref)):
        turned = ref[...].T
        for h in range(out_ref.shape[0]):
            out_ref[h, i * HEAD_DIM : (i + 1) * HEAD_DIM, :] = turned[
                h * HEAD_DIM : (h + 1) * HEAD_DIM
            ]


def with_ones(values):
    return jnp.concatenate([values, jnp.ones((LANES - HEAD_DIM, values.shape[1]), BF16)], axis=0)


def partial_softmax(query, keys, values):
    scores = contract(query, keys, 0, 0)
    top = scores.max(-1, keepdims=True)
    weights = jnp.exp((scores - top) * SCALE).astype(BF16)
    return contract(weights, with_ones(values), 1, 1), top * SCALE


def fresh_kernel(
    core_ref, q_ref, k_ref, v_ref, routes_ref, gates_ref, own_ref, other_ref, picks_ref, gates_out_ref
):
    q, k, v = q_ref[...].T, k_ref[...].T, v_ref[...].T
    half = q.shape[1] // 2
    first = core_ref[0] == 0
    lane = lax.broadcasted_iota(jnp.int32, (2 * half, LANES), 1)
    for h in range(q.shape[0] // HEAD_DIM):
        rows = slice(h * HEAD_DIM, (h + 1) * HEAD_DIM)
        sums, top = partial_softmax(q[rows], k[rows], v[rows])
        sums = jnp.where(lane == HEAD_DIM + 1, top, sums)
        lanes = slice(h * LANES, (h + 1) * LANES)
        own_ref[:, lanes] = jnp.where(first, sums[:half], sums[half:])
        other_ref[:, lanes] = jnp.where(first, sums[half:], sums[:half])
    slots = picks_ref.shape[2]
    for k, slot in enumerate(slots_of(routes_ref[...], slots // EXPERTS)):
        picks_ref[k] = chosen(slot, slots)
    gates_out_ref[...] = gates_ref[...]


def attend_kernel(in_ref, fresh_ref, out_ref):
    patches, tokens = in_ref.shape[0], in_ref.shape[2]
    half = tokens // 2
    lane = lax.broadcasted_iota(jnp.int32, (tokens, LANES), 1)
    for p in range(patches):
        others = [j for j in range(patches) if j != p]
        keys = jnp.concatenate([in_ref[j, HEAD_DIM : 2 * HEAD_DIM] for j in others], axis=1)
        values = jnp.concatenate([in_ref[j, 2 * HEAD_DIM :] for j in others], axis=1)
        sums, top = partial_softmax(in_ref[p, :HEAD_DIM], keys, values)
        total = sums[:, HEAD_DIM : HEAD_DIM + 1]
        log_total = top + jnp.log(total)
        high = log_total.astype(BF16).astype(F32)
        rest = log_total - high
        middle = rest.astype(BF16).astype(F32)
        result = sums / total
        result = jnp.where(lane == HEAD_DIM, high, result)
        result = jnp.where(lane == HEAD_DIM + 1, middle, result)
        result = jnp.where(lane == HEAD_DIM + 2, rest - middle, result)
        result = result.astype(BF16)
        out_ref[2 * p] = result[:half]
        out_ref[2 * p + 1] = result[half:]


def slots_of(routes, capacity):
    rows = routes.shape[0]
    expert = lax.broadcasted_iota(jnp.int32, (rows, EXPERTS), 1)
    names = [expert == routes[:, k : k + 1] for k in range(TOPK)]
    named = sum(n.astype(F32) for n in names).astype(BF16)
    earlier = (
        lax.broadcasted_iota(jnp.int32, (rows, rows), 1)
        < lax.broadcasted_iota(jnp.int32, (rows, rows), 0)
    ).astype(F32).astype(BF16)
    count = jnp.dot(earlier, named, preferred_element_type=F32)
    return [
        routes[:, k : k + 1] * capacity
        + jnp.where(names[k], count, 0.0).sum(-1, keepdims=True).astype(jnp.int32)
        for k in range(TOPK)
    ]


def chosen(slot, slots):
    return (
        (lax.broadcasted_iota(jnp.int32, (slot.shape[0], slots), 1) == slot).astype(F32).astype(BF16)
    )


def home_kernel(
    core_ref, far_ref, own_ref, other_ref, w_own_ref, w_other_ref, residual_ref, modulation_ref,
    picks_ref, hidden_ref, buffer_ref, attended_ref,
):
    heads = far_ref.shape[0]
    core = core_ref[0]
    projected = None
    for side, (near_ref, w_ref) in enumerate(((own_ref, w_own_ref), (other_ref, w_other_ref))):
        which = core if side == 0 else 1 - core
        for h in range(heads):
            far = far_ref[h, which].astype(F32)
            near = near_ref[:, h * LANES : (h + 1) * LANES]
            far_log = (
                far[:, HEAD_DIM : HEAD_DIM + 1]
                + far[:, HEAD_DIM + 1 : HEAD_DIM + 2]
                + far[:, HEAD_DIM + 2 : HEAD_DIM + 3]
            )
            near_total = near[:, HEAD_DIM : HEAD_DIM + 1]
            near_top = near[:, HEAD_DIM + 1 : HEAD_DIM + 2]
            top = jnp.maximum(far_log, near_top)
            far_weight = jnp.exp(far_log - top)
            near_weight = jnp.exp(near_top - top)
            scale = 1.0 / (far_weight + near_total * near_weight)
            merged = far * (far_weight * scale) + near * (near_weight * scale)
            attended_ref[side, :, h * HEAD_DIM : (h + 1) * HEAD_DIM] = merged[:, :HEAD_DIM].astype(BF16)
        part = jnp.dot(attended_ref[side], w_ref[...], preferred_element_type=F32)
        projected = part if projected is None else projected + part
    hidden = residual_ref[...].astype(F32) + projected
    hidden_ref[...] = hidden
    centered = hidden - hidden.mean(-1, keepdims=True)
    variance = (centered * centered).mean(-1, keepdims=True)
    normed = (
        centered / jnp.sqrt(variance + 1e-06) * (1.0 + modulation_ref[1:2]) + modulation_ref[0:1]
    ).astype(BF16)
    buffer_ref[...] = contract(picks_ref[0] + picks_ref[1], normed, 0, 0).astype(BF16)


def attention_by_heads(queries, fresh_keys, fresh_values, stale_keys, stale_values, out_weight, residual, modulation, routes, gates):
    tokens, width = queries.shape
    heads = width // HEAD_DIM
    rows, features = residual.shape
    core = lax.axis_index("expert").astype(jnp.int32).reshape(1)
    swap = [(0, 1), (1, 0)]
    packed = pl.pallas_call(
        pack_kernel,
        out_shape=jax.ShapeDtypeStruct((heads, 3 * HEAD_DIM, tokens), BF16),
        in_specs=[VMEM] * 3,
        out_specs=VMEM,
        name="pack",
    )(queries, stale_keys, stale_values)
    w_other = lax.ppermute(out_weight, "expert", swap)
    gathered = lax.all_to_all(packed, "patch", split_axis=0, concat_axis=0, tiled=True)
    fresh_shape = jax.ShapeDtypeStruct((tokens // 2, heads * LANES), F32)
    slots = EXPERTS * (rows // 4)
    fresh_own, fresh_away, picks, gates = pl.pallas_call(
        fresh_kernel,
        out_shape=(
            fresh_shape,
            fresh_shape,
            jax.ShapeDtypeStruct((TOPK, rows, slots), BF16),
            jax.ShapeDtypeStruct(gates.shape, F32),
        ),
        in_specs=[SMEM] + [VMEM] * 5,
        out_specs=(VMEM,) * 4,
        compiler_params=pltpu.CompilerParams(vmem_limit_bytes=16 << 20),
        cost_estimate=pl.CostEstimate(flops=5_000_000_000, bytes_accessed=2_000_000, transcendentals=200_000),
        name="fresh",
    )(core, queries, fresh_keys, fresh_values, routes, gates)
    fresh_other = lax.ppermute(fresh_away, "expert", swap)
    stale = pl.pallas_call(
        attend_kernel,
        out_shape=jax.ShapeDtypeStruct((2 * heads, tokens // 2, LANES), BF16),
        in_specs=[VMEM, ANY],
        out_specs=VMEM,
        compiler_params=pltpu.CompilerParams(vmem_limit_bytes=16 << 20),
        cost_estimate=pl.CostEstimate(flops=100_000_000_000, bytes_accessed=2_000_000, transcendentals=1_000_000),
        name="attend",
    )(gathered, fresh_other)
    far = lax.all_to_all(stale, ("patch", "expert"), split_axis=0, concat_axis=0, tiled=True)
    hidden, buffer = pl.pallas_call(
        home_kernel,
        out_shape=(
            jax.ShapeDtypeStruct((rows, features), F32),
            jax.ShapeDtypeStruct((EXPERTS * (rows // 4), features), BF16),
        ),
        in_specs=[SMEM] + [VMEM] * 8,
        out_specs=(VMEM, VMEM),
        scratch_shapes=[pltpu.VMEM((2, rows, width), BF16)],
        compiler_params=pltpu.CompilerParams(vmem_limit_bytes=16 << 20),
        cost_estimate=pl.CostEstimate(flops=200_000_000_000, bytes_accessed=8_000_000, transcendentals=100_000),
        name="home",
    )(core, far.reshape(heads, 2, rows, LANES), fresh_own, fresh_other, out_weight, w_other, residual, modulation, picks)
    return hidden, buffer, picks, gates


def split_heads(block_rows):
    return block_rows.reshape(block_rows.shape[0], block_rows.shape[1] // HEAD_DIM, HEAD_DIM)


def head_scores(query_heads, key_rows):
    products = jnp.einsum("qhd,khd->qhk", query_heads, split_heads(key_rows), preferred_element_type=F32)
    return products * SCALE


def weighted_values(weights, value_rows):
    return jnp.einsum(
        "qhk,khd->qhd", weights.astype(BF16), split_heads(value_rows), preferred_element_type=F32
    )


def attention_by_gather(queries, fresh_keys, fresh_values, stale_keys, stale_values, out_weight, residual, modulation, routes, gates):
    row_count = queries.shape[0]
    own_start = lax.axis_index("patch") * row_count
    query_heads = split_heads(queries)
    scores = head_scores(query_heads, fresh_keys)
    running_max = scores.max(-1)
    weights = jnp.exp(scores - running_max[..., None])
    denominator, numerator = weights.sum(-1), weighted_values(weights, fresh_values)
    piece_keys = lax.all_gather(stale_keys, "patch", axis=0, tiled=True)
    piece_values = lax.all_gather(stale_values, "patch", axis=0, tiled=True)
    scores = head_scores(query_heads, piece_keys)
    positions = jnp.arange(piece_keys.shape[0], dtype=jnp.int32)
    own_rows = (positions >= own_start) & (positions < own_start + row_count)
    scores = jnp.where(own_rows[None, None, :], -1e30, scores)
    newest = jnp.maximum(running_max, scores.max(-1))
    rescale = jnp.exp(running_max - newest)
    weights = jnp.where(own_rows[None, None, :], 0.0, jnp.exp(scores - newest[..., None]))
    denominator = denominator * rescale + weights.sum(-1)
    numerator = numerator * rescale[..., None] + weighted_values(weights, piece_values)
    attended = (numerator / denominator[..., None]).reshape(queries.shape).astype(BF16)
    hidden = residual.astype(F32) + lax.psum_scatter(
        jnp.dot(attended, out_weight, preferred_element_type=F32).astype(BF16),
        "expert",
        scatter_dimension=0,
        tiled=True,
    ).astype(F32)
    centered = hidden - hidden.mean(-1, keepdims=True)
    variance = (centered * centered).mean(-1, keepdims=True)
    normed = (centered / jnp.sqrt(variance + 1e-06) * (1.0 + modulation[1]) + modulation[0]).astype(BF16)
    capacity = residual.shape[0] // 4
    picks = [chosen(slot, EXPERTS * capacity) for slot in slots_of(routes, capacity)]
    return hidden, contract(picks[0] + picks[1], normed, 0, 0).astype(BF16), jnp.stack(picks), gates


def expert_kernel(x_ref, up_ref, down_ref, out_ref, units_ref):
    for part in chunks(up_ref.shape[2]):
        units_ref[:, part] = jax.nn.gelu(
            jnp.dot(x_ref[...], up_ref[0, :, part], preferred_element_type=F32), approximate=True
        ).astype(BF16)
    for part in chunks(out_ref.shape[1]):
        out_ref[:, part] = jnp.dot(
            units_ref[...], down_ref[0, :, part], preferred_element_type=F32
        ).astype(BF16)


def chunks(width):
    step = 896 if width % 896 == 0 else LANES
    return [slice(i, i + step) for i in range(0, width, step)]


def expert_slice(inputs, up_weight, down_weight):
    rows, features = inputs.shape
    return pl.pallas_call(
        expert_kernel,
        out_shape=jax.ShapeDtypeStruct((rows, features), BF16),
        in_specs=[VMEM] * 3,
        out_specs=VMEM,
        scratch_shapes=[pltpu.VMEM((rows, up_weight.shape[2]), BF16)],
        compiler_params=pltpu.CompilerParams(vmem_limit_bytes=16 << 20),
        name="experts",
    )(inputs, up_weight, down_weight)


def combine_kernel(hidden_ref, picks_ref, gates_ref, returned_ref, out_ref):
    slices = returned_ref.shape[1]
    slots = returned_ref.shape[0] * returned_ref.shape[2]
    mixed = hidden_ref[...]
    for s in range(slices):
        rows = returned_ref[:, s].reshape(slots, returned_ref.shape[3])
        for k in range(TOPK):
            mixed += gates_ref[:, k : k + 1] * jnp.dot(picks_ref[k], rows, preferred_element_type=F32)
    out_ref[...] = mixed.astype(BF16)


def body(
    queries, fresh_keys, fresh_values, stale_keys, stale_values, residual, out_weight, modulation,
    up_weight, down_weight, routes, gates,
):
    rows, features = residual.shape
    patch_count = lax.axis_size("patch")
    device_count = patch_count * lax.axis_size("expert")
    by_heads = queries.shape[1] // HEAD_DIM == patch_count and lax.axis_size("expert") == 2
    attention = attention_by_heads if by_heads else attention_by_gather
    hidden, buffer, picks, gates = attention(
        queries, fresh_keys, fresh_values, stale_keys, stale_values, out_weight, residual, modulation, routes, gates
    )
    capacity = rows // 4
    slice_count = device_count // EXPERTS
    outgoing = jnp.broadcast_to(
        buffer.reshape(EXPERTS, 1, capacity, features), (EXPERTS, slice_count, capacity, features)
    ).reshape(device_count, capacity, features)
    arrived = lax.all_to_all(outgoing, ("patch", "expert"), split_axis=0, concat_axis=0, tiled=True)
    outputs = expert_slice(arrived.reshape(device_count * capacity, features), up_weight, down_weight)
    returned = lax.all_to_all(
        outputs.reshape(device_count, capacity, features),
        ("patch", "expert"),
        split_axis=0,
        concat_axis=0,
        tiled=True,
    )
    return pl.pallas_call(
        combine_kernel,
        out_shape=jax.ShapeDtypeStruct((rows, features), BF16),
        in_specs=[VMEM] * 4,
        out_specs=VMEM,
        compiler_params=pltpu.CompilerParams(vmem_limit_bytes=32 << 20),
        name="combine",
    )(hidden, picks, gates, returned.reshape(EXPERTS, slice_count, capacity, features))


def solution(mesh):
    tokens = P(("group", "patch"), "expert")
    rows = P(("group", "patch", "expert"), None)
    weight = P(("patch", "expert"), None, None)
    placed = (
        tokens, tokens, tokens, tokens, tokens, rows, P("expert", None), P("group", None), weight, weight, rows, rows,
    )
    return jax.shard_map(body, mesh=mesh, in_specs=placed, out_specs=rows, check_vma=False)
```

```python
import functools
import math

import jax
import jax.numpy as jnp
from jax import lax
from jax.experimental import pallas as pl
from jax.experimental.pallas import tpu as pltpu
from jax.sharding import PartitionSpec as P

HEAD_DIM = 112
EXPERTS = 16
TOPK = 2
LANES = 128
SCALE = 1.0 / math.sqrt(HEAD_DIM)
BF16 = jnp.bfloat16
F32 = jnp.float32
VMEM = pl.BlockSpec(memory_space=pltpu.VMEM)
SMEM = pl.BlockSpec(memory_space=pltpu.SMEM)
ANY = pl.BlockSpec(memory_space=pl.ANY)


def contract(a, b, dim_a, dim_b):
    return lax.dot_general(a, b, (((dim_a,), (dim_b,)), ((), ())), preferred_element_type=F32)


def pack_kernel(q_ref, k_ref, v_ref, out_ref):
    for i, ref in enumerate((q_ref, k_ref, v_ref)):
        turned = ref[...].T
        for h in range(out_ref.shape[0]):
            out_ref[h, i * HEAD_DIM : (i + 1) * HEAD_DIM, :] = turned[
                h * HEAD_DIM : (h + 1) * HEAD_DIM
            ]


def with_ones(values):
    return jnp.concatenate([values, jnp.ones((LANES - HEAD_DIM, values.shape[1]), BF16)], axis=0)


def partial_softmax(query, keys, values):
    scores = contract(query, keys, 0, 0)
    top = scores.max(-1, keepdims=True)
    weights = jnp.exp((scores - top) * SCALE).astype(BF16)
    return contract(weights, with_ones(values), 1, 1), top * SCALE


def fresh_kernel(
    core_ref, q_ref, k_ref, v_ref, routes_ref, gates_ref, own_ref, other_ref, picks_ref, gates_out_ref
):
    q, k, v = q_ref[...].T, k_ref[...].T, v_ref[...].T
    half = q.shape[1] // 2
    first = core_ref[0] == 0
    lane = lax.broadcasted_iota(jnp.int32, (2 * half, LANES), 1)
    for h in range(q.shape[0] // HEAD_DIM):
        rows = slice(h * HEAD_DIM, (h + 1) * HEAD_DIM)
        sums, top = partial_softmax(q[rows], k[rows], v[rows])
        sums = jnp.where(lane == HEAD_DIM + 1, top, sums)
        lanes = slice(h * LANES, (h + 1) * LANES)
        own_ref[:, lanes] = jnp.where(first, sums[:half], sums[half:])
        other_ref[:, lanes] = jnp.where(first, sums[half:], sums[:half])
    slots = picks_ref.shape[2]
    for k, slot in enumerate(slots_of(routes_ref[...], slots // EXPERTS)):
        picks_ref[k] = chosen(slot, slots)
    gates_out_ref[...] = gates_ref[...]


def attend_kernel(in_ref, fresh_ref, out_ref):
    patches, tokens = in_ref.shape[0], in_ref.shape[2]
    half, rows, steps = tokens // 2, 2 * tokens, patches // 2
    keys = jnp.concatenate([in_ref[j, HEAD_DIM : 2 * HEAD_DIM] for j in range(patches)], axis=1)
    values = with_ones(jnp.concatenate([in_ref[j, 2 * HEAD_DIM :] for j in range(patches)], axis=1))
    lane = lax.broadcasted_iota(jnp.int32, (rows, LANES), 1)
    own = (lax.broadcasted_iota(jnp.int32, (rows, rows), 0) < tokens) == (
        lax.broadcasted_iota(jnp.int32, (rows, rows), 1) < tokens
    )

    def scores_of(step):
        query = jnp.concatenate([in_ref[2 * step + i, :HEAD_DIM] for i in range(2)], axis=1)
        scores = contract(query, keys, 0, 0)
        first, last = step * rows, (step + 1) * rows
        parts = [jnp.where(own, -1e30, scores[:, first:last])]
        if step > 0:
            parts.insert(0, scores[:, :first])
        if step < steps - 1:
            parts.append(scores[:, last:])
        return jnp.concatenate(parts, axis=1)

    scores = scores_of(0)
    for step in range(steps):
        following = scores_of(step + 1) if step < steps - 1 else None
        top = scores.max(-1, keepdims=True)
        weights = jnp.exp2((scores - top) * (SCALE * math.log2(math.e))).astype(BF16)
        sums = contract(weights, values, 1, 1)
        total = sums[:, HEAD_DIM : HEAD_DIM + 1]
        log_total = top * SCALE + jnp.log(total)
        high = log_total.astype(BF16).astype(F32)
        rest = log_total - high
        middle = rest.astype(BF16).astype(F32)
        result = sums * (1.0 / total)
        result = jnp.where(lane == HEAD_DIM, high, result)
        result = jnp.where(lane == HEAD_DIM + 1, middle, result)
        result = jnp.where(lane == HEAD_DIM + 2, rest - middle, result)
        result = result.astype(BF16)
        for i in range(4):
            out_ref[4 * step + i] = result[i * half : (i + 1) * half]
        scores = following


def slots_of(routes, capacity):
    rows = routes.shape[0]
    expert = lax.broadcasted_iota(jnp.int32, (rows, EXPERTS), 1)
    names = [expert == routes[:, k : k + 1] for k in range(TOPK)]
    named = sum(n.astype(F32) for n in names).astype(BF16)
    earlier = (
        lax.broadcasted_iota(jnp.int32, (rows, rows), 1)
        < lax.broadcasted_iota(jnp.int32, (rows, rows), 0)
    ).astype(F32).astype(BF16)
    count = jnp.dot(earlier, named, preferred_element_type=F32)
    return [
        routes[:, k : k + 1] * capacity
        + jnp.where(names[k], count, 0.0).sum(-1, keepdims=True).astype(jnp.int32)
        for k in range(TOPK)
    ]


def chosen(slot, slots):
    return (
        (lax.broadcasted_iota(jnp.int32, (slot.shape[0], slots), 1) == slot).astype(F32).astype(BF16)
    )


def home_kernel(
    core_ref, far_ref, own_ref, other_ref, w_own_ref, w_other_ref, residual_ref, modulation_ref,
    picks_ref, hidden_ref, buffer_ref, attended_ref, w_ref, loaded_ref,
):
    loads = [
        pltpu.make_async_copy(source, w_ref.at[i], loaded_ref.at[i])
        for i, source in enumerate((w_own_ref, w_other_ref))
    ]
    for load in loads:
        load.start()
    heads = far_ref.shape[0]
    core = core_ref[0]
    projected = None
    for side, near_ref in enumerate((own_ref, other_ref)):
        which = core if side == 0 else 1 - core
        for h in range(heads):
            far = far_ref[h, which].astype(F32)
            near = near_ref[:, h * LANES : (h + 1) * LANES]
            far_log = (
                far[:, HEAD_DIM : HEAD_DIM + 1]
                + far[:, HEAD_DIM + 1 : HEAD_DIM + 2]
                + far[:, HEAD_DIM + 2 : HEAD_DIM + 3]
            )
            near_total = near[:, HEAD_DIM : HEAD_DIM + 1]
            near_top = near[:, HEAD_DIM + 1 : HEAD_DIM + 2]
            top = jnp.maximum(far_log, near_top)
            far_weight = jnp.exp(far_log - top)
            near_weight = jnp.exp(near_top - top)
            scale = 1.0 / (far_weight + near_total * near_weight)
            merged = far * (far_weight * scale) + near * (near_weight * scale)
            attended_ref[side, :, h * HEAD_DIM : (h + 1) * HEAD_DIM] = merged[:, :HEAD_DIM].astype(BF16)
    for side in range(2):
        loads[side].wait()
        part = jnp.dot(attended_ref[side], w_ref[side], preferred_element_type=F32)
        projected = part if projected is None else projected + part
    hidden = residual_ref[...].astype(F32) + projected
    hidden_ref[...] = hidden
    centered = hidden - hidden.mean(-1, keepdims=True)
    variance = (centered * centered).mean(-1, keepdims=True)
    normed = (
        centered / jnp.sqrt(variance + 1e-06) * (1.0 + modulation_ref[1:2]) + modulation_ref[0:1]
    ).astype(BF16)
    buffer_ref[...] = contract(picks_ref[0] + picks_ref[1], normed, 0, 0).astype(BF16)


def attention_by_heads(queries, fresh_keys, fresh_values, stale_keys, stale_values, out_weight, residual, modulation, routes, gates):
    tokens, width = queries.shape
    heads = width // HEAD_DIM
    rows, features = residual.shape
    core = lax.axis_index("expert").astype(jnp.int32).reshape(1)
    swap = [(0, 1), (1, 0)]
    packed = pl.pallas_call(
        pack_kernel,
        out_shape=jax.ShapeDtypeStruct((heads, 3 * HEAD_DIM, tokens), BF16),
        in_specs=[VMEM] * 3,
        out_specs=VMEM,
        name="pack",
    )(queries, stale_keys, stale_values)
    w_other = lax.ppermute(out_weight, "expert", swap)
    gathered = lax.all_to_all(packed, "patch", split_axis=0, concat_axis=0, tiled=True)
    fresh_shape = jax.ShapeDtypeStruct((tokens // 2, heads * LANES), F32)
    slots = EXPERTS * (rows // 4)
    fresh_own, fresh_away, picks, gates = pl.pallas_call(
        fresh_kernel,
        out_shape=(
            fresh_shape,
            fresh_shape,
            jax.ShapeDtypeStruct((TOPK, rows, slots), BF16),
            jax.ShapeDtypeStruct(gates.shape, F32),
        ),
        in_specs=[SMEM] + [VMEM] * 5,
        out_specs=(VMEM,) * 4,
        compiler_params=pltpu.CompilerParams(vmem_limit_bytes=16 << 20),
        cost_estimate=pl.CostEstimate(flops=5_000_000_000, bytes_accessed=2_000_000, transcendentals=200_000),
        name="fresh",
    )(core, queries, fresh_keys, fresh_values, routes, gates)
    fresh_other = lax.ppermute(fresh_away, "expert", swap)
    stale = pl.pallas_call(
        attend_kernel,
        out_shape=jax.ShapeDtypeStruct((2 * heads, tokens // 2, LANES), BF16),
        in_specs=[VMEM, ANY],
        out_specs=VMEM,
        compiler_params=pltpu.CompilerParams(vmem_limit_bytes=16 << 20),
        cost_estimate=pl.CostEstimate(flops=100_000_000_000, bytes_accessed=2_000_000, transcendentals=1_000_000),
        name="attend",
    )(gathered, fresh_other)
    far = lax.all_to_all(stale, ("patch", "expert"), split_axis=0, concat_axis=0, tiled=True)
    hidden, buffer = pl.pallas_call(
        home_kernel,
        out_shape=(
            jax.ShapeDtypeStruct((rows, features), F32),
            jax.ShapeDtypeStruct((EXPERTS * (rows // 4), features), BF16),
        ),
        in_specs=[SMEM] + [VMEM] * 3 + [ANY] * 2 + [VMEM] * 3,
        out_specs=(VMEM, VMEM),
        scratch_shapes=[
            pltpu.VMEM((2, rows, width), BF16),
            pltpu.VMEM((2,) + out_weight.shape, BF16),
            pltpu.SemaphoreType.DMA((2,)),
        ],
        compiler_params=pltpu.CompilerParams(vmem_limit_bytes=20 << 20),
        cost_estimate=pl.CostEstimate(flops=200_000_000_000, bytes_accessed=8_000_000, transcendentals=100_000),
        name="home",
    )(core, far.reshape(heads, 2, rows, LANES), fresh_own, fresh_other, out_weight, w_other, residual, modulation, picks)
    return hidden, buffer, picks, gates


def split_heads(block_rows):
    return block_rows.reshape(block_rows.shape[0], block_rows.shape[1] // HEAD_DIM, HEAD_DIM)


def head_scores(query_heads, key_rows):
    products = jnp.einsum("qhd,khd->qhk", query_heads, split_heads(key_rows), preferred_element_type=F32)
    return products * SCALE


def weighted_values(weights, value_rows):
    return jnp.einsum(
        "qhk,khd->qhd", weights.astype(BF16), split_heads(value_rows), preferred_element_type=F32
    )


def attention_by_gather(queries, fresh_keys, fresh_values, stale_keys, stale_values, out_weight, residual, modulation, routes, gates):
    row_count = queries.shape[0]
    own_start = lax.axis_index("patch") * row_count
    query_heads = split_heads(queries)
    scores = head_scores(query_heads, fresh_keys)
    running_max = scores.max(-1)
    weights = jnp.exp(scores - running_max[..., None])
    denominator, numerator = weights.sum(-1), weighted_values(weights, fresh_values)
    piece_keys = lax.all_gather(stale_keys, "patch", axis=0, tiled=True)
    piece_values = lax.all_gather(stale_values, "patch", axis=0, tiled=True)
    scores = head_scores(query_heads, piece_keys)
    positions = jnp.arange(piece_keys.shape[0], dtype=jnp.int32)
    own_rows = (positions >= own_start) & (positions < own_start + row_count)
    scores = jnp.where(own_rows[None, None, :], -1e30, scores)
    newest = jnp.maximum(running_max, scores.max(-1))
    rescale = jnp.exp(running_max - newest)
    weights = jnp.where(own_rows[None, None, :], 0.0, jnp.exp(scores - newest[..., None]))
    denominator = denominator * rescale + weights.sum(-1)
    numerator = numerator * rescale[..., None] + weighted_values(weights, piece_values)
    attended = (numerator / denominator[..., None]).reshape(queries.shape).astype(BF16)
    hidden = residual.astype(F32) + lax.psum_scatter(
        jnp.dot(attended, out_weight, preferred_element_type=F32).astype(BF16),
        "expert",
        scatter_dimension=0,
        tiled=True,
    ).astype(F32)
    centered = hidden - hidden.mean(-1, keepdims=True)
    variance = (centered * centered).mean(-1, keepdims=True)
    normed = (centered / jnp.sqrt(variance + 1e-06) * (1.0 + modulation[1]) + modulation[0]).astype(BF16)
    capacity = residual.shape[0] // 4
    picks = [chosen(slot, EXPERTS * capacity) for slot in slots_of(routes, capacity)]
    return hidden, contract(picks[0] + picks[1], normed, 0, 0).astype(BF16), jnp.stack(picks), gates


def expert_kernel(x_ref, up_ref, down_ref, out_ref, units_ref):
    for part in chunks(up_ref.shape[2]):
        units_ref[:, part] = jax.nn.gelu(
            jnp.dot(x_ref[...], up_ref[0, :, part], preferred_element_type=F32), approximate=True
        ).astype(BF16)
    for part in chunks(out_ref.shape[1]):
        out_ref[:, part] = jnp.dot(
            units_ref[...], down_ref[0, :, part], preferred_element_type=F32
        ).astype(BF16)


def chunks(width):
    step = 896 if width % 896 == 0 else LANES
    return [slice(i, i + step) for i in range(0, width, step)]


def expert_slice(inputs, up_weight, down_weight):
    rows, features = inputs.shape
    return pl.pallas_call(
        expert_kernel,
        out_shape=jax.ShapeDtypeStruct((rows, features), BF16),
        in_specs=[VMEM] * 3,
        out_specs=VMEM,
        scratch_shapes=[pltpu.VMEM((rows, up_weight.shape[2]), BF16)],
        compiler_params=pltpu.CompilerParams(vmem_limit_bytes=16 << 20),
        name="experts",
    )(inputs, up_weight, down_weight)


def combine_kernel(hidden_ref, picks_ref, gates_ref, returned_ref, out_ref):
    slices = returned_ref.shape[1]
    slots = returned_ref.shape[0] * returned_ref.shape[2]
    mixed = hidden_ref[...]
    for s in range(slices):
        rows = returned_ref[:, s].reshape(slots, returned_ref.shape[3])
        for k in range(TOPK):
            mixed += gates_ref[:, k : k + 1] * jnp.dot(picks_ref[k], rows, preferred_element_type=F32)
    out_ref[...] = mixed.astype(BF16)


def body(
    queries, fresh_keys, fresh_values, stale_keys, stale_values, residual, out_weight, modulation,
    up_weight, down_weight, routes, gates,
):
    rows, features = residual.shape
    patch_count = lax.axis_size("patch")
    device_count = patch_count * lax.axis_size("expert")
    by_heads = queries.shape[1] // HEAD_DIM == patch_count and patch_count % 2 == 0 and lax.axis_size("expert") == 2
    attention = attention_by_heads if by_heads else attention_by_gather
    hidden, buffer, picks, gates = attention(
        queries, fresh_keys, fresh_values, stale_keys, stale_values, out_weight, residual, modulation, routes, gates
    )
    capacity = rows // 4
    slice_count = device_count // EXPERTS
    outgoing = jnp.broadcast_to(
        buffer.reshape(EXPERTS, 1, capacity, features), (EXPERTS, slice_count, capacity, features)
    ).reshape(device_count, capacity, features)
    arrived = lax.all_to_all(outgoing, ("patch", "expert"), split_axis=0, concat_axis=0, tiled=True)
    outputs = expert_slice(arrived.reshape(device_count * capacity, features), up_weight, down_weight)
    returned = lax.all_to_all(
        outputs.reshape(device_count, capacity, features),
        ("patch", "expert"),
        split_axis=0,
        concat_axis=0,
        tiled=True,
    )
    return pl.pallas_call(
        combine_kernel,
        out_shape=jax.ShapeDtypeStruct((rows, features), BF16),
        in_specs=[VMEM] * 4,
        out_specs=VMEM,
        compiler_params=pltpu.CompilerParams(vmem_limit_bytes=20 << 20),
        name="combine",
    )(hidden, picks, gates, returned.reshape(EXPERTS, slice_count, capacity, features))


def solution(mesh):
    tokens = P(("group", "patch"), "expert")
    rows = P(("group", "patch", "expert"), None)
    weight = P(("patch", "expert"), None, None)
    placed = (
        tokens, tokens, tokens, tokens, tokens, rows, P("expert", None), P("group", None), weight, weight, rows, rows,
    )
    return jax.shard_map(body, mesh=mesh, in_specs=placed, out_specs=rows, check_vma=False)
```

```python
import functools
import math

import jax
import jax.numpy as jnp
from jax import lax
from jax.experimental import pallas as pl
from jax.experimental.pallas import tpu as pltpu
from jax.sharding import PartitionSpec as P

HEAD_DIM = 112
EXPERTS = 16
TOPK = 2
LANES = 128
SCALE = 1.0 / math.sqrt(HEAD_DIM)
BF16 = jnp.bfloat16
F32 = jnp.float32
VMEM = pl.BlockSpec(memory_space=pltpu.VMEM)
SMEM = pl.BlockSpec(memory_space=pltpu.SMEM)
ANY = pl.BlockSpec(memory_space=pl.ANY)


def contract(a, b, dim_a, dim_b):
    return lax.dot_general(a, b, (((dim_a,), (dim_b,)), ((), ())), preferred_element_type=F32)


def pack_kernel(q_ref, k_ref, v_ref, out_ref):
    for i, ref in enumerate((q_ref, k_ref, v_ref)):
        turned = ref[...].T
        for h in range(out_ref.shape[0]):
            out_ref[h, i * HEAD_DIM : (i + 1) * HEAD_DIM, :] = turned[
                h * HEAD_DIM : (h + 1) * HEAD_DIM
            ]


def with_ones(values):
    return jnp.concatenate([values, jnp.ones((LANES - HEAD_DIM, values.shape[1]), BF16)], axis=0)


def partial_softmax(query, keys, values):
    scores = contract(query, keys, 0, 0)
    top = scores.max(-1, keepdims=True)
    weights = jnp.exp((scores - top) * SCALE).astype(BF16)
    return contract(weights, with_ones(values), 1, 1), top * SCALE


def fresh_kernel(
    core_ref, q_ref, k_ref, v_ref, routes_ref, gates_ref, own_ref, other_ref, picks_ref, gates_out_ref
):
    q, k, v = q_ref[...].T, k_ref[...].T, v_ref[...].T
    half = q.shape[1] // 2
    first = core_ref[0] == 0
    lane = lax.broadcasted_iota(jnp.int32, (2 * half, LANES), 1)
    for h in range(q.shape[0] // HEAD_DIM):
        rows = slice(h * HEAD_DIM, (h + 1) * HEAD_DIM)
        sums, top = partial_softmax(q[rows], k[rows], v[rows])
        sums = jnp.where(lane == HEAD_DIM + 1, top, sums)
        lanes = slice(h * LANES, (h + 1) * LANES)
        own_ref[:, lanes] = jnp.where(first, sums[:half], sums[half:])
        other_ref[:, lanes] = jnp.where(first, sums[half:], sums[:half])
    slots = picks_ref.shape[2]
    for k, slot in enumerate(slots_of(routes_ref[...], slots // EXPERTS)):
        picks_ref[k] = chosen(slot, slots)
    gates_out_ref[...] = gates_ref[...]


def attend_kernel(in_ref, fresh_ref, out_ref):
    patches, tokens = in_ref.shape[0], in_ref.shape[2]
    half, rows, steps = tokens // 2, 2 * tokens, patches // 2
    keys = jnp.concatenate([in_ref[j, HEAD_DIM : 2 * HEAD_DIM] for j in range(patches)], axis=1)
    values = with_ones(jnp.concatenate([in_ref[j, 2 * HEAD_DIM :] for j in range(patches)], axis=1))
    lane = lax.broadcasted_iota(jnp.int32, (rows, LANES), 1)
    own = (lax.broadcasted_iota(jnp.int32, (rows, rows), 0) < tokens) == (
        lax.broadcasted_iota(jnp.int32, (rows, rows), 1) < tokens
    )

    def scores_of(step):
        query = jnp.concatenate([in_ref[2 * step + i, :HEAD_DIM] for i in range(2)], axis=1)
        scores = contract(query, keys, 0, 0)
        first, last = step * rows, (step + 1) * rows
        parts = [jnp.where(own, -1e30, scores[:, first:last])]
        if step > 0:
            parts.insert(0, scores[:, :first])
        if step < steps - 1:
            parts.append(scores[:, last:])
        return jnp.concatenate(parts, axis=1)

    scores = scores_of(0)
    for step in range(steps):
        following = scores_of(step + 1) if step < steps - 1 else None
        top = scores.max(-1, keepdims=True)
        weights = jnp.exp2((scores - top) * (SCALE * math.log2(math.e))).astype(BF16)
        sums = contract(weights, values, 1, 1)
        total = sums[:, HEAD_DIM : HEAD_DIM + 1]
        log_total = top * SCALE + jnp.log(total)
        high = log_total.astype(BF16).astype(F32)
        rest = log_total - high
        middle = rest.astype(BF16).astype(F32)
        result = sums * (1.0 / total)
        result = jnp.where(lane == HEAD_DIM, high, result)
        result = jnp.where(lane == HEAD_DIM + 1, middle, result)
        result = jnp.where(lane == HEAD_DIM + 2, rest - middle, result)
        result = result.astype(BF16)
        for i in range(4):
            out_ref[4 * step + i] = result[i * half : (i + 1) * half]
        scores = following


def slots_of(routes, capacity):
    rows = routes.shape[0]
    expert = lax.broadcasted_iota(jnp.int32, (rows, EXPERTS), 1)
    names = [expert == routes[:, k : k + 1] for k in range(TOPK)]
    named = sum(n.astype(F32) for n in names).astype(BF16)
    earlier = (
        lax.broadcasted_iota(jnp.int32, (rows, rows), 1)
        < lax.broadcasted_iota(jnp.int32, (rows, rows), 0)
    ).astype(F32).astype(BF16)
    count = jnp.dot(earlier, named, preferred_element_type=F32)
    return [
        routes[:, k : k + 1] * capacity
        + jnp.where(names[k], count, 0.0).sum(-1, keepdims=True).astype(jnp.int32)
        for k in range(TOPK)
    ]


def chosen(slot, slots):
    return (
        (lax.broadcasted_iota(jnp.int32, (slot.shape[0], slots), 1) == slot).astype(F32).astype(BF16)
    )


def home_kernel(
    core_ref, far_ref, own_ref, other_ref, w_own_ref, w_other_ref, residual_ref, modulation_ref,
    hidden_ref, normed_ref, attended_ref, w_ref, loaded_ref,
):
    loads = [
        pltpu.make_async_copy(source, w_ref.at[i], loaded_ref.at[i])
        for i, source in enumerate((w_own_ref, w_other_ref))
    ]
    for load in loads:
        load.start()
    heads = far_ref.shape[0]
    core = core_ref[0]
    projected = None
    for side, near_ref in enumerate((own_ref, other_ref)):
        which = core if side == 0 else 1 - core
        for h in range(heads):
            far = far_ref[h, which].astype(F32)
            near = near_ref[:, h * LANES : (h + 1) * LANES]
            far_log = (
                far[:, HEAD_DIM : HEAD_DIM + 1]
                + far[:, HEAD_DIM + 1 : HEAD_DIM + 2]
                + far[:, HEAD_DIM + 2 : HEAD_DIM + 3]
            )
            near_total = near[:, HEAD_DIM : HEAD_DIM + 1]
            near_top = near[:, HEAD_DIM + 1 : HEAD_DIM + 2]
            top = jnp.maximum(far_log, near_top)
            far_weight = jnp.exp(far_log - top)
            near_weight = jnp.exp(near_top - top)
            scale = 1.0 / (far_weight + near_total * near_weight)
            merged = far * (far_weight * scale) + near * (near_weight * scale)
            attended_ref[side, :, h * HEAD_DIM : (h + 1) * HEAD_DIM] = merged[:, :HEAD_DIM].astype(BF16)
    for side in range(2):
        loads[side].wait()
        part = jnp.dot(attended_ref[side], w_ref[side], preferred_element_type=F32)
        projected = part if projected is None else projected + part
    hidden = residual_ref[...].astype(F32) + projected
    hidden_ref[...] = hidden
    centered = hidden - hidden.mean(-1, keepdims=True)
    variance = (centered * centered).mean(-1, keepdims=True)
    normed_ref[...] = (
        centered / jnp.sqrt(variance + 1e-06) * (1.0 + modulation_ref[1:2]) + modulation_ref[0:1]
    ).astype(BF16)


def slots_kernel(normed_ref, picks_ref, buffer_ref):
    buffer_ref[...] = contract(picks_ref[0] + picks_ref[1], normed_ref[...], 0, 0).astype(BF16)


def attention_by_heads(queries, fresh_keys, fresh_values, stale_keys, stale_values, out_weight, residual, modulation, routes, gates):
    tokens, width = queries.shape
    heads = width // HEAD_DIM
    rows, features = residual.shape
    core = lax.axis_index("expert").astype(jnp.int32).reshape(1)
    swap = [(0, 1), (1, 0)]
    packed = pl.pallas_call(
        pack_kernel,
        out_shape=jax.ShapeDtypeStruct((heads, 3 * HEAD_DIM, tokens), BF16),
        in_specs=[VMEM] * 3,
        out_specs=VMEM,
        name="pack",
    )(queries, stale_keys, stale_values)
    w_other = lax.ppermute(out_weight, "expert", swap)
    gathered = lax.all_to_all(packed, "patch", split_axis=0, concat_axis=0, tiled=True)
    fresh_shape = jax.ShapeDtypeStruct((tokens // 2, heads * LANES), F32)
    slots = EXPERTS * (rows // 4)
    fresh_own, fresh_away, picks, gates = pl.pallas_call(
        fresh_kernel,
        out_shape=(
            fresh_shape,
            fresh_shape,
            jax.ShapeDtypeStruct((TOPK, rows, slots), BF16),
            jax.ShapeDtypeStruct(gates.shape, F32),
        ),
        in_specs=[SMEM] + [VMEM] * 5,
        out_specs=(VMEM,) * 4,
        compiler_params=pltpu.CompilerParams(vmem_limit_bytes=16 << 20),
        cost_estimate=pl.CostEstimate(flops=5_000_000_000, bytes_accessed=2_000_000, transcendentals=200_000),
        name="fresh",
    )(core, queries, fresh_keys, fresh_values, routes, gates)
    fresh_other = lax.ppermute(fresh_away, "expert", swap)
    stale = pl.pallas_call(
        attend_kernel,
        out_shape=jax.ShapeDtypeStruct((2 * heads, tokens // 2, LANES), BF16),
        in_specs=[VMEM, ANY],
        out_specs=VMEM,
        compiler_params=pltpu.CompilerParams(vmem_limit_bytes=16 << 20),
        cost_estimate=pl.CostEstimate(flops=100_000_000_000, bytes_accessed=2_000_000, transcendentals=1_000_000),
        name="attend",
    )(gathered, fresh_other)
    far = lax.all_to_all(stale, ("patch", "expert"), split_axis=0, concat_axis=0, tiled=True)
    hidden, normed = pl.pallas_call(
        home_kernel,
        out_shape=(
            jax.ShapeDtypeStruct((rows, features), F32),
            jax.ShapeDtypeStruct((rows, features), BF16),
        ),
        in_specs=[SMEM] + [VMEM] * 3 + [ANY] * 2 + [VMEM] * 2,
        out_specs=(VMEM, VMEM),
        scratch_shapes=[
            pltpu.VMEM((2, rows, width), BF16),
            pltpu.VMEM((2,) + out_weight.shape, BF16),
            pltpu.SemaphoreType.DMA((2,)),
        ],
        compiler_params=pltpu.CompilerParams(vmem_limit_bytes=20 << 20),
        cost_estimate=pl.CostEstimate(flops=4_000_000_000, bytes_accessed=8_000_000, transcendentals=100_000),
        name="home",
    )(core, far.reshape(heads, 2, rows, LANES), fresh_own, fresh_other, out_weight, w_other, residual, modulation)
    buffer = pl.pallas_call(
        slots_kernel,
        out_shape=jax.ShapeDtypeStruct((slots, features), BF16),
        in_specs=[VMEM] * 2,
        out_specs=VMEM,
        compiler_params=pltpu.CompilerParams(vmem_limit_bytes=12 << 20),
        cost_estimate=pl.CostEstimate(flops=200_000_000_000, bytes_accessed=8_000_000, transcendentals=100_000),
        name="slots",
    )(normed, picks)
    return hidden, buffer, picks, gates


def split_heads(block_rows):
    return block_rows.reshape(block_rows.shape[0], block_rows.shape[1] // HEAD_DIM, HEAD_DIM)


def head_scores(query_heads, key_rows):
    products = jnp.einsum("qhd,khd->qhk", query_heads, split_heads(key_rows), preferred_element_type=F32)
    return products * SCALE


def weighted_values(weights, value_rows):
    return jnp.einsum(
        "qhk,khd->qhd", weights.astype(BF16), split_heads(value_rows), preferred_element_type=F32
    )


def attention_by_gather(queries, fresh_keys, fresh_values, stale_keys, stale_values, out_weight, residual, modulation, routes, gates):
    row_count = queries.shape[0]
    own_start = lax.axis_index("patch") * row_count
    query_heads = split_heads(queries)
    scores = head_scores(query_heads, fresh_keys)
    running_max = scores.max(-1)
    weights = jnp.exp(scores - running_max[..., None])
    denominator, numerator = weights.sum(-1), weighted_values(weights, fresh_values)
    piece_keys = lax.all_gather(stale_keys, "patch", axis=0, tiled=True)
    piece_values = lax.all_gather(stale_values, "patch", axis=0, tiled=True)
    scores = head_scores(query_heads, piece_keys)
    positions = jnp.arange(piece_keys.shape[0], dtype=jnp.int32)
    own_rows = (positions >= own_start) & (positions < own_start + row_count)
    scores = jnp.where(own_rows[None, None, :], -1e30, scores)
    newest = jnp.maximum(running_max, scores.max(-1))
    rescale = jnp.exp(running_max - newest)
    weights = jnp.where(own_rows[None, None, :], 0.0, jnp.exp(scores - newest[..., None]))
    denominator = denominator * rescale + weights.sum(-1)
    numerator = numerator * rescale[..., None] + weighted_values(weights, piece_values)
    attended = (numerator / denominator[..., None]).reshape(queries.shape).astype(BF16)
    hidden = residual.astype(F32) + lax.psum_scatter(
        jnp.dot(attended, out_weight, preferred_element_type=F32).astype(BF16),
        "expert",
        scatter_dimension=0,
        tiled=True,
    ).astype(F32)
    centered = hidden - hidden.mean(-1, keepdims=True)
    variance = (centered * centered).mean(-1, keepdims=True)
    normed = (centered / jnp.sqrt(variance + 1e-06) * (1.0 + modulation[1]) + modulation[0]).astype(BF16)
    capacity = residual.shape[0] // 4
    picks = [chosen(slot, EXPERTS * capacity) for slot in slots_of(routes, capacity)]
    return hidden, contract(picks[0] + picks[1], normed, 0, 0).astype(BF16), jnp.stack(picks), gates


def expert_kernel(x_ref, up_ref, down_ref, out_ref, units_ref):
    for part in chunks(up_ref.shape[2]):
        units_ref[:, part] = jax.nn.gelu(
            jnp.dot(x_ref[...], up_ref[0, :, part], preferred_element_type=F32), approximate=True
        ).astype(BF16)
    for part in chunks(out_ref.shape[1]):
        out_ref[:, part] = jnp.dot(
            units_ref[...], down_ref[0, :, part], preferred_element_type=F32
        ).astype(BF16)


def chunks(width):
    step = 896 if width % 896 == 0 else LANES
    return [slice(i, i + step) for i in range(0, width, step)]


def expert_slice(inputs, up_weight, down_weight):
    rows, features = inputs.shape
    return pl.pallas_call(
        expert_kernel,
        out_shape=jax.ShapeDtypeStruct((rows, features), BF16),
        in_specs=[VMEM] * 3,
        out_specs=VMEM,
        scratch_shapes=[pltpu.VMEM((rows, up_weight.shape[2]), BF16)],
        compiler_params=pltpu.CompilerParams(vmem_limit_bytes=16 << 20),
        name="experts",
    )(inputs, up_weight, down_weight)


def combine_kernel(hidden_ref, picks_ref, gates_ref, returned_ref, out_ref):
    slices = returned_ref.shape[1]
    slots = returned_ref.shape[0] * returned_ref.shape[2]
    mixed = hidden_ref[...]
    for s in range(slices):
        rows = returned_ref[:, s].reshape(slots, returned_ref.shape[3])
        for k in range(TOPK):
            mixed += gates_ref[:, k : k + 1] * jnp.dot(picks_ref[k], rows, preferred_element_type=F32)
    out_ref[...] = mixed.astype(BF16)


def body(
    queries, fresh_keys, fresh_values, stale_keys, stale_values, residual, out_weight, modulation,
    up_weight, down_weight, routes, gates,
):
    rows, features = residual.shape
    patch_count = lax.axis_size("patch")
    device_count = patch_count * lax.axis_size("expert")
    by_heads = queries.shape[1] // HEAD_DIM == patch_count and patch_count % 2 == 0 and lax.axis_size("expert") == 2
    attention = attention_by_heads if by_heads else attention_by_gather
    hidden, buffer, picks, gates = attention(
        queries, fresh_keys, fresh_values, stale_keys, stale_values, out_weight, residual, modulation, routes, gates
    )
    capacity = rows // 4
    slice_count = device_count // EXPERTS
    outgoing = jnp.broadcast_to(
        buffer.reshape(EXPERTS, 1, capacity, features), (EXPERTS, slice_count, capacity, features)
    ).reshape(device_count, capacity, features)
    arrived = lax.all_to_all(outgoing, ("patch", "expert"), split_axis=0, concat_axis=0, tiled=True)
    outputs = expert_slice(arrived.reshape(device_count * capacity, features), up_weight, down_weight)
    returned = lax.all_to_all(
        outputs.reshape(device_count, capacity, features),
        ("patch", "expert"),
        split_axis=0,
        concat_axis=0,
        tiled=True,
    )
    return pl.pallas_call(
        combine_kernel,
        out_shape=jax.ShapeDtypeStruct((rows, features), BF16),
        in_specs=[VMEM] * 4,
        out_specs=VMEM,
        compiler_params=pltpu.CompilerParams(vmem_limit_bytes=20 << 20),
        name="combine",
    )(hidden, picks, gates, returned.reshape(EXPERTS, slice_count, capacity, features))


def solution(mesh):
    tokens = P(("group", "patch"), "expert")
    rows = P(("group", "patch", "expert"), None)
    weight = P(("patch", "expert"), None, None)
    placed = (
        tokens, tokens, tokens, tokens, tokens, rows, P("expert", None), P("group", None), weight, weight, rows, rows,
    )
    return jax.shard_map(body, mesh=mesh, in_specs=placed, out_specs=rows, check_vma=False)
```

```python
import functools
import math

import jax
import jax.numpy as jnp
from jax import lax
from jax.experimental import pallas as pl
from jax.experimental.pallas import tpu as pltpu
from jax.sharding import PartitionSpec as P

HEAD_DIM = 112
EXPERTS = 16
TOPK = 2
LANES = 128
SCALE = 1.0 / math.sqrt(HEAD_DIM)
BF16 = jnp.bfloat16
F32 = jnp.float32
VMEM = pl.BlockSpec(memory_space=pltpu.VMEM)
SMEM = pl.BlockSpec(memory_space=pltpu.SMEM)
ANY = pl.BlockSpec(memory_space=pl.ANY)


def contract(a, b, dim_a, dim_b):
    return lax.dot_general(a, b, (((dim_a,), (dim_b,)), ((), ())), preferred_element_type=F32)


def pack_kernel(q_ref, k_ref, v_ref, out_ref):
    for i, ref in enumerate((q_ref, k_ref, v_ref)):
        turned = ref[...].T
        for h in range(out_ref.shape[0]):
            out_ref[h, i * HEAD_DIM : (i + 1) * HEAD_DIM, :] = turned[
                h * HEAD_DIM : (h + 1) * HEAD_DIM
            ]


def with_ones(values):
    return jnp.concatenate([values, jnp.ones((LANES - HEAD_DIM, values.shape[1]), BF16)], axis=0)


def partial_softmax(query, keys, values):
    scores = contract(query, keys, 0, 0)
    top = scores.max(-1, keepdims=True)
    weights = jnp.exp((scores - top) * SCALE).astype(BF16)
    return contract(weights, with_ones(values), 1, 1), top * SCALE


def fresh_kernel(
    core_ref, q_ref, k_ref, v_ref, routes_ref, gates_ref, own_ref, other_ref, picks_ref, gates_out_ref
):
    q, k, v = q_ref[...].T, k_ref[...].T, v_ref[...].T
    half = q.shape[1] // 2
    first = core_ref[0] == 0
    lane = lax.broadcasted_iota(jnp.int32, (2 * half, LANES), 1)
    for h in range(q.shape[0] // HEAD_DIM):
        rows = slice(h * HEAD_DIM, (h + 1) * HEAD_DIM)
        sums, top = partial_softmax(q[rows], k[rows], v[rows])
        sums = jnp.where(lane == HEAD_DIM + 1, top, sums)
        lanes = slice(h * LANES, (h + 1) * LANES)
        own_ref[:, lanes] = jnp.where(first, sums[:half], sums[half:])
        other_ref[:, lanes] = jnp.where(first, sums[half:], sums[:half])
    slots = picks_ref.shape[2]
    for k, slot in enumerate(slots_of(routes_ref[...], slots // EXPERTS)):
        picks_ref[k] = chosen(slot, slots)
    gates_out_ref[...] = gates_ref[...]


def attend_kernel(in_ref, fresh_ref, out_ref):
    patches, tokens = in_ref.shape[0], in_ref.shape[2]
    half, rows, steps = tokens // 2, 2 * tokens, patches // 2
    keys = jnp.concatenate([in_ref[j, HEAD_DIM : 2 * HEAD_DIM] for j in range(patches)], axis=1)
    values = with_ones(jnp.concatenate([in_ref[j, 2 * HEAD_DIM :] for j in range(patches)], axis=1))
    lane = lax.broadcasted_iota(jnp.int32, (rows, LANES), 1)
    own = (lax.broadcasted_iota(jnp.int32, (rows, rows), 0) < tokens) == (
        lax.broadcasted_iota(jnp.int32, (rows, rows), 1) < tokens
    )

    def scores_of(step):
        query = jnp.concatenate([in_ref[2 * step + i, :HEAD_DIM] for i in range(2)], axis=1)
        scores = contract(query, keys, 0, 0)
        first, last = step * rows, (step + 1) * rows
        parts = [jnp.where(own, -1e30, scores[:, first:last])]
        if step > 0:
            parts.insert(0, scores[:, :first])
        if step < steps - 1:
            parts.append(scores[:, last:])
        return jnp.concatenate(parts, axis=1)

    scores = scores_of(0)
    for step in range(steps):
        following = scores_of(step + 1) if step < steps - 1 else None
        top = scores.max(-1, keepdims=True)
        weights = jnp.exp2((scores - top) * (SCALE * math.log2(math.e))).astype(BF16)
        sums = contract(weights, values, 1, 1)
        total = sums[:, HEAD_DIM : HEAD_DIM + 1]
        log_total = top * SCALE + jnp.log(total)
        high = log_total.astype(BF16).astype(F32)
        rest = log_total - high
        middle = rest.astype(BF16).astype(F32)
        result = sums * (1.0 / total)
        result = jnp.where(lane == HEAD_DIM, high, result)
        result = jnp.where(lane == HEAD_DIM + 1, middle, result)
        result = jnp.where(lane == HEAD_DIM + 2, rest - middle, result)
        result = result.astype(BF16)
        for i in range(4):
            out_ref[4 * step + i] = result[i * half : (i + 1) * half]
        scores = following


def slots_of(routes, capacity):
    rows = routes.shape[0]
    expert = lax.broadcasted_iota(jnp.int32, (rows, EXPERTS), 1)
    names = [expert == routes[:, k : k + 1] for k in range(TOPK)]
    named = sum(n.astype(F32) for n in names).astype(BF16)
    earlier = (
        lax.broadcasted_iota(jnp.int32, (rows, rows), 1)
        < lax.broadcasted_iota(jnp.int32, (rows, rows), 0)
    ).astype(F32).astype(BF16)
    count = jnp.dot(earlier, named, preferred_element_type=F32)
    return [
        routes[:, k : k + 1] * capacity
        + jnp.where(names[k], count, 0.0).sum(-1, keepdims=True).astype(jnp.int32)
        for k in range(TOPK)
    ]


def chosen(slot, slots):
    return (
        (lax.broadcasted_iota(jnp.int32, (slot.shape[0], slots), 1) == slot).astype(F32).astype(BF16)
    )


def home_kernel(
    core_ref, far_ref, own_ref, other_ref, w_own_ref, w_other_ref, residual_ref, modulation_ref,
    hidden_ref, normed_ref, attended_ref, w_ref, loaded_ref,
):
    parts = loaded_ref.shape[1]
    share = w_own_ref.shape[0] // parts
    loads = [
        [
            pltpu.make_async_copy(
                source.at[pl.ds(j * share, share)], w_ref.at[i, pl.ds(j * share, share)], loaded_ref.at[i, j]
            )
            for j in range(parts)
        ]
        for i, source in enumerate((w_own_ref, w_other_ref))
    ]
    for load in loads[0] + loads[1]:
        load.start()
    heads = far_ref.shape[0]
    core = core_ref[0]
    projected = None
    for side, near_ref in enumerate((own_ref, other_ref)):
        which = core if side == 0 else 1 - core
        for h in range(heads):
            far = far_ref[h, which].astype(F32)
            near = near_ref[:, h * LANES : (h + 1) * LANES]
            far_log = (
                far[:, HEAD_DIM : HEAD_DIM + 1]
                + far[:, HEAD_DIM + 1 : HEAD_DIM + 2]
                + far[:, HEAD_DIM + 2 : HEAD_DIM + 3]
            )
            near_total = near[:, HEAD_DIM : HEAD_DIM + 1]
            near_top = near[:, HEAD_DIM + 1 : HEAD_DIM + 2]
            top = jnp.maximum(far_log, near_top)
            far_weight = jnp.exp(far_log - top)
            near_weight = jnp.exp(near_top - top)
            scale = 1.0 / (far_weight + near_total * near_weight)
            merged = far * (far_weight * scale) + near * (near_weight * scale)
            attended_ref[side, :, h * HEAD_DIM : (h + 1) * HEAD_DIM] = merged[:, :HEAD_DIM].astype(BF16)
    for side in range(2):
        for load in loads[side]:
            load.wait()
        part = jnp.dot(attended_ref[side], w_ref[side], preferred_element_type=F32)
        projected = part if projected is None else projected + part
    hidden = residual_ref[...].astype(F32) + projected
    hidden_ref[...] = hidden
    centered = hidden - hidden.mean(-1, keepdims=True)
    variance = (centered * centered).mean(-1, keepdims=True)
    normed_ref[...] = (
        centered / jnp.sqrt(variance + 1e-06) * (1.0 + modulation_ref[1:2]) + modulation_ref[0:1]
    ).astype(BF16)


def slots_kernel(normed_ref, picks_ref, buffer_ref):
    buffer_ref[...] = contract(picks_ref[0] + picks_ref[1], normed_ref[...], 0, 0).astype(BF16)


def attention_by_heads(queries, fresh_keys, fresh_values, stale_keys, stale_values, out_weight, residual, modulation, routes, gates):
    tokens, width = queries.shape
    heads = width // HEAD_DIM
    rows, features = residual.shape
    core = lax.axis_index("expert").astype(jnp.int32).reshape(1)
    swap = [(0, 1), (1, 0)]
    packed = pl.pallas_call(
        pack_kernel,
        out_shape=jax.ShapeDtypeStruct((heads, 3 * HEAD_DIM, tokens), BF16),
        in_specs=[VMEM] * 3,
        out_specs=VMEM,
        name="pack",
    )(queries, stale_keys, stale_values)
    w_other = lax.ppermute(out_weight, "expert", swap)
    gathered = lax.all_to_all(packed, "patch", split_axis=0, concat_axis=0, tiled=True)
    fresh_shape = jax.ShapeDtypeStruct((tokens // 2, heads * LANES), F32)
    slots = EXPERTS * (rows // 4)
    fresh_own, fresh_away, picks, gates = pl.pallas_call(
        fresh_kernel,
        out_shape=(
            fresh_shape,
            fresh_shape,
            jax.ShapeDtypeStruct((TOPK, rows, slots), BF16),
            jax.ShapeDtypeStruct(gates.shape, F32),
        ),
        in_specs=[SMEM] + [VMEM] * 5,
        out_specs=(VMEM,) * 4,
        compiler_params=pltpu.CompilerParams(vmem_limit_bytes=16 << 20),
        cost_estimate=pl.CostEstimate(flops=5_000_000_000, bytes_accessed=2_000_000, transcendentals=200_000),
        name="fresh",
    )(core, queries, fresh_keys, fresh_values, routes, gates)
    fresh_other = lax.ppermute(fresh_away, "expert", swap)
    stale = pl.pallas_call(
        attend_kernel,
        out_shape=jax.ShapeDtypeStruct((2 * heads, tokens // 2, LANES), BF16),
        in_specs=[VMEM, ANY],
        out_specs=VMEM,
        compiler_params=pltpu.CompilerParams(vmem_limit_bytes=16 << 20),
        cost_estimate=pl.CostEstimate(flops=100_000_000_000, bytes_accessed=2_000_000, transcendentals=1_000_000),
        name="attend",
    )(gathered, fresh_other)
    far = lax.all_to_all(stale, ("patch", "expert"), split_axis=0, concat_axis=0, tiled=True)
    hidden, normed = pl.pallas_call(
        home_kernel,
        out_shape=(
            jax.ShapeDtypeStruct((rows, features), F32),
            jax.ShapeDtypeStruct((rows, features), BF16),
        ),
        in_specs=[SMEM] + [VMEM] * 3 + [ANY] * 2 + [VMEM] * 2,
        out_specs=(VMEM, VMEM),
        scratch_shapes=[
            pltpu.VMEM((2, rows, width), BF16),
            pltpu.VMEM((2,) + out_weight.shape, BF16),
            pltpu.SemaphoreType.DMA((2, 7)),
        ],
        compiler_params=pltpu.CompilerParams(vmem_limit_bytes=20 << 20),
        cost_estimate=pl.CostEstimate(flops=4_000_000_000, bytes_accessed=8_000_000, transcendentals=100_000),
        name="home",
    )(core, far.reshape(heads, 2, rows, LANES), fresh_own, fresh_other, out_weight, w_other, residual, modulation)
    buffer = pl.pallas_call(
        slots_kernel,
        out_shape=jax.ShapeDtypeStruct((slots, features), BF16),
        in_specs=[VMEM] * 2,
        out_specs=VMEM,
        compiler_params=pltpu.CompilerParams(vmem_limit_bytes=12 << 20),
        cost_estimate=pl.CostEstimate(flops=200_000_000_000, bytes_accessed=8_000_000, transcendentals=100_000),
        name="slots",
    )(normed, picks)
    return hidden, buffer, picks, gates


def split_heads(block_rows):
    return block_rows.reshape(block_rows.shape[0], block_rows.shape[1] // HEAD_DIM, HEAD_DIM)


def head_scores(query_heads, key_rows):
    products = jnp.einsum("qhd,khd->qhk", query_heads, split_heads(key_rows), preferred_element_type=F32)
    return products * SCALE


def weighted_values(weights, value_rows):
    return jnp.einsum(
        "qhk,khd->qhd", weights.astype(BF16), split_heads(value_rows), preferred_element_type=F32
    )


def attention_by_gather(queries, fresh_keys, fresh_values, stale_keys, stale_values, out_weight, residual, modulation, routes, gates):
    row_count = queries.shape[0]
    own_start = lax.axis_index("patch") * row_count
    query_heads = split_heads(queries)
    scores = head_scores(query_heads, fresh_keys)
    running_max = scores.max(-1)
    weights = jnp.exp(scores - running_max[..., None])
    denominator, numerator = weights.sum(-1), weighted_values(weights, fresh_values)
    piece_keys = lax.all_gather(stale_keys, "patch", axis=0, tiled=True)
    piece_values = lax.all_gather(stale_values, "patch", axis=0, tiled=True)
    scores = head_scores(query_heads, piece_keys)
    positions = jnp.arange(piece_keys.shape[0], dtype=jnp.int32)
    own_rows = (positions >= own_start) & (positions < own_start + row_count)
    scores = jnp.where(own_rows[None, None, :], -1e30, scores)
    newest = jnp.maximum(running_max, scores.max(-1))
    rescale = jnp.exp(running_max - newest)
    weights = jnp.where(own_rows[None, None, :], 0.0, jnp.exp(scores - newest[..., None]))
    denominator = denominator * rescale + weights.sum(-1)
    numerator = numerator * rescale[..., None] + weighted_values(weights, piece_values)
    attended = (numerator / denominator[..., None]).reshape(queries.shape).astype(BF16)
    hidden = residual.astype(F32) + lax.psum_scatter(
        jnp.dot(attended, out_weight, preferred_element_type=F32).astype(BF16),
        "expert",
        scatter_dimension=0,
        tiled=True,
    ).astype(F32)
    centered = hidden - hidden.mean(-1, keepdims=True)
    variance = (centered * centered).mean(-1, keepdims=True)
    normed = (centered / jnp.sqrt(variance + 1e-06) * (1.0 + modulation[1]) + modulation[0]).astype(BF16)
    capacity = residual.shape[0] // 4
    picks = [chosen(slot, EXPERTS * capacity) for slot in slots_of(routes, capacity)]
    return hidden, contract(picks[0] + picks[1], normed, 0, 0).astype(BF16), jnp.stack(picks), gates


def expert_kernel(x_ref, up_ref, down_ref, out_ref, units_ref):
    for part in chunks(up_ref.shape[2]):
        units_ref[:, part] = jax.nn.gelu(
            jnp.dot(x_ref[...], up_ref[0, :, part], preferred_element_type=F32), approximate=True
        ).astype(BF16)
    for part in chunks(out_ref.shape[1]):
        out_ref[:, part] = jnp.dot(
            units_ref[...], down_ref[0, :, part], preferred_element_type=F32
        ).astype(BF16)


def chunks(width):
    step = 896 if width % 896 == 0 else LANES
    return [slice(i, i + step) for i in range(0, width, step)]


def expert_slice(inputs, up_weight, down_weight):
    rows, features = inputs.shape
    return pl.pallas_call(
        expert_kernel,
        out_shape=jax.ShapeDtypeStruct((rows, features), BF16),
        in_specs=[VMEM] * 3,
        out_specs=VMEM,
        scratch_shapes=[pltpu.VMEM((rows, up_weight.shape[2]), BF16)],
        compiler_params=pltpu.CompilerParams(vmem_limit_bytes=16 << 20),
        name="experts",
    )(inputs, up_weight, down_weight)


def combine_kernel(hidden_ref, picks_ref, gates_ref, returned_ref, out_ref):
    slices = returned_ref.shape[1]
    slots = returned_ref.shape[0] * returned_ref.shape[2]
    mixed = hidden_ref[...]
    for s in range(slices):
        rows = returned_ref[:, s].reshape(slots, returned_ref.shape[3])
        for k in range(TOPK):
            mixed += gates_ref[:, k : k + 1] * jnp.dot(picks_ref[k], rows, preferred_element_type=F32)
    out_ref[...] = mixed.astype(BF16)


def body(
    queries, fresh_keys, fresh_values, stale_keys, stale_values, residual, out_weight, modulation,
    up_weight, down_weight, routes, gates,
):
    rows, features = residual.shape
    patch_count = lax.axis_size("patch")
    device_count = patch_count * lax.axis_size("expert")
    by_heads = queries.shape[1] // HEAD_DIM == patch_count and patch_count % 2 == 0 and lax.axis_size("expert") == 2
    attention = attention_by_heads if by_heads else attention_by_gather
    hidden, buffer, picks, gates = attention(
        queries, fresh_keys, fresh_values, stale_keys, stale_values, out_weight, residual, modulation, routes, gates
    )
    capacity = rows // 4
    slice_count = device_count // EXPERTS
    outgoing = jnp.broadcast_to(
        buffer.reshape(EXPERTS, 1, capacity, features), (EXPERTS, slice_count, capacity, features)
    ).reshape(device_count, capacity, features)
    arrived = lax.all_to_all(outgoing, ("patch", "expert"), split_axis=0, concat_axis=0, tiled=True)
    outputs = expert_slice(arrived.reshape(device_count * capacity, features), up_weight, down_weight)
    returned = lax.all_to_all(
        outputs.reshape(device_count, capacity, features),
        ("patch", "expert"),
        split_axis=0,
        concat_axis=0,
        tiled=True,
    )
    return pl.pallas_call(
        combine_kernel,
        out_shape=jax.ShapeDtypeStruct((rows, features), BF16),
        in_specs=[VMEM] * 4,
        out_specs=VMEM,
        compiler_params=pltpu.CompilerParams(vmem_limit_bytes=20 << 20),
        name="combine",
    )(hidden, picks, gates, returned.reshape(EXPERTS, slice_count, capacity, features))


def solution(mesh):
    tokens = P(("group", "patch"), "expert")
    rows = P(("group", "patch", "expert"), None)
    weight = P(("patch", "expert"), None, None)
    placed = (
        tokens, tokens, tokens, tokens, tokens, rows, P("expert", None), P("group", None), weight, weight, rows, rows,
    )
    return jax.shard_map(body, mesh=mesh, in_specs=placed, out_specs=rows, check_vma=False)
```

```python
import functools
import math

import jax
import jax.numpy as jnp
from jax import lax
from jax.experimental import pallas as pl
from jax.experimental.pallas import tpu as pltpu
from jax.sharding import PartitionSpec as P

HEAD_DIM = 112
EXPERTS = 16
TOPK = 2
LANES = 128
SCALE = 1.0 / math.sqrt(HEAD_DIM)
BF16 = jnp.bfloat16
F32 = jnp.float32
VMEM = pl.BlockSpec(memory_space=pltpu.VMEM)
SMEM = pl.BlockSpec(memory_space=pltpu.SMEM)
ANY = pl.BlockSpec(memory_space=pl.ANY)


def contract(a, b, dim_a, dim_b):
    return lax.dot_general(a, b, (((dim_a,), (dim_b,)), ((), ())), preferred_element_type=F32)


def pack_kernel(q_ref, k_ref, v_ref, out_ref):
    for i, ref in enumerate((q_ref, k_ref, v_ref)):
        turned = ref[...].T
        for h in range(out_ref.shape[0]):
            out_ref[h, i * HEAD_DIM : (i + 1) * HEAD_DIM, :] = turned[
                h * HEAD_DIM : (h + 1) * HEAD_DIM
            ]


def with_ones(values):
    return jnp.concatenate([values, jnp.ones((LANES - HEAD_DIM, values.shape[1]), BF16)], axis=0)


def partial_softmax(query, keys, values):
    scores = contract(query, keys, 0, 0)
    top = scores.max(-1, keepdims=True)
    weights = jnp.exp((scores - top) * SCALE).astype(BF16)
    return contract(weights, with_ones(values), 1, 1), top * SCALE


def fresh_kernel(
    core_ref, q_ref, k_ref, v_ref, routes_ref, gates_ref, own_ref, other_ref, picks_ref, gates_out_ref
):
    q, k, v = q_ref[...].T, k_ref[...].T, v_ref[...].T
    half = q.shape[1] // 2
    first = core_ref[0] == 0
    lane = lax.broadcasted_iota(jnp.int32, (2 * half, LANES), 1)
    for h in range(q.shape[0] // HEAD_DIM):
        rows = slice(h * HEAD_DIM, (h + 1) * HEAD_DIM)
        sums, top = partial_softmax(q[rows], k[rows], v[rows])
        sums = jnp.where(lane == HEAD_DIM + 1, top, sums)
        lanes = slice(h * LANES, (h + 1) * LANES)
        own_ref[:, lanes] = jnp.where(first, sums[:half], sums[half:])
        other_ref[:, lanes] = jnp.where(first, sums[half:], sums[:half])
    slots = picks_ref.shape[2]
    for k, slot in enumerate(slots_of(routes_ref[...], slots // EXPERTS)):
        picks_ref[k] = chosen(slot, slots)
    gates_out_ref[...] = gates_ref[...]


def attend_kernel(in_ref, fresh_ref, out_ref):
    patches, tokens = in_ref.shape[0], in_ref.shape[2]
    half, rows, steps = tokens // 2, 2 * tokens, patches // 2
    keys = jnp.concatenate([in_ref[j, HEAD_DIM : 2 * HEAD_DIM] for j in range(patches)], axis=1)
    values = with_ones(jnp.concatenate([in_ref[j, 2 * HEAD_DIM :] for j in range(patches)], axis=1))
    lane = lax.broadcasted_iota(jnp.int32, (rows, LANES), 1)
    own = (lax.broadcasted_iota(jnp.int32, (rows, rows), 0) < tokens) == (
        lax.broadcasted_iota(jnp.int32, (rows, rows), 1) < tokens
    )

    def scores_of(step):
        query = jnp.concatenate([in_ref[2 * step + i, :HEAD_DIM] for i in range(2)], axis=1)
        scores = contract(query, keys, 0, 0)
        first, last = step * rows, (step + 1) * rows
        parts = [jnp.where(own, -1e30, scores[:, first:last])]
        if step > 0:
            parts.insert(0, scores[:, :first])
        if step < steps - 1:
            parts.append(scores[:, last:])
        return jnp.concatenate(parts, axis=1)

    scores = scores_of(0)
    for step in range(steps):
        following = scores_of(step + 1) if step < steps - 1 else None
        top = scores.max(-1, keepdims=True)
        weights = jnp.exp2((scores - top) * (SCALE * math.log2(math.e))).astype(BF16)
        sums = contract(weights, values, 1, 1)
        total = sums[:, HEAD_DIM : HEAD_DIM + 1]
        log_total = top * SCALE + jnp.log(total)
        high = log_total.astype(BF16).astype(F32)
        rest = log_total - high
        middle = rest.astype(BF16).astype(F32)
        result = sums * (1.0 / total)
        result = jnp.where(lane == HEAD_DIM, high, result)
        result = jnp.where(lane == HEAD_DIM + 1, middle, result)
        result = jnp.where(lane == HEAD_DIM + 2, rest - middle, result)
        result = result.astype(BF16)
        for i in range(4):
            out_ref[4 * step + i] = result[i * half : (i + 1) * half]
        scores = following


def slots_of(routes, capacity):
    rows = routes.shape[0]
    expert = lax.broadcasted_iota(jnp.int32, (rows, EXPERTS), 1)
    names = [expert == routes[:, k : k + 1] for k in range(TOPK)]
    named = sum(n.astype(F32) for n in names).astype(BF16)
    earlier = (
        lax.broadcasted_iota(jnp.int32, (rows, rows), 1)
        < lax.broadcasted_iota(jnp.int32, (rows, rows), 0)
    ).astype(F32).astype(BF16)
    count = jnp.dot(earlier, named, preferred_element_type=F32)
    return [
        routes[:, k : k + 1] * capacity
        + jnp.where(names[k], count, 0.0).sum(-1, keepdims=True).astype(jnp.int32)
        for k in range(TOPK)
    ]


def chosen(slot, slots):
    return (
        (lax.broadcasted_iota(jnp.int32, (slot.shape[0], slots), 1) == slot).astype(F32).astype(BF16)
    )


def home_kernel(
    core_ref, far_ref, own_ref, other_ref, w_own_ref, w_other_ref, residual_ref, modulation_ref,
    hidden_ref, normed_ref, attended_ref,
):
    heads = far_ref.shape[0]
    core = core_ref[0]
    projected = None
    for side, near_ref in enumerate((own_ref, other_ref)):
        which = core if side == 0 else 1 - core
        for h in range(heads):
            far = far_ref[h, which].astype(F32)
            near = near_ref[:, h * LANES : (h + 1) * LANES]
            far_log = (
                far[:, HEAD_DIM : HEAD_DIM + 1]
                + far[:, HEAD_DIM + 1 : HEAD_DIM + 2]
                + far[:, HEAD_DIM + 2 : HEAD_DIM + 3]
            )
            near_total = near[:, HEAD_DIM : HEAD_DIM + 1]
            near_top = near[:, HEAD_DIM + 1 : HEAD_DIM + 2]
            top = jnp.maximum(far_log, near_top)
            far_weight = jnp.exp(far_log - top)
            near_weight = jnp.exp(near_top - top)
            scale = 1.0 / (far_weight + near_total * near_weight)
            merged = far * (far_weight * scale) + near * (near_weight * scale)
            attended_ref[side, :, h * HEAD_DIM : (h + 1) * HEAD_DIM] = merged[:, :HEAD_DIM].astype(BF16)
    for side, w_ref in enumerate((w_own_ref, w_other_ref)):
        part = jnp.dot(attended_ref[side], w_ref[...], preferred_element_type=F32)
        projected = part if projected is None else projected + part
    hidden = residual_ref[...].astype(F32) + projected
    hidden_ref[...] = hidden
    centered = hidden - hidden.mean(-1, keepdims=True)
    variance = (centered * centered).mean(-1, keepdims=True)
    normed_ref[...] = (
        centered / jnp.sqrt(variance + 1e-06) * (1.0 + modulation_ref[1:2]) + modulation_ref[0:1]
    ).astype(BF16)


def slots_kernel(normed_ref, picks_ref, buffer_ref):
    buffer_ref[...] = contract(picks_ref[0] + picks_ref[1], normed_ref[...], 0, 0).astype(BF16)


def attention_by_heads(queries, fresh_keys, fresh_values, stale_keys, stale_values, out_weight, residual, modulation, routes, gates):
    tokens, width = queries.shape
    heads = width // HEAD_DIM
    rows, features = residual.shape
    core = lax.axis_index("expert").astype(jnp.int32).reshape(1)
    swap = [(0, 1), (1, 0)]
    packed = pl.pallas_call(
        pack_kernel,
        out_shape=jax.ShapeDtypeStruct((heads, 3 * HEAD_DIM, tokens), BF16),
        in_specs=[VMEM] * 3,
        out_specs=VMEM,
        name="pack",
    )(queries, stale_keys, stale_values)
    w_other = lax.ppermute(out_weight, "expert", swap)
    gathered = lax.all_to_all(packed, "patch", split_axis=0, concat_axis=0, tiled=True)
    fresh_shape = jax.ShapeDtypeStruct((tokens // 2, heads * LANES), F32)
    slots = EXPERTS * (rows // 4)
    fresh_own, fresh_away, picks, gates = pl.pallas_call(
        fresh_kernel,
        out_shape=(
            fresh_shape,
            fresh_shape,
            jax.ShapeDtypeStruct((TOPK, rows, slots), BF16),
            jax.ShapeDtypeStruct(gates.shape, F32),
        ),
        in_specs=[SMEM] + [VMEM] * 5,
        out_specs=(VMEM,) * 4,
        compiler_params=pltpu.CompilerParams(vmem_limit_bytes=16 << 20),
        cost_estimate=pl.CostEstimate(flops=5_000_000_000, bytes_accessed=2_000_000, transcendentals=200_000),
        name="fresh",
    )(core, queries, fresh_keys, fresh_values, routes, gates)
    fresh_other = lax.ppermute(fresh_away, "expert", swap)
    stale = pl.pallas_call(
        attend_kernel,
        out_shape=jax.ShapeDtypeStruct((2 * heads, tokens // 2, LANES), BF16),
        in_specs=[VMEM, ANY],
        out_specs=VMEM,
        compiler_params=pltpu.CompilerParams(vmem_limit_bytes=16 << 20),
        cost_estimate=pl.CostEstimate(flops=100_000_000_000, bytes_accessed=2_000_000, transcendentals=1_000_000),
        name="attend",
    )(gathered, fresh_other)
    far = lax.all_to_all(stale, ("patch", "expert"), split_axis=0, concat_axis=0, tiled=True)
    hidden, normed = pl.pallas_call(
        home_kernel,
        out_shape=(
            jax.ShapeDtypeStruct((rows, features), F32),
            jax.ShapeDtypeStruct((rows, features), BF16),
        ),
        in_specs=[SMEM] + [VMEM] * 7,
        out_specs=(VMEM, VMEM),
        scratch_shapes=[pltpu.VMEM((2, rows, width), BF16)],
        compiler_params=pltpu.CompilerParams(vmem_limit_bytes=20 << 20),
        cost_estimate=pl.CostEstimate(flops=4_000_000_000, bytes_accessed=8_000_000, transcendentals=100_000),
        name="home",
    )(core, far.reshape(heads, 2, rows, LANES), fresh_own, fresh_other, out_weight, w_other, residual, modulation)
    buffer = pl.pallas_call(
        slots_kernel,
        out_shape=jax.ShapeDtypeStruct((slots, features), BF16),
        in_specs=[VMEM] * 2,
        out_specs=VMEM,
        compiler_params=pltpu.CompilerParams(vmem_limit_bytes=12 << 20),
        cost_estimate=pl.CostEstimate(flops=200_000_000_000, bytes_accessed=8_000_000, transcendentals=100_000),
        name="slots",
    )(normed, picks)
    return hidden, buffer, picks, gates


def split_heads(block_rows):
    return block_rows.reshape(block_rows.shape[0], block_rows.shape[1] // HEAD_DIM, HEAD_DIM)


def head_scores(query_heads, key_rows):
    products = jnp.einsum("qhd,khd->qhk", query_heads, split_heads(key_rows), preferred_element_type=F32)
    return products * SCALE


def weighted_values(weights, value_rows):
    return jnp.einsum(
        "qhk,khd->qhd", weights.astype(BF16), split_heads(value_rows), preferred_element_type=F32
    )


def attention_by_gather(queries, fresh_keys, fresh_values, stale_keys, stale_values, out_weight, residual, modulation, routes, gates):
    row_count = queries.shape[0]
    own_start = lax.axis_index("patch") * row_count
    query_heads = split_heads(queries)
    scores = head_scores(query_heads, fresh_keys)
    running_max = scores.max(-1)
    weights = jnp.exp(scores - running_max[..., None])
    denominator, numerator = weights.sum(-1), weighted_values(weights, fresh_values)
    piece_keys = lax.all_gather(stale_keys, "patch", axis=0, tiled=True)
    piece_values = lax.all_gather(stale_values, "patch", axis=0, tiled=True)
    scores = head_scores(query_heads, piece_keys)
    positions = jnp.arange(piece_keys.shape[0], dtype=jnp.int32)
    own_rows = (positions >= own_start) & (positions < own_start + row_count)
    scores = jnp.where(own_rows[None, None, :], -1e30, scores)
    newest = jnp.maximum(running_max, scores.max(-1))
    rescale = jnp.exp(running_max - newest)
    weights = jnp.where(own_rows[None, None, :], 0.0, jnp.exp(scores - newest[..., None]))
    denominator = denominator * rescale + weights.sum(-1)
    numerator = numerator * rescale[..., None] + weighted_values(weights, piece_values)
    attended = (numerator / denominator[..., None]).reshape(queries.shape).astype(BF16)
    hidden = residual.astype(F32) + lax.psum_scatter(
        jnp.dot(attended, out_weight, preferred_element_type=F32).astype(BF16),
        "expert",
        scatter_dimension=0,
        tiled=True,
    ).astype(F32)
    centered = hidden - hidden.mean(-1, keepdims=True)
    variance = (centered * centered).mean(-1, keepdims=True)
    normed = (centered / jnp.sqrt(variance + 1e-06) * (1.0 + modulation[1]) + modulation[0]).astype(BF16)
    capacity = residual.shape[0] // 4
    picks = [chosen(slot, EXPERTS * capacity) for slot in slots_of(routes, capacity)]
    return hidden, contract(picks[0] + picks[1], normed, 0, 0).astype(BF16), jnp.stack(picks), gates


def expert_kernel(x_ref, up_ref, down_ref, out_ref, units_ref):
    for part in chunks(up_ref.shape[2]):
        units_ref[:, part] = jax.nn.gelu(
            jnp.dot(x_ref[...], up_ref[0, :, part], preferred_element_type=F32), approximate=True
        ).astype(BF16)
    for part in chunks(out_ref.shape[1]):
        out_ref[:, part] = jnp.dot(
            units_ref[...], down_ref[0, :, part], preferred_element_type=F32
        ).astype(BF16)


def chunks(width):
    step = 896 if width % 896 == 0 else LANES
    return [slice(i, i + step) for i in range(0, width, step)]


def expert_slice(inputs, up_weight, down_weight):
    rows, features = inputs.shape
    return pl.pallas_call(
        expert_kernel,
        out_shape=jax.ShapeDtypeStruct((rows, features), BF16),
        in_specs=[VMEM] * 3,
        out_specs=VMEM,
        scratch_shapes=[pltpu.VMEM((rows, up_weight.shape[2]), BF16)],
        compiler_params=pltpu.CompilerParams(vmem_limit_bytes=16 << 20),
        name="experts",
    )(inputs, up_weight, down_weight)


def combine_kernel(hidden_ref, picks_ref, gates_ref, returned_ref, out_ref):
    slices = returned_ref.shape[1]
    slots = returned_ref.shape[0] * returned_ref.shape[2]
    mixed = hidden_ref[...]
    for s in range(slices):
        rows = returned_ref[:, s].reshape(slots, returned_ref.shape[3])
        for k in range(TOPK):
            mixed += gates_ref[:, k : k + 1] * jnp.dot(picks_ref[k], rows, preferred_element_type=F32)
    out_ref[...] = mixed.astype(BF16)


def body(
    queries, fresh_keys, fresh_values, stale_keys, stale_values, residual, out_weight, modulation,
    up_weight, down_weight, routes, gates,
):
    rows, features = residual.shape
    patch_count = lax.axis_size("patch")
    device_count = patch_count * lax.axis_size("expert")
    by_heads = queries.shape[1] // HEAD_DIM == patch_count and patch_count % 2 == 0 and lax.axis_size("expert") == 2
    attention = attention_by_heads if by_heads else attention_by_gather
    hidden, buffer, picks, gates = attention(
        queries, fresh_keys, fresh_values, stale_keys, stale_values, out_weight, residual, modulation, routes, gates
    )
    capacity = rows // 4
    slice_count = device_count // EXPERTS
    outgoing = jnp.broadcast_to(
        buffer.reshape(EXPERTS, 1, capacity, features), (EXPERTS, slice_count, capacity, features)
    ).reshape(device_count, capacity, features)
    arrived = lax.all_to_all(outgoing, ("patch", "expert"), split_axis=0, concat_axis=0, tiled=True)
    outputs = expert_slice(arrived.reshape(device_count * capacity, features), up_weight, down_weight)
    returned = lax.all_to_all(
        outputs.reshape(device_count, capacity, features),
        ("patch", "expert"),
        split_axis=0,
        concat_axis=0,
        tiled=True,
    )
    return pl.pallas_call(
        combine_kernel,
        out_shape=jax.ShapeDtypeStruct((rows, features), BF16),
        in_specs=[VMEM] * 4,
        out_specs=VMEM,
        compiler_params=pltpu.CompilerParams(vmem_limit_bytes=20 << 20),
        name="combine",
    )(hidden, picks, gates, returned.reshape(EXPERTS, slice_count, capacity, features))


def solution(mesh):
    tokens = P(("group", "patch"), "expert")
    rows = P(("group", "patch", "expert"), None)
    weight = P(("patch", "expert"), None, None)
    placed = (
        tokens, tokens, tokens, tokens, tokens, rows, P("expert", None), P("group", None), weight, weight, rows, rows,
    )
    return jax.shard_map(body, mesh=mesh, in_specs=placed, out_specs=rows, check_vma=False)
```

```python
import functools
import math

import jax
import jax.numpy as jnp
from jax import lax
from jax.experimental import pallas as pl
from jax.experimental.pallas import tpu as pltpu
from jax.sharding import PartitionSpec as P

HEAD_DIM = 112
EXPERTS = 16
TOPK = 2
LANES = 128
SCALE = 1.0 / math.sqrt(HEAD_DIM)
BF16 = jnp.bfloat16
F32 = jnp.float32
VMEM = pl.BlockSpec(memory_space=pltpu.VMEM)
SMEM = pl.BlockSpec(memory_space=pltpu.SMEM)
ANY = pl.BlockSpec(memory_space=pl.ANY)


def contract(a, b, dim_a, dim_b):
    return lax.dot_general(a, b, (((dim_a,), (dim_b,)), ((), ())), preferred_element_type=F32)


def pack_kernel(q_ref, k_ref, v_ref, out_ref):
    for i, ref in enumerate((q_ref, k_ref, v_ref)):
        turned = ref[...].T
        for h in range(out_ref.shape[0]):
            out_ref[h, i * HEAD_DIM : (i + 1) * HEAD_DIM, :] = turned[
                h * HEAD_DIM : (h + 1) * HEAD_DIM
            ]


def with_ones(values):
    return jnp.concatenate([values, jnp.ones((LANES - HEAD_DIM, values.shape[1]), BF16)], axis=0)


def partial_softmax(query, keys, values):
    scores = contract(query, keys, 0, 0)
    top = scores.max(-1, keepdims=True)
    weights = jnp.exp((scores - top) * SCALE).astype(BF16)
    return contract(weights, with_ones(values), 1, 1), top * SCALE


def fresh_kernel(
    core_ref, q_ref, k_ref, v_ref, routes_ref, gates_ref, w_own_ref, w_other_ref,
    own_ref, other_ref, picks_ref, gates_out_ref, w_ref, done_ref,
):
    share = w_own_ref.shape[0] // 2
    copies = [
        pltpu.make_async_copy(
            source.at[pl.ds(j * share, share)], w_ref.at[i, pl.ds(j * share, share)], done_ref.at[i, j]
        )
        for i, source in enumerate((w_own_ref, w_other_ref))
        for j in range(2)
    ]
    for copy in copies:
        copy.start()
    q, k, v = q_ref[...].T, k_ref[...].T, v_ref[...].T
    half = q.shape[1] // 2
    first = core_ref[0] == 0
    lane = lax.broadcasted_iota(jnp.int32, (2 * half, LANES), 1)
    for h in range(q.shape[0] // HEAD_DIM):
        rows = slice(h * HEAD_DIM, (h + 1) * HEAD_DIM)
        sums, top = partial_softmax(q[rows], k[rows], v[rows])
        sums = jnp.where(lane == HEAD_DIM + 1, top, sums)
        lanes = slice(h * LANES, (h + 1) * LANES)
        own_ref[:, lanes] = jnp.where(first, sums[:half], sums[half:])
        other_ref[:, lanes] = jnp.where(first, sums[half:], sums[:half])
    slots = picks_ref.shape[2]
    for k, slot in enumerate(slots_of(routes_ref[...], slots // EXPERTS)):
        picks_ref[k] = chosen(slot, slots)
    gates_out_ref[...] = gates_ref[...]
    for copy in copies:
        copy.wait()


def attend_kernel(in_ref, fresh_ref, out_ref):
    patches, tokens = in_ref.shape[0], in_ref.shape[2]
    half, rows, steps = tokens // 2, 2 * tokens, patches // 2
    keys = jnp.concatenate([in_ref[j, HEAD_DIM : 2 * HEAD_DIM] for j in range(patches)], axis=1)
    values = with_ones(jnp.concatenate([in_ref[j, 2 * HEAD_DIM :] for j in range(patches)], axis=1))
    lane = lax.broadcasted_iota(jnp.int32, (rows, LANES), 1)
    own = (lax.broadcasted_iota(jnp.int32, (rows, rows), 0) < tokens) == (
        lax.broadcasted_iota(jnp.int32, (rows, rows), 1) < tokens
    )

    def scores_of(step):
        query = jnp.concatenate([in_ref[2 * step + i, :HEAD_DIM] for i in range(2)], axis=1)
        scores = contract(query, keys, 0, 0)
        first, last = step * rows, (step + 1) * rows
        parts = [jnp.where(own, -1e30, scores[:, first:last])]
        if step > 0:
            parts.insert(0, scores[:, :first])
        if step < steps - 1:
            parts.append(scores[:, last:])
        return jnp.concatenate(parts, axis=1)

    scores = scores_of(0)
    for step in range(steps):
        following = scores_of(step + 1) if step < steps - 1 else None
        top = scores.max(-1, keepdims=True)
        weights = jnp.exp2((scores - top) * (SCALE * math.log2(math.e))).astype(BF16)
        sums = contract(weights, values, 1, 1)
        total = sums[:, HEAD_DIM : HEAD_DIM + 1]
        log_total = top * SCALE + jnp.log(total)
        high = log_total.astype(BF16).astype(F32)
        rest = log_total - high
        middle = rest.astype(BF16).astype(F32)
        result = sums * (1.0 / total)
        result = jnp.where(lane == HEAD_DIM, high, result)
        result = jnp.where(lane == HEAD_DIM + 1, middle, result)
        result = jnp.where(lane == HEAD_DIM + 2, rest - middle, result)
        result = result.astype(BF16)
        for i in range(4):
            out_ref[4 * step + i] = result[i * half : (i + 1) * half]
        scores = following


def slots_of(routes, capacity):
    rows = routes.shape[0]
    expert = lax.broadcasted_iota(jnp.int32, (rows, EXPERTS), 1)
    names = [expert == routes[:, k : k + 1] for k in range(TOPK)]
    named = sum(n.astype(F32) for n in names).astype(BF16)
    earlier = (
        lax.broadcasted_iota(jnp.int32, (rows, rows), 1)
        < lax.broadcasted_iota(jnp.int32, (rows, rows), 0)
    ).astype(F32).astype(BF16)
    count = jnp.dot(earlier, named, preferred_element_type=F32)
    return [
        routes[:, k : k + 1] * capacity
        + jnp.where(names[k], count, 0.0).sum(-1, keepdims=True).astype(jnp.int32)
        for k in range(TOPK)
    ]


def chosen(slot, slots):
    return (
        (lax.broadcasted_iota(jnp.int32, (slot.shape[0], slots), 1) == slot).astype(F32).astype(BF16)
    )


def home_kernel(
    core_ref, far_ref, own_ref, other_ref, w_ref, residual_ref, modulation_ref,
    hidden_ref, normed_ref, attended_ref,
):
    heads = far_ref.shape[0]
    core = core_ref[0]
    projected = None
    for side, near_ref in enumerate((own_ref, other_ref)):
        which = core if side == 0 else 1 - core
        for h in range(heads):
            far = far_ref[h, which].astype(F32)
            near = near_ref[:, h * LANES : (h + 1) * LANES]
            far_log = (
                far[:, HEAD_DIM : HEAD_DIM + 1]
                + far[:, HEAD_DIM + 1 : HEAD_DIM + 2]
                + far[:, HEAD_DIM + 2 : HEAD_DIM + 3]
            )
            near_total = near[:, HEAD_DIM : HEAD_DIM + 1]
            near_top = near[:, HEAD_DIM + 1 : HEAD_DIM + 2]
            top = jnp.maximum(far_log, near_top)
            far_weight = jnp.exp(far_log - top)
            near_weight = jnp.exp(near_top - top)
            scale = 1.0 / (far_weight + near_total * near_weight)
            merged = far * (far_weight * scale) + near * (near_weight * scale)
            attended_ref[side, :, h * HEAD_DIM : (h + 1) * HEAD_DIM] = merged[:, :HEAD_DIM].astype(BF16)
    for side in range(2):
        part = jnp.dot(attended_ref[side], w_ref[side], preferred_element_type=F32)
        projected = part if projected is None else projected + part
    hidden = residual_ref[...].astype(F32) + projected
    hidden_ref[...] = hidden
    centered = hidden - hidden.mean(-1, keepdims=True)
    variance = (centered * centered).mean(-1, keepdims=True)
    normed_ref[...] = (
        centered / jnp.sqrt(variance + 1e-06) * (1.0 + modulation_ref[1:2]) + modulation_ref[0:1]
    ).astype(BF16)


def slots_kernel(normed_ref, picks_ref, buffer_ref):
    buffer_ref[...] = contract(picks_ref[0] + picks_ref[1], normed_ref[...], 0, 0).astype(BF16)


def attention_by_heads(queries, fresh_keys, fresh_values, stale_keys, stale_values, out_weight, residual, modulation, routes, gates):
    tokens, width = queries.shape
    heads = width // HEAD_DIM
    rows, features = residual.shape
    core = lax.axis_index("expert").astype(jnp.int32).reshape(1)
    swap = [(0, 1), (1, 0)]
    packed = pl.pallas_call(
        pack_kernel,
        out_shape=jax.ShapeDtypeStruct((heads, 3 * HEAD_DIM, tokens), BF16),
        in_specs=[VMEM] * 3,
        out_specs=VMEM,
        name="pack",
    )(queries, stale_keys, stale_values)
    w_other = lax.ppermute(out_weight, "expert", swap)
    gathered = lax.all_to_all(packed, "patch", split_axis=0, concat_axis=0, tiled=True)
    fresh_shape = jax.ShapeDtypeStruct((tokens // 2, heads * LANES), F32)
    slots = EXPERTS * (rows // 4)
    fresh_own, fresh_away, picks, gates, weights = pl.pallas_call(
        fresh_kernel,
        out_shape=(
            fresh_shape,
            fresh_shape,
            jax.ShapeDtypeStruct((TOPK, rows, slots), BF16),
            jax.ShapeDtypeStruct(gates.shape, F32),
            jax.ShapeDtypeStruct((2,) + out_weight.shape, BF16),
        ),
        in_specs=[SMEM] + [VMEM] * 5 + [ANY] * 2,
        out_specs=(VMEM,) * 4 + (ANY,),
        scratch_shapes=[pltpu.SemaphoreType.DMA((2, 2))],
        compiler_params=pltpu.CompilerParams(vmem_limit_bytes=16 << 20),
        cost_estimate=pl.CostEstimate(flops=5_000_000_000, bytes_accessed=2_000_000, transcendentals=200_000),
        name="fresh",
    )(core, queries, fresh_keys, fresh_values, routes, gates, out_weight, w_other)
    fresh_other = lax.ppermute(fresh_away, "expert", swap)
    stale = pl.pallas_call(
        attend_kernel,
        out_shape=jax.ShapeDtypeStruct((2 * heads, tokens // 2, LANES), BF16),
        in_specs=[VMEM, ANY],
        out_specs=VMEM,
        compiler_params=pltpu.CompilerParams(vmem_limit_bytes=16 << 20),
        cost_estimate=pl.CostEstimate(flops=100_000_000_000, bytes_accessed=2_000_000, transcendentals=1_000_000),
        name="attend",
    )(gathered, fresh_other)
    far = lax.all_to_all(stale, ("patch", "expert"), split_axis=0, concat_axis=0, tiled=True)
    hidden, normed = pl.pallas_call(
        home_kernel,
        out_shape=(
            jax.ShapeDtypeStruct((rows, features), F32),
            jax.ShapeDtypeStruct((rows, features), BF16),
        ),
        in_specs=[SMEM] + [VMEM] * 6,
        out_specs=(VMEM, VMEM),
        scratch_shapes=[pltpu.VMEM((2, rows, width), BF16)],
        compiler_params=pltpu.CompilerParams(vmem_limit_bytes=20 << 20),
        cost_estimate=pl.CostEstimate(flops=4_000_000_000, bytes_accessed=8_000_000, transcendentals=100_000),
        name="home",
    )(core, far.reshape(heads, 2, rows, LANES), fresh_own, fresh_other, weights, residual, modulation)
    buffer = pl.pallas_call(
        slots_kernel,
        out_shape=jax.ShapeDtypeStruct((slots, features), BF16),
        in_specs=[VMEM] * 2,
        out_specs=VMEM,
        compiler_params=pltpu.CompilerParams(vmem_limit_bytes=12 << 20),
        cost_estimate=pl.CostEstimate(flops=100_000_000_000, bytes_accessed=8_000_000, transcendentals=100_000),
        name="slots",
    )(normed, picks)
    return hidden, buffer, picks, gates


def split_heads(block_rows):
    return block_rows.reshape(block_rows.shape[0], block_rows.shape[1] // HEAD_DIM, HEAD_DIM)


def head_scores(query_heads, key_rows):
    products = jnp.einsum("qhd,khd->qhk", query_heads, split_heads(key_rows), preferred_element_type=F32)
    return products * SCALE


def weighted_values(weights, value_rows):
    return jnp.einsum(
        "qhk,khd->qhd", weights.astype(BF16), split_heads(value_rows), preferred_element_type=F32
    )


def attention_by_gather(queries, fresh_keys, fresh_values, stale_keys, stale_values, out_weight, residual, modulation, routes, gates):
    row_count = queries.shape[0]
    own_start = lax.axis_index("patch") * row_count
    query_heads = split_heads(queries)
    scores = head_scores(query_heads, fresh_keys)
    running_max = scores.max(-1)
    weights = jnp.exp(scores - running_max[..., None])
    denominator, numerator = weights.sum(-1), weighted_values(weights, fresh_values)
    piece_keys = lax.all_gather(stale_keys, "patch", axis=0, tiled=True)
    piece_values = lax.all_gather(stale_values, "patch", axis=0, tiled=True)
    scores = head_scores(query_heads, piece_keys)
    positions = jnp.arange(piece_keys.shape[0], dtype=jnp.int32)
    own_rows = (positions >= own_start) & (positions < own_start + row_count)
    scores = jnp.where(own_rows[None, None, :], -1e30, scores)
    newest = jnp.maximum(running_max, scores.max(-1))
    rescale = jnp.exp(running_max - newest)
    weights = jnp.where(own_rows[None, None, :], 0.0, jnp.exp(scores - newest[..., None]))
    denominator = denominator * rescale + weights.sum(-1)
    numerator = numerator * rescale[..., None] + weighted_values(weights, piece_values)
    attended = (numerator / denominator[..., None]).reshape(queries.shape).astype(BF16)
    hidden = residual.astype(F32) + lax.psum_scatter(
        jnp.dot(attended, out_weight, preferred_element_type=F32).astype(BF16),
        "expert",
        scatter_dimension=0,
        tiled=True,
    ).astype(F32)
    centered = hidden - hidden.mean(-1, keepdims=True)
    variance = (centered * centered).mean(-1, keepdims=True)
    normed = (centered / jnp.sqrt(variance + 1e-06) * (1.0 + modulation[1]) + modulation[0]).astype(BF16)
    capacity = residual.shape[0] // 4
    picks = [chosen(slot, EXPERTS * capacity) for slot in slots_of(routes, capacity)]
    return hidden, contract(picks[0] + picks[1], normed, 0, 0).astype(BF16), jnp.stack(picks), gates


def expert_kernel(x_ref, up_ref, down_ref, out_ref, units_ref):
    for part in chunks(up_ref.shape[2]):
        units_ref[:, part] = jax.nn.gelu(
            jnp.dot(x_ref[...], up_ref[0, :, part], preferred_element_type=F32), approximate=True
        ).astype(BF16)
    for part in chunks(out_ref.shape[1]):
        out_ref[:, part] = jnp.dot(
            units_ref[...], down_ref[0, :, part], preferred_element_type=F32
        ).astype(BF16)


def chunks(width):
    step = 896 if width % 896 == 0 else LANES
    return [slice(i, i + step) for i in range(0, width, step)]


def expert_slice(inputs, up_weight, down_weight):
    rows, features = inputs.shape
    return pl.pallas_call(
        expert_kernel,
        out_shape=jax.ShapeDtypeStruct((rows, features), BF16),
        in_specs=[VMEM] * 3,
        out_specs=VMEM,
        scratch_shapes=[pltpu.VMEM((rows, up_weight.shape[2]), BF16)],
        compiler_params=pltpu.CompilerParams(vmem_limit_bytes=16 << 20),
        name="experts",
    )(inputs, up_weight, down_weight)


def combine_kernel(hidden_ref, picks_ref, gates_ref, returned_ref, out_ref):
    slices = returned_ref.shape[1]
    slots = returned_ref.shape[0] * returned_ref.shape[2]
    mixed = hidden_ref[...]
    for s in range(slices):
        rows = returned_ref[:, s].reshape(slots, returned_ref.shape[3])
        for k in range(TOPK):
            mixed += gates_ref[:, k : k + 1] * jnp.dot(picks_ref[k], rows, preferred_element_type=F32)
    out_ref[...] = mixed.astype(BF16)


def body(
    queries, fresh_keys, fresh_values, stale_keys, stale_values, residual, out_weight, modulation,
    up_weight, down_weight, routes, gates,
):
    rows, features = residual.shape
    patch_count = lax.axis_size("patch")
    device_count = patch_count * lax.axis_size("expert")
    by_heads = queries.shape[1] // HEAD_DIM == patch_count and patch_count % 2 == 0 and lax.axis_size("expert") == 2
    attention = attention_by_heads if by_heads else attention_by_gather
    hidden, buffer, picks, gates = attention(
        queries, fresh_keys, fresh_values, stale_keys, stale_values, out_weight, residual, modulation, routes, gates
    )
    capacity = rows // 4
    slice_count = device_count // EXPERTS
    outgoing = jnp.broadcast_to(
        buffer.reshape(EXPERTS, 1, capacity, features), (EXPERTS, slice_count, capacity, features)
    ).reshape(device_count, capacity, features)
    arrived = lax.all_to_all(outgoing, ("patch", "expert"), split_axis=0, concat_axis=0, tiled=True)
    outputs = expert_slice(arrived.reshape(device_count * capacity, features), up_weight, down_weight)
    returned = lax.all_to_all(
        outputs.reshape(device_count, capacity, features),
        ("patch", "expert"),
        split_axis=0,
        concat_axis=0,
        tiled=True,
    )
    return pl.pallas_call(
        combine_kernel,
        out_shape=jax.ShapeDtypeStruct((rows, features), BF16),
        in_specs=[VMEM] * 4,
        out_specs=VMEM,
        compiler_params=pltpu.CompilerParams(vmem_limit_bytes=20 << 20),
        name="combine",
    )(hidden, picks, gates, returned.reshape(EXPERTS, slice_count, capacity, features))


def solution(mesh):
    tokens = P(("group", "patch"), "expert")
    rows = P(("group", "patch", "expert"), None)
    weight = P(("patch", "expert"), None, None)
    placed = (
        tokens, tokens, tokens, tokens, tokens, rows, P("expert", None), P("group", None), weight, weight, rows, rows,
    )
    return jax.shard_map(body, mesh=mesh, in_specs=placed, out_specs=rows, check_vma=False)
```

```python
import functools
import math

import jax
import jax.numpy as jnp
from jax import lax
from jax.experimental import pallas as pl
from jax.experimental.pallas import tpu as pltpu
from jax.sharding import PartitionSpec as P

HEAD_DIM = 112
EXPERTS = 16
TOPK = 2
LANES = 128
SCALE = 1.0 / math.sqrt(HEAD_DIM)
BF16 = jnp.bfloat16
F32 = jnp.float32
VMEM = pl.BlockSpec(memory_space=pltpu.VMEM)
SMEM = pl.BlockSpec(memory_space=pltpu.SMEM)
ANY = pl.BlockSpec(memory_space=pl.ANY)


def contract(a, b, dim_a, dim_b):
    return lax.dot_general(a, b, (((dim_a,), (dim_b,)), ((), ())), preferred_element_type=F32)


def pack_kernel(q_ref, k_ref, v_ref, out_ref, rows_ref, turned_ref, in_sem, out_sem):
    loads = [
        pltpu.make_async_copy(ref, rows_ref.at[i], in_sem.at[i]) for i, ref in enumerate((q_ref, k_ref, v_ref))
    ]
    stores = [
        pltpu.make_async_copy(
            turned_ref.at[:, pl.ds(i * HEAD_DIM, HEAD_DIM)],
            out_ref.at[:, pl.ds(i * HEAD_DIM, HEAD_DIM)],
            out_sem.at[i],
        )
        for i in range(3)
    ]
    for load in loads:
        load.start()
    for i in range(3):
        loads[i].wait()
        turned = rows_ref[i].T
        for h in range(turned_ref.shape[0]):
            turned_ref[h, i * HEAD_DIM : (i + 1) * HEAD_DIM, :] = turned[h * HEAD_DIM : (h + 1) * HEAD_DIM]
        stores[i].start()
    for store in stores:
        store.wait()


def with_ones(values):
    return jnp.concatenate([values, jnp.ones((LANES - HEAD_DIM, values.shape[1]), BF16)], axis=0)


def partial_softmax(query, keys, values):
    scores = contract(query, keys, 0, 0)
    top = scores.max(-1, keepdims=True)
    weights = jnp.exp((scores - top) * SCALE).astype(BF16)
    return contract(weights, with_ones(values), 1, 1), top * SCALE


def fresh_kernel(
    core_ref, q_ref, k_ref, v_ref, routes_ref, gates_ref, w_own_ref, w_other_ref,
    own_ref, other_ref, picks_ref, gates_out_ref, w_ref, done_ref,
):
    share = w_own_ref.shape[0] // 2
    copies = [
        pltpu.make_async_copy(
            source.at[pl.ds(j * share, share)], w_ref.at[i, pl.ds(j * share, share)], done_ref.at[i, j]
        )
        for i, source in enumerate((w_own_ref, w_other_ref))
        for j in range(2)
    ]
    for copy in copies:
        copy.start()
    q, k, v = q_ref[...].T, k_ref[...].T, v_ref[...].T
    half = q.shape[1] // 2
    first = core_ref[0] == 0
    lane = lax.broadcasted_iota(jnp.int32, (2 * half, LANES), 1)
    for h in range(q.shape[0] // HEAD_DIM):
        rows = slice(h * HEAD_DIM, (h + 1) * HEAD_DIM)
        sums, top = partial_softmax(q[rows], k[rows], v[rows])
        sums = jnp.where(lane == HEAD_DIM + 1, top, sums)
        lanes = slice(h * LANES, (h + 1) * LANES)
        own_ref[:, lanes] = jnp.where(first, sums[:half], sums[half:])
        other_ref[:, lanes] = jnp.where(first, sums[half:], sums[:half])
    slots = picks_ref.shape[2]
    for k, slot in enumerate(slots_of(routes_ref[...], slots // EXPERTS)):
        picks_ref[k] = chosen(slot, slots)
    gates_out_ref[...] = gates_ref[...]
    for copy in copies:
        copy.wait()


def attend_kernel(in_ref, fresh_ref, out_ref):
    patches, tokens = in_ref.shape[0], in_ref.shape[2]
    half, rows, steps = tokens // 2, 2 * tokens, patches // 2
    keys = jnp.concatenate([in_ref[j, HEAD_DIM : 2 * HEAD_DIM] for j in range(patches)], axis=1)
    values = with_ones(jnp.concatenate([in_ref[j, 2 * HEAD_DIM :] for j in range(patches)], axis=1))
    lane = lax.broadcasted_iota(jnp.int32, (rows, LANES), 1)
    own = (lax.broadcasted_iota(jnp.int32, (rows, rows), 0) < tokens) == (
        lax.broadcasted_iota(jnp.int32, (rows, rows), 1) < tokens
    )

    def scores_of(step):
        query = jnp.concatenate([in_ref[2 * step + i, :HEAD_DIM] for i in range(2)], axis=1)
        scores = contract(query, keys, 0, 0)
        first, last = step * rows, (step + 1) * rows
        parts = [jnp.where(own, -1e30, scores[:, first:last])]
        if step > 0:
            parts.insert(0, scores[:, :first])
        if step < steps - 1:
            parts.append(scores[:, last:])
        return jnp.concatenate(parts, axis=1)

    scores = scores_of(0)
    for step in range(steps):
        following = scores_of(step + 1) if step < steps - 1 else None
        top = scores.max(-1, keepdims=True)
        weights = jnp.exp2((scores - top) * (SCALE * math.log2(math.e))).astype(BF16)
        sums = contract(weights, values, 1, 1)
        total = sums[:, HEAD_DIM : HEAD_DIM + 1]
        log_total = top * SCALE + jnp.log(total)
        high = log_total.astype(BF16).astype(F32)
        rest = log_total - high
        middle = rest.astype(BF16).astype(F32)
        result = sums * (1.0 / total)
        result = jnp.where(lane == HEAD_DIM, high, result)
        result = jnp.where(lane == HEAD_DIM + 1, middle, result)
        result = jnp.where(lane == HEAD_DIM + 2, rest - middle, result)
        result = result.astype(BF16)
        for i in range(4):
            out_ref[4 * step + i] = result[i * half : (i + 1) * half]
        scores = following


def slots_of(routes, capacity):
    rows = routes.shape[0]
    expert = lax.broadcasted_iota(jnp.int32, (rows, EXPERTS), 1)
    names = [expert == routes[:, k : k + 1] for k in range(TOPK)]
    named = sum(n.astype(F32) for n in names).astype(BF16)
    earlier = (
        lax.broadcasted_iota(jnp.int32, (rows, rows), 1)
        < lax.broadcasted_iota(jnp.int32, (rows, rows), 0)
    ).astype(F32).astype(BF16)
    count = jnp.dot(earlier, named, preferred_element_type=F32)
    return [
        routes[:, k : k + 1] * capacity
        + jnp.where(names[k], count, 0.0).sum(-1, keepdims=True).astype(jnp.int32)
        for k in range(TOPK)
    ]


def chosen(slot, slots):
    return (
        (lax.broadcasted_iota(jnp.int32, (slot.shape[0], slots), 1) == slot).astype(F32).astype(BF16)
    )


def home_kernel(
    core_ref, far_ref, own_ref, other_ref, w_ref, residual_ref, modulation_ref,
    picks_ref, hidden_ref, buffer_ref, attended_ref,
):
    heads = far_ref.shape[0]
    core = core_ref[0]
    projected = None
    for side, near_ref in enumerate((own_ref, other_ref)):
        which = core if side == 0 else 1 - core
        for h in range(heads):
            far = far_ref[h, which].astype(F32)
            near = near_ref[:, h * LANES : (h + 1) * LANES]
            far_log = (
                far[:, HEAD_DIM : HEAD_DIM + 1]
                + far[:, HEAD_DIM + 1 : HEAD_DIM + 2]
                + far[:, HEAD_DIM + 2 : HEAD_DIM + 3]
            )
            near_total = near[:, HEAD_DIM : HEAD_DIM + 1]
            near_top = near[:, HEAD_DIM + 1 : HEAD_DIM + 2]
            top = jnp.maximum(far_log, near_top)
            far_weight = jnp.exp(far_log - top)
            near_weight = jnp.exp(near_top - top)
            scale = 1.0 / (far_weight + near_total * near_weight)
            merged = far * (far_weight * scale) + near * (near_weight * scale)
            attended_ref[side, :, h * HEAD_DIM : (h + 1) * HEAD_DIM] = merged[:, :HEAD_DIM].astype(BF16)
    for side in range(2):
        part = jnp.dot(attended_ref[side], w_ref[side], preferred_element_type=F32)
        projected = part if projected is None else projected + part
    hidden = residual_ref[...].astype(F32) + projected
    hidden_ref[...] = hidden
    centered = hidden - hidden.mean(-1, keepdims=True)
    variance = (centered * centered).mean(-1, keepdims=True)
    normed = (
        centered / jnp.sqrt(variance + 1e-06) * (1.0 + modulation_ref[1:2]) + modulation_ref[0:1]
    ).astype(BF16)
    buffer_ref[...] = contract(picks_ref[0] + picks_ref[1], normed, 0, 0).astype(BF16)


def attention_by_heads(queries, fresh_keys, fresh_values, stale_keys, stale_values, out_weight, residual, modulation, routes, gates):
    tokens, width = queries.shape
    heads = width // HEAD_DIM
    rows, features = residual.shape
    core = lax.axis_index("expert").astype(jnp.int32).reshape(1)
    swap = [(0, 1), (1, 0)]
    packed = pl.pallas_call(
        pack_kernel,
        out_shape=jax.ShapeDtypeStruct((heads, 3 * HEAD_DIM, tokens), BF16),
        in_specs=[ANY] * 3,
        out_specs=ANY,
        scratch_shapes=[
            pltpu.VMEM((3, tokens, width), BF16),
            pltpu.VMEM((heads, 3 * HEAD_DIM, tokens), BF16),
            pltpu.SemaphoreType.DMA((3,)),
            pltpu.SemaphoreType.DMA((3,)),
        ],
        compiler_params=pltpu.CompilerParams(vmem_limit_bytes=56 << 20),
        name="pack",
    )(queries, stale_keys, stale_values)
    w_other = lax.ppermute(out_weight, "expert", swap)
    gathered = lax.all_to_all(packed, "patch", split_axis=0, concat_axis=0, tiled=True)
    fresh_shape = jax.ShapeDtypeStruct((tokens // 2, heads * LANES), F32)
    slots = EXPERTS * (rows // 4)
    fresh_own, fresh_away, picks, gates, weights = pl.pallas_call(
        fresh_kernel,
        out_shape=(
            fresh_shape,
            fresh_shape,
            jax.ShapeDtypeStruct((TOPK, rows, slots), BF16),
            jax.ShapeDtypeStruct(gates.shape, F32),
            jax.ShapeDtypeStruct((2,) + out_weight.shape, BF16),
        ),
        in_specs=[SMEM] + [VMEM] * 5 + [ANY] * 2,
        out_specs=(VMEM,) * 4 + (ANY,),
        scratch_shapes=[pltpu.SemaphoreType.DMA((2, 2))],
        compiler_params=pltpu.CompilerParams(vmem_limit_bytes=16 << 20),
        cost_estimate=pl.CostEstimate(flops=5_000_000_000, bytes_accessed=2_000_000, transcendentals=200_000),
        name="fresh",
    )(core, queries, fresh_keys, fresh_values, routes, gates, out_weight, w_other)
    fresh_other = lax.ppermute(fresh_away, "expert", swap)
    stale = pl.pallas_call(
        attend_kernel,
        out_shape=jax.ShapeDtypeStruct((2 * heads, tokens // 2, LANES), BF16),
        in_specs=[VMEM, ANY],
        out_specs=VMEM,
        compiler_params=pltpu.CompilerParams(vmem_limit_bytes=16 << 20),
        cost_estimate=pl.CostEstimate(flops=100_000_000_000, bytes_accessed=2_000_000, transcendentals=1_000_000),
        name="attend",
    )(gathered, fresh_other)
    far = lax.all_to_all(stale, ("patch", "expert"), split_axis=0, concat_axis=0, tiled=True)
    hidden, buffer = pl.pallas_call(
        home_kernel,
        out_shape=(
            jax.ShapeDtypeStruct((rows, features), F32),
            jax.ShapeDtypeStruct((slots, features), BF16),
        ),
        in_specs=[SMEM] + [VMEM] * 7,
        out_specs=(VMEM, VMEM),
        scratch_shapes=[pltpu.VMEM((2, rows, width), BF16)],
        compiler_params=pltpu.CompilerParams(vmem_limit_bytes=20 << 20),
        cost_estimate=pl.CostEstimate(flops=100_000_000_000, bytes_accessed=8_000_000, transcendentals=100_000),
        name="home",
    )(core, far.reshape(heads, 2, rows, LANES), fresh_own, fresh_other, weights, residual, modulation, picks)
    return hidden, buffer, picks, gates


def split_heads(block_rows):
    return block_rows.reshape(block_rows.shape[0], block_rows.shape[1] // HEAD_DIM, HEAD_DIM)


def head_scores(query_heads, key_rows):
    products = jnp.einsum("qhd,khd->qhk", query_heads, split_heads(key_rows), preferred_element_type=F32)
    return products * SCALE


def weighted_values(weights, value_rows):
    return jnp.einsum(
        "qhk,khd->qhd", weights.astype(BF16), split_heads(value_rows), preferred_element_type=F32
    )


def attention_by_gather(queries, fresh_keys, fresh_values, stale_keys, stale_values, out_weight, residual, modulation, routes, gates):
    row_count = queries.shape[0]
    own_start = lax.axis_index("patch") * row_count
    query_heads = split_heads(queries)
    scores = head_scores(query_heads, fresh_keys)
    running_max = scores.max(-1)
    weights = jnp.exp(scores - running_max[..., None])
    denominator, numerator = weights.sum(-1), weighted_values(weights, fresh_values)
    piece_keys = lax.all_gather(stale_keys, "patch", axis=0, tiled=True)
    piece_values = lax.all_gather(stale_values, "patch", axis=0, tiled=True)
    scores = head_scores(query_heads, piece_keys)
    positions = jnp.arange(piece_keys.shape[0], dtype=jnp.int32)
    own_rows = (positions >= own_start) & (positions < own_start + row_count)
    scores = jnp.where(own_rows[None, None, :], -1e30, scores)
    newest = jnp.maximum(running_max, scores.max(-1))
    rescale = jnp.exp(running_max - newest)
    weights = jnp.where(own_rows[None, None, :], 0.0, jnp.exp(scores - newest[..., None]))
    denominator = denominator * rescale + weights.sum(-1)
    numerator = numerator * rescale[..., None] + weighted_values(weights, piece_values)
    attended = (numerator / denominator[..., None]).reshape(queries.shape).astype(BF16)
    hidden = residual.astype(F32) + lax.psum_scatter(
        jnp.dot(attended, out_weight, preferred_element_type=F32).astype(BF16),
        "expert",
        scatter_dimension=0,
        tiled=True,
    ).astype(F32)
    centered = hidden - hidden.mean(-1, keepdims=True)
    variance = (centered * centered).mean(-1, keepdims=True)
    normed = (centered / jnp.sqrt(variance + 1e-06) * (1.0 + modulation[1]) + modulation[0]).astype(BF16)
    capacity = residual.shape[0] // 4
    picks = [chosen(slot, EXPERTS * capacity) for slot in slots_of(routes, capacity)]
    return hidden, contract(picks[0] + picks[1], normed, 0, 0).astype(BF16), jnp.stack(picks), gates


def expert_kernel(x_ref, up_ref, down_ref, out_ref, units_ref):
    for part in chunks(up_ref.shape[2]):
        units_ref[:, part] = jax.nn.gelu(
            jnp.dot(x_ref[...], up_ref[0, :, part], preferred_element_type=F32), approximate=True
        ).astype(BF16)
    for part in chunks(out_ref.shape[1]):
        out_ref[:, part] = jnp.dot(
            units_ref[...], down_ref[0, :, part], preferred_element_type=F32
        ).astype(BF16)


def chunks(width):
    step = 896 if width % 896 == 0 else LANES
    return [slice(i, i + step) for i in range(0, width, step)]


def expert_slice(inputs, up_weight, down_weight):
    rows, features = inputs.shape
    return pl.pallas_call(
        expert_kernel,
        out_shape=jax.ShapeDtypeStruct((rows, features), BF16),
        in_specs=[VMEM] * 3,
        out_specs=VMEM,
        scratch_shapes=[pltpu.VMEM((rows, up_weight.shape[2]), BF16)],
        compiler_params=pltpu.CompilerParams(vmem_limit_bytes=16 << 20),
        name="experts",
    )(inputs, up_weight, down_weight)


def combine_kernel(hidden_ref, picks_ref, gates_ref, returned_ref, out_ref):
    slices = returned_ref.shape[1]
    slots = returned_ref.shape[0] * returned_ref.shape[2]
    mixed = hidden_ref[...]
    for s in range(slices):
        rows = returned_ref[:, s].reshape(slots, returned_ref.shape[3])
        for k in range(TOPK):
            mixed += gates_ref[:, k : k + 1] * jnp.dot(picks_ref[k], rows, preferred_element_type=F32)
    out_ref[...] = mixed.astype(BF16)


def body(
    queries, fresh_keys, fresh_values, stale_keys, stale_values, residual, out_weight, modulation,
    up_weight, down_weight, routes, gates,
):
    rows, features = residual.shape
    patch_count = lax.axis_size("patch")
    device_count = patch_count * lax.axis_size("expert")
    by_heads = queries.shape[1] // HEAD_DIM == patch_count and patch_count % 2 == 0 and lax.axis_size("expert") == 2
    attention = attention_by_heads if by_heads else attention_by_gather
    hidden, buffer, picks, gates = attention(
        queries, fresh_keys, fresh_values, stale_keys, stale_values, out_weight, residual, modulation, routes, gates
    )
    capacity = rows // 4
    slice_count = device_count // EXPERTS
    outgoing = jnp.broadcast_to(
        buffer.reshape(EXPERTS, 1, capacity, features), (EXPERTS, slice_count, capacity, features)
    ).reshape(device_count, capacity, features)
    arrived = lax.all_to_all(outgoing, ("patch", "expert"), split_axis=0, concat_axis=0, tiled=True)
    outputs = expert_slice(arrived.reshape(device_count * capacity, features), up_weight, down_weight)
    returned = lax.all_to_all(
        outputs.reshape(device_count, capacity, features),
        ("patch", "expert"),
        split_axis=0,
        concat_axis=0,
        tiled=True,
    )
    return pl.pallas_call(
        combine_kernel,
        out_shape=jax.ShapeDtypeStruct((rows, features), BF16),
        in_specs=[VMEM] * 4,
        out_specs=VMEM,
        compiler_params=pltpu.CompilerParams(vmem_limit_bytes=20 << 20),
        name="combine",
    )(hidden, picks, gates, returned.reshape(EXPERTS, slice_count, capacity, features))


def solution(mesh):
    tokens = P(("group", "patch"), "expert")
    rows = P(("group", "patch", "expert"), None)
    weight = P(("patch", "expert"), None, None)
    placed = (
        tokens, tokens, tokens, tokens, tokens, rows, P("expert", None), P("group", None), weight, weight, rows, rows,
    )
    return jax.shard_map(body, mesh=mesh, in_specs=placed, out_specs=rows, check_vma=False)
```

```python
import functools
import math

import jax
import jax.numpy as jnp
from jax import lax
from jax.experimental import pallas as pl
from jax.experimental.pallas import tpu as pltpu
from jax.sharding import PartitionSpec as P

HEAD_DIM = 112
EXPERTS = 16
TOPK = 2
LANES = 128
SCALE = 1.0 / math.sqrt(HEAD_DIM)
BF16 = jnp.bfloat16
F32 = jnp.float32
VMEM = pl.BlockSpec(memory_space=pltpu.VMEM)
SMEM = pl.BlockSpec(memory_space=pltpu.SMEM)
ANY = pl.BlockSpec(memory_space=pl.ANY)


def contract(a, b, dim_a, dim_b):
    return lax.dot_general(a, b, (((dim_a,), (dim_b,)), ((), ())), preferred_element_type=F32)


def pack_kernel(q_ref, k_ref, v_ref, out_ref, rows_ref, turned_ref, in_sem, out_sem):
    loads = [
        pltpu.make_async_copy(ref, rows_ref.at[i], in_sem.at[i]) for i, ref in enumerate((q_ref, k_ref, v_ref))
    ]
    stores = [
        pltpu.make_async_copy(
            turned_ref.at[:, pl.ds(i * HEAD_DIM, HEAD_DIM)],
            out_ref.at[:, pl.ds(i * HEAD_DIM, HEAD_DIM)],
            out_sem.at[i],
        )
        for i in range(3)
    ]
    for load in loads:
        load.start()
    for i in range(3):
        loads[i].wait()
        turned = rows_ref[i].T
        for h in range(turned_ref.shape[0]):
            turned_ref[h, i * HEAD_DIM : (i + 1) * HEAD_DIM, :] = turned[h * HEAD_DIM : (h + 1) * HEAD_DIM]
        stores[i].start()
    for store in stores:
        store.wait()


def with_ones(values):
    return jnp.concatenate([values, jnp.ones((LANES - HEAD_DIM, values.shape[1]), BF16)], axis=0)


def partial_softmax(query, keys, values):
    scores = contract(query, keys, 0, 0)
    top = scores.max(-1, keepdims=True)
    weights = jnp.exp((scores - top) * SCALE).astype(BF16)
    return contract(weights, with_ones(values), 1, 1), top * SCALE


def fresh_kernel(
    core_ref, q_ref, k_ref, v_ref, routes_ref, gates_ref, w_own_ref, w_other_ref,
    own_ref, other_ref, picks_ref, gates_out_ref, w_ref, done_ref,
):
    share = w_own_ref.shape[0] // 2
    copies = [
        pltpu.make_async_copy(
            source.at[pl.ds(j * share, share)], w_ref.at[i, pl.ds(j * share, share)], done_ref.at[i, j]
        )
        for i, source in enumerate((w_own_ref, w_other_ref))
        for j in range(2)
    ]
    for copy in copies:
        copy.start()
    q, k, v = q_ref[...].T, k_ref[...].T, v_ref[...].T
    half = q.shape[1] // 2
    first = core_ref[0] == 0
    lane = lax.broadcasted_iota(jnp.int32, (2 * half, LANES), 1)
    for h in range(q.shape[0] // HEAD_DIM):
        rows = slice(h * HEAD_DIM, (h + 1) * HEAD_DIM)
        sums, top = partial_softmax(q[rows], k[rows], v[rows])
        sums = jnp.where(lane == HEAD_DIM + 1, top, sums)
        lanes = slice(h * LANES, (h + 1) * LANES)
        own_ref[:, lanes] = jnp.where(first, sums[:half], sums[half:])
        other_ref[:, lanes] = jnp.where(first, sums[half:], sums[:half])
    slots = picks_ref.shape[2]
    for k, slot in enumerate(slots_of(routes_ref[...], slots // EXPERTS)):
        picks_ref[k] = chosen(slot, slots)
    gates_out_ref[...] = gates_ref[...]
    for copy in copies:
        copy.wait()


def attend_kernel(in_ref, fresh_ref, out_ref):
    patches, tokens = in_ref.shape[0], in_ref.shape[2]
    half, rows, steps = tokens // 2, 2 * tokens, patches // 2
    keys = jnp.concatenate([in_ref[j, HEAD_DIM : 2 * HEAD_DIM] for j in range(patches)], axis=1)
    values = with_ones(jnp.concatenate([in_ref[j, 2 * HEAD_DIM :] for j in range(patches)], axis=1))
    lane = lax.broadcasted_iota(jnp.int32, (rows, LANES), 1)
    own = (lax.broadcasted_iota(jnp.int32, (rows, rows), 0) < tokens) == (
        lax.broadcasted_iota(jnp.int32, (rows, rows), 1) < tokens
    )

    def scores_of(step):
        query = jnp.concatenate([in_ref[2 * step + i, :HEAD_DIM] for i in range(2)], axis=1)
        scores = contract(query, keys, 0, 0)
        first, last = step * rows, (step + 1) * rows
        parts = [jnp.where(own, -1e30, scores[:, first:last])]
        if step > 0:
            parts.insert(0, scores[:, :first])
        if step < steps - 1:
            parts.append(scores[:, last:])
        return jnp.concatenate(parts, axis=1)

    scores = scores_of(0)
    for step in range(steps):
        following = scores_of(step + 1) if step < steps - 1 else None
        top = scores.max(-1, keepdims=True)
        weights = jnp.exp2((scores - top) * (SCALE * math.log2(math.e))).astype(BF16)
        sums = contract(weights, values, 1, 1)
        total = sums[:, HEAD_DIM : HEAD_DIM + 1]
        log_total = top * SCALE + jnp.log(total)
        high = log_total.astype(BF16).astype(F32)
        rest = log_total - high
        middle = rest.astype(BF16).astype(F32)
        result = sums * (1.0 / total)
        result = jnp.where(lane == HEAD_DIM, high, result)
        result = jnp.where(lane == HEAD_DIM + 1, middle, result)
        result = jnp.where(lane == HEAD_DIM + 2, rest - middle, result)
        result = result.astype(BF16)
        for i in range(4):
            out_ref[4 * step + i] = result[i * half : (i + 1) * half]
        scores = following


def slots_of(routes, capacity):
    rows = routes.shape[0]
    expert = lax.broadcasted_iota(jnp.int32, (rows, EXPERTS), 1)
    names = [expert == routes[:, k : k + 1] for k in range(TOPK)]
    named = sum(n.astype(F32) for n in names).astype(BF16)
    earlier = (
        lax.broadcasted_iota(jnp.int32, (rows, rows), 1)
        < lax.broadcasted_iota(jnp.int32, (rows, rows), 0)
    ).astype(F32).astype(BF16)
    count = jnp.dot(earlier, named, preferred_element_type=F32)
    return [
        routes[:, k : k + 1] * capacity
        + jnp.where(names[k], count, 0.0).sum(-1, keepdims=True).astype(jnp.int32)
        for k in range(TOPK)
    ]


def chosen(slot, slots):
    return (
        (lax.broadcasted_iota(jnp.int32, (slot.shape[0], slots), 1) == slot).astype(F32).astype(BF16)
    )


def home_kernel(
    core_ref, far_ref, own_ref, other_ref, w_ref, residual_ref, modulation_ref,
    picks_ref, hidden_ref, buffer_ref, attended_ref,
):
    heads = far_ref.shape[0]
    core = core_ref[0]
    projected = None
    for side, near_ref in enumerate((own_ref, other_ref)):
        which = core if side == 0 else 1 - core
        for h in range(heads):
            far = far_ref[h, which].astype(F32)
            near = near_ref[:, h * LANES : (h + 1) * LANES]
            far_log = (
                far[:, HEAD_DIM : HEAD_DIM + 1]
                + far[:, HEAD_DIM + 1 : HEAD_DIM + 2]
                + far[:, HEAD_DIM + 2 : HEAD_DIM + 3]
            )
            near_total = near[:, HEAD_DIM : HEAD_DIM + 1]
            near_top = near[:, HEAD_DIM + 1 : HEAD_DIM + 2]
            top = jnp.maximum(far_log, near_top)
            far_weight = jnp.exp(far_log - top)
            near_weight = jnp.exp(near_top - top)
            scale = 1.0 / (far_weight + near_total * near_weight)
            merged = far * (far_weight * scale) + near * (near_weight * scale)
            attended_ref[side, :, h * HEAD_DIM : (h + 1) * HEAD_DIM] = merged[:, :HEAD_DIM].astype(BF16)
    for side in range(2):
        part = jnp.dot(attended_ref[side], w_ref[side], preferred_element_type=F32)
        projected = part if projected is None else projected + part
    hidden = residual_ref[...].astype(F32) + projected
    hidden_ref[...] = hidden
    centered = hidden - hidden.mean(-1, keepdims=True)
    variance = (centered * centered).mean(-1, keepdims=True)
    normed = (
        centered / jnp.sqrt(variance + 1e-06) * (1.0 + modulation_ref[1:2]) + modulation_ref[0:1]
    ).astype(BF16)
    buffer_ref[...] = contract(picks_ref[0] + picks_ref[1], normed, 0, 0).astype(BF16)


def attention_by_heads(queries, fresh_keys, fresh_values, stale_keys, stale_values, out_weight, residual, modulation, routes, gates):
    tokens, width = queries.shape
    heads = width // HEAD_DIM
    rows, features = residual.shape
    core = lax.axis_index("expert").astype(jnp.int32).reshape(1)
    swap = [(0, 1), (1, 0)]
    packed = pl.pallas_call(
        pack_kernel,
        out_shape=jax.ShapeDtypeStruct((heads, 3 * HEAD_DIM, tokens), BF16),
        in_specs=[ANY] * 3,
        out_specs=ANY,
        scratch_shapes=[
            pltpu.VMEM((3, tokens, width), BF16),
            pltpu.VMEM((heads, 3 * HEAD_DIM, tokens), BF16),
            pltpu.SemaphoreType.DMA((3,)),
            pltpu.SemaphoreType.DMA((3,)),
        ],
        compiler_params=pltpu.CompilerParams(vmem_limit_bytes=56 << 20),
        name="pack",
    )(queries, stale_keys, stale_values)
    w_other = lax.ppermute(out_weight, "expert", swap)
    gathered = lax.all_to_all(packed, "patch", split_axis=0, concat_axis=0, tiled=True)
    fresh_shape = jax.ShapeDtypeStruct((tokens // 2, heads * LANES), F32)
    slots = EXPERTS * (rows // 4)
    fresh_own, fresh_away, picks, gates, weights = pl.pallas_call(
        fresh_kernel,
        out_shape=(
            fresh_shape,
            fresh_shape,
            jax.ShapeDtypeStruct((TOPK, rows, slots), BF16),
            jax.ShapeDtypeStruct(gates.shape, F32),
            jax.ShapeDtypeStruct((2,) + out_weight.shape, BF16),
        ),
        in_specs=[SMEM] + [VMEM] * 5 + [ANY] * 2,
        out_specs=(VMEM,) * 4 + (ANY,),
        scratch_shapes=[pltpu.SemaphoreType.DMA((2, 2))],
        compiler_params=pltpu.CompilerParams(vmem_limit_bytes=16 << 20),
        cost_estimate=pl.CostEstimate(flops=5_000_000_000, bytes_accessed=2_000_000, transcendentals=200_000),
        name="fresh",
    )(core, queries, fresh_keys, fresh_values, routes, gates, out_weight, w_other)
    fresh_other = lax.ppermute(fresh_away, "expert", swap)
    stale = pl.pallas_call(
        attend_kernel,
        out_shape=jax.ShapeDtypeStruct((2 * heads, tokens // 2, LANES), BF16),
        in_specs=[VMEM, ANY],
        out_specs=VMEM,
        compiler_params=pltpu.CompilerParams(vmem_limit_bytes=16 << 20),
        cost_estimate=pl.CostEstimate(flops=100_000_000_000, bytes_accessed=2_000_000, transcendentals=1_000_000),
        name="attend",
    )(gathered, fresh_other)
    far = lax.all_to_all(stale, ("patch", "expert"), split_axis=0, concat_axis=0, tiled=True)
    hidden, buffer = pl.pallas_call(
        home_kernel,
        out_shape=(
            jax.ShapeDtypeStruct((rows, features), F32),
            jax.ShapeDtypeStruct((slots, features), BF16),
        ),
        in_specs=[SMEM] + [VMEM] * 7,
        out_specs=(VMEM, VMEM),
        scratch_shapes=[pltpu.VMEM((2, rows, width), BF16)],
        compiler_params=pltpu.CompilerParams(vmem_limit_bytes=20 << 20),
        cost_estimate=pl.CostEstimate(flops=100_000_000_000, bytes_accessed=8_000_000, transcendentals=100_000),
        name="home",
    )(core, far.reshape(heads, 2, rows, LANES), fresh_own, fresh_other, weights, residual, modulation, picks)
    return hidden, buffer, picks, gates


def split_heads(block_rows):
    return block_rows.reshape(block_rows.shape[0], block_rows.shape[1] // HEAD_DIM, HEAD_DIM)


def head_scores(query_heads, key_rows):
    products = jnp.einsum("qhd,khd->qhk", query_heads, split_heads(key_rows), preferred_element_type=F32)
    return products * SCALE


def weighted_values(weights, value_rows):
    return jnp.einsum(
        "qhk,khd->qhd", weights.astype(BF16), split_heads(value_rows), preferred_element_type=F32
    )


def attention_by_gather(queries, fresh_keys, fresh_values, stale_keys, stale_values, out_weight, residual, modulation, routes, gates):
    row_count = queries.shape[0]
    own_start = lax.axis_index("patch") * row_count
    query_heads = split_heads(queries)
    scores = head_scores(query_heads, fresh_keys)
    running_max = scores.max(-1)
    weights = jnp.exp(scores - running_max[..., None])
    denominator, numerator = weights.sum(-1), weighted_values(weights, fresh_values)
    piece_keys = lax.all_gather(stale_keys, "patch", axis=0, tiled=True)
    piece_values = lax.all_gather(stale_values, "patch", axis=0, tiled=True)
    scores = head_scores(query_heads, piece_keys)
    positions = jnp.arange(piece_keys.shape[0], dtype=jnp.int32)
    own_rows = (positions >= own_start) & (positions < own_start + row_count)
    scores = jnp.where(own_rows[None, None, :], -1e30, scores)
    newest = jnp.maximum(running_max, scores.max(-1))
    rescale = jnp.exp(running_max - newest)
    weights = jnp.where(own_rows[None, None, :], 0.0, jnp.exp(scores - newest[..., None]))
    denominator = denominator * rescale + weights.sum(-1)
    numerator = numerator * rescale[..., None] + weighted_values(weights, piece_values)
    attended = (numerator / denominator[..., None]).reshape(queries.shape).astype(BF16)
    hidden = residual.astype(F32) + lax.psum_scatter(
        jnp.dot(attended, out_weight, preferred_element_type=F32).astype(BF16),
        "expert",
        scatter_dimension=0,
        tiled=True,
    ).astype(F32)
    centered = hidden - hidden.mean(-1, keepdims=True)
    variance = (centered * centered).mean(-1, keepdims=True)
    normed = (centered / jnp.sqrt(variance + 1e-06) * (1.0 + modulation[1]) + modulation[0]).astype(BF16)
    capacity = residual.shape[0] // 4
    picks = [chosen(slot, EXPERTS * capacity) for slot in slots_of(routes, capacity)]
    return hidden, contract(picks[0] + picks[1], normed, 0, 0).astype(BF16), jnp.stack(picks), gates


def expert_kernel(x_ref, up_ref, down_ref, out_ref, units_ref):
    for part in chunks(up_ref.shape[2]):
        units_ref[:, part] = jax.nn.gelu(
            jnp.dot(x_ref[...], up_ref[0, :, part], preferred_element_type=F32), approximate=True
        ).astype(BF16)
    for part in chunks(out_ref.shape[1]):
        out_ref[:, part] = jnp.dot(
            units_ref[...], down_ref[0, :, part], preferred_element_type=F32
        ).astype(BF16)


def chunks(width):
    step = next(c for c in (1792, 896, LANES) if width % c == 0)
    return [slice(i, i + step) for i in range(0, width, step)]


def expert_slice(inputs, up_weight, down_weight):
    rows, features = inputs.shape
    return pl.pallas_call(
        expert_kernel,
        out_shape=jax.ShapeDtypeStruct((rows, features), BF16),
        in_specs=[VMEM] * 3,
        out_specs=VMEM,
        scratch_shapes=[pltpu.VMEM((rows, up_weight.shape[2]), BF16)],
        compiler_params=pltpu.CompilerParams(vmem_limit_bytes=16 << 20),
        name="experts",
    )(inputs, up_weight, down_weight)


def combine_kernel(hidden_ref, picks_ref, gates_ref, returned_ref, out_ref):
    slices = returned_ref.shape[1]
    slots = returned_ref.shape[0] * returned_ref.shape[2]
    mixed = hidden_ref[...]
    for s in range(slices):
        rows = returned_ref[:, s].reshape(slots, returned_ref.shape[3])
        for k in range(TOPK):
            mixed += gates_ref[:, k : k + 1] * jnp.dot(picks_ref[k], rows, preferred_element_type=F32)
    out_ref[...] = mixed.astype(BF16)


def body(
    queries, fresh_keys, fresh_values, stale_keys, stale_values, residual, out_weight, modulation,
    up_weight, down_weight, routes, gates,
):
    rows, features = residual.shape
    patch_count = lax.axis_size("patch")
    device_count = patch_count * lax.axis_size("expert")
    by_heads = queries.shape[1] // HEAD_DIM == patch_count and patch_count % 2 == 0 and lax.axis_size("expert") == 2
    attention = attention_by_heads if by_heads else attention_by_gather
    hidden, buffer, picks, gates = attention(
        queries, fresh_keys, fresh_values, stale_keys, stale_values, out_weight, residual, modulation, routes, gates
    )
    capacity = rows // 4
    slice_count = device_count // EXPERTS
    outgoing = jnp.broadcast_to(
        buffer.reshape(EXPERTS, 1, capacity, features), (EXPERTS, slice_count, capacity, features)
    ).reshape(device_count, capacity, features)
    arrived = lax.all_to_all(outgoing, ("patch", "expert"), split_axis=0, concat_axis=0, tiled=True)
    outputs = expert_slice(arrived.reshape(device_count * capacity, features), up_weight, down_weight)
    returned = lax.all_to_all(
        outputs.reshape(device_count, capacity, features),
        ("patch", "expert"),
        split_axis=0,
        concat_axis=0,
        tiled=True,
    )
    return pl.pallas_call(
        combine_kernel,
        out_shape=jax.ShapeDtypeStruct((rows, features), BF16),
        in_specs=[VMEM] * 4,
        out_specs=VMEM,
        compiler_params=pltpu.CompilerParams(vmem_limit_bytes=20 << 20),
        name="combine",
    )(hidden, picks, gates, returned.reshape(EXPERTS, slice_count, capacity, features))


def solution(mesh):
    tokens = P(("group", "patch"), "expert")
    rows = P(("group", "patch", "expert"), None)
    weight = P(("patch", "expert"), None, None)
    placed = (
        tokens, tokens, tokens, tokens, tokens, rows, P("expert", None), P("group", None), weight, weight, rows, rows,
    )
    return jax.shard_map(body, mesh=mesh, in_specs=placed, out_specs=rows, check_vma=False)
```

```python
import functools
import math

import jax
import jax.numpy as jnp
from jax import lax
from jax.experimental import pallas as pl
from jax.experimental.pallas import tpu as pltpu
from jax.sharding import PartitionSpec as P

HEAD_DIM = 112
EXPERTS = 16
TOPK = 2
LANES = 128
SCALE = 1.0 / math.sqrt(HEAD_DIM)
BF16 = jnp.bfloat16
F32 = jnp.float32
VMEM = pl.BlockSpec(memory_space=pltpu.VMEM)
SMEM = pl.BlockSpec(memory_space=pltpu.SMEM)
ANY = pl.BlockSpec(memory_space=pl.ANY)


def contract(a, b, dim_a, dim_b):
    return lax.dot_general(a, b, (((dim_a,), (dim_b,)), ((), ())), preferred_element_type=F32)


def pack_kernel(q_ref, k_ref, v_ref, out_ref, rows_ref, turned_ref, in_sem, out_sem):
    loads = [
        pltpu.make_async_copy(ref, rows_ref.at[i], in_sem.at[i]) for i, ref in enumerate((q_ref, k_ref, v_ref))
    ]
    stores = [
        pltpu.make_async_copy(
            turned_ref.at[:, pl.ds(i * HEAD_DIM, HEAD_DIM)],
            out_ref.at[:, pl.ds(i * HEAD_DIM, HEAD_DIM)],
            out_sem.at[i],
        )
        for i in range(3)
    ]
    for load in loads:
        load.start()
    for i in range(3):
        loads[i].wait()
        turned = rows_ref[i].T
        for h in range(turned_ref.shape[0]):
            turned_ref[h, i * HEAD_DIM : (i + 1) * HEAD_DIM, :] = turned[h * HEAD_DIM : (h + 1) * HEAD_DIM]
        stores[i].start()
    for store in stores:
        store.wait()


def with_ones(values):
    return jnp.concatenate([values, jnp.ones((LANES - HEAD_DIM, values.shape[1]), BF16)], axis=0)


def partial_softmax(query, keys, values):
    scores = contract(query, keys, 0, 0)
    top = scores.max(-1, keepdims=True)
    weights = jnp.exp((scores - top) * SCALE).astype(BF16)
    return contract(weights, with_ones(values), 1, 1), top * SCALE


def fresh_kernel(
    core_ref, q_ref, k_ref, v_ref, routes_ref, gates_ref, w_own_ref, w_other_ref,
    own_ref, other_ref, picks_ref, gates_out_ref, w_ref, done_ref,
):
    share = w_own_ref.shape[0] // 2
    copies = [
        pltpu.make_async_copy(
            source.at[pl.ds(j * share, share)], w_ref.at[i, pl.ds(j * share, share)], done_ref.at[i, j]
        )
        for i, source in enumerate((w_own_ref, w_other_ref))
        for j in range(2)
    ]
    for copy in copies:
        copy.start()
    q, k, v = q_ref[...].T, k_ref[...].T, v_ref[...].T
    half = q.shape[1] // 2
    first = core_ref[0] == 0
    lane = lax.broadcasted_iota(jnp.int32, (2 * half, LANES), 1)
    for h in range(q.shape[0] // HEAD_DIM):
        rows = slice(h * HEAD_DIM, (h + 1) * HEAD_DIM)
        sums, top = partial_softmax(q[rows], k[rows], v[rows])
        total = sums[:, HEAD_DIM : HEAD_DIM + 1]
        sums = jnp.where(lane == HEAD_DIM, top + jnp.log(total), sums * (1.0 / total))
        lanes = slice(h * LANES, (h + 1) * LANES)
        own_ref[:, lanes] = jnp.where(first, sums[:half], sums[half:])
        other_ref[:, lanes] = jnp.where(first, sums[half:], sums[:half])
    slots = picks_ref.shape[2]
    for k, slot in enumerate(slots_of(routes_ref[...], slots // EXPERTS)):
        picks_ref[k] = chosen(slot, slots)
    gates_out_ref[...] = gates_ref[...]
    for copy in copies:
        copy.wait()


def attend_kernel(in_ref, fresh_ref, out_ref):
    patches, tokens = in_ref.shape[0], in_ref.shape[2]
    half, rows, steps = tokens // 2, 2 * tokens, patches // 2
    keys = jnp.concatenate([in_ref[j, HEAD_DIM : 2 * HEAD_DIM] for j in range(patches)], axis=1)
    values = with_ones(jnp.concatenate([in_ref[j, 2 * HEAD_DIM :] for j in range(patches)], axis=1))
    lane = lax.broadcasted_iota(jnp.int32, (rows, LANES), 1)
    own = (lax.broadcasted_iota(jnp.int32, (rows, rows), 0) < tokens) == (
        lax.broadcasted_iota(jnp.int32, (rows, rows), 1) < tokens
    )

    def scores_of(step):
        query = jnp.concatenate([in_ref[2 * step + i, :HEAD_DIM] for i in range(2)], axis=1)
        scores = contract(query, keys, 0, 0)
        first, last = step * rows, (step + 1) * rows
        parts = [jnp.where(own, -1e30, scores[:, first:last])]
        if step > 0:
            parts.insert(0, scores[:, :first])
        if step < steps - 1:
            parts.append(scores[:, last:])
        return jnp.concatenate(parts, axis=1)

    scores = scores_of(0)
    for step in range(steps):
        following = scores_of(step + 1) if step < steps - 1 else None
        top = scores.max(-1, keepdims=True)
        weights = jnp.exp2((scores - top) * (SCALE * math.log2(math.e))).astype(BF16)
        sums = contract(weights, values, 1, 1)
        total = sums[:, HEAD_DIM : HEAD_DIM + 1]
        log_total = top * SCALE + jnp.log(total)
        high = log_total.astype(BF16).astype(F32)
        rest = log_total - high
        middle = rest.astype(BF16).astype(F32)
        result = sums * (1.0 / total)
        result = jnp.where(lane == HEAD_DIM, high, result)
        result = jnp.where(lane == HEAD_DIM + 1, middle, result)
        result = jnp.where(lane == HEAD_DIM + 2, rest - middle, result)
        result = result.astype(BF16)
        for i in range(4):
            out_ref[4 * step + i] = result[i * half : (i + 1) * half]
        scores = following


def slots_of(routes, capacity):
    rows = routes.shape[0]
    expert = lax.broadcasted_iota(jnp.int32, (rows, EXPERTS), 1)
    names = [expert == routes[:, k : k + 1] for k in range(TOPK)]
    named = sum(n.astype(F32) for n in names).astype(BF16)
    earlier = (
        lax.broadcasted_iota(jnp.int32, (rows, rows), 1)
        < lax.broadcasted_iota(jnp.int32, (rows, rows), 0)
    ).astype(F32).astype(BF16)
    count = jnp.dot(earlier, named, preferred_element_type=F32)
    return [
        routes[:, k : k + 1] * capacity
        + jnp.where(names[k], count, 0.0).sum(-1, keepdims=True).astype(jnp.int32)
        for k in range(TOPK)
    ]


def chosen(slot, slots):
    return (
        (lax.broadcasted_iota(jnp.int32, (slot.shape[0], slots), 1) == slot).astype(F32).astype(BF16)
    )


def home_kernel(
    core_ref, far_ref, own_ref, other_ref, w_ref, residual_ref, modulation_ref,
    picks_ref, hidden_ref, buffer_ref, attended_ref,
):
    heads = far_ref.shape[0]
    core = core_ref[0]
    projected = None
    for side, near_ref in enumerate((own_ref, other_ref)):
        which = core if side == 0 else 1 - core
        for h in range(heads):
            far = far_ref[h, which].astype(F32)
            near = near_ref[:, h * LANES : (h + 1) * LANES]
            far_log = (
                far[:, HEAD_DIM : HEAD_DIM + 1]
                + far[:, HEAD_DIM + 1 : HEAD_DIM + 2]
                + far[:, HEAD_DIM + 2 : HEAD_DIM + 3]
            )
            near_log = near[:, HEAD_DIM : HEAD_DIM + 1]
            near_share = 1.0 / (1.0 + jnp.exp(jnp.minimum(far_log - near_log, 80.0)))
            merged = far + (near - far) * near_share
            attended_ref[side, :, h * HEAD_DIM : (h + 1) * HEAD_DIM] = merged[:, :HEAD_DIM].astype(BF16)
    for side in range(2):
        part = jnp.dot(attended_ref[side], w_ref[side], preferred_element_type=F32)
        projected = part if projected is None else projected + part
    hidden = residual_ref[...].astype(F32) + projected
    hidden_ref[...] = hidden
    centered = hidden - hidden.mean(-1, keepdims=True)
    variance = (centered * centered).mean(-1, keepdims=True)
    normed = (
        centered / jnp.sqrt(variance + 1e-06) * (1.0 + modulation_ref[1:2]) + modulation_ref[0:1]
    ).astype(BF16)
    buffer_ref[...] = contract(picks_ref[0] + picks_ref[1], normed, 0, 0).astype(BF16)


def attention_by_heads(queries, fresh_keys, fresh_values, stale_keys, stale_values, out_weight, residual, modulation, routes, gates):
    tokens, width = queries.shape
    heads = width // HEAD_DIM
    rows, features = residual.shape
    core = lax.axis_index("expert").astype(jnp.int32).reshape(1)
    swap = [(0, 1), (1, 0)]
    packed = pl.pallas_call(
        pack_kernel,
        out_shape=jax.ShapeDtypeStruct((heads, 3 * HEAD_DIM, tokens), BF16),
        in_specs=[ANY] * 3,
        out_specs=ANY,
        scratch_shapes=[
            pltpu.VMEM((3, tokens, width), BF16),
            pltpu.VMEM((heads, 3 * HEAD_DIM, tokens), BF16),
            pltpu.SemaphoreType.DMA((3,)),
            pltpu.SemaphoreType.DMA((3,)),
        ],
        compiler_params=pltpu.CompilerParams(vmem_limit_bytes=56 << 20),
        name="pack",
    )(queries, stale_keys, stale_values)
    w_other = lax.ppermute(out_weight, "expert", swap)
    gathered = lax.all_to_all(packed, "patch", split_axis=0, concat_axis=0, tiled=True)
    fresh_shape = jax.ShapeDtypeStruct((tokens // 2, heads * LANES), F32)
    slots = EXPERTS * (rows // 4)
    fresh_own, fresh_away, picks, gates, weights = pl.pallas_call(
        fresh_kernel,
        out_shape=(
            fresh_shape,
            fresh_shape,
            jax.ShapeDtypeStruct((TOPK, rows, slots), BF16),
            jax.ShapeDtypeStruct(gates.shape, F32),
            jax.ShapeDtypeStruct((2,) + out_weight.shape, BF16),
        ),
        in_specs=[SMEM] + [VMEM] * 5 + [ANY] * 2,
        out_specs=(VMEM,) * 4 + (ANY,),
        scratch_shapes=[pltpu.SemaphoreType.DMA((2, 2))],
        compiler_params=pltpu.CompilerParams(vmem_limit_bytes=16 << 20),
        cost_estimate=pl.CostEstimate(flops=5_000_000_000, bytes_accessed=2_000_000, transcendentals=200_000),
        name="fresh",
    )(core, queries, fresh_keys, fresh_values, routes, gates, out_weight, w_other)
    fresh_other = lax.ppermute(fresh_away, "expert", swap)
    stale = pl.pallas_call(
        attend_kernel,
        out_shape=jax.ShapeDtypeStruct((2 * heads, tokens // 2, LANES), BF16),
        in_specs=[VMEM, ANY],
        out_specs=VMEM,
        compiler_params=pltpu.CompilerParams(vmem_limit_bytes=16 << 20),
        cost_estimate=pl.CostEstimate(flops=100_000_000_000, bytes_accessed=2_000_000, transcendentals=1_000_000),
        name="attend",
    )(gathered, fresh_other)
    far = lax.all_to_all(stale, ("patch", "expert"), split_axis=0, concat_axis=0, tiled=True)
    hidden, buffer = pl.pallas_call(
        home_kernel,
        out_shape=(
            jax.ShapeDtypeStruct((rows, features), F32),
            jax.ShapeDtypeStruct((slots, features), BF16),
        ),
        in_specs=[SMEM] + [VMEM] * 7,
        out_specs=(VMEM, VMEM),
        scratch_shapes=[pltpu.VMEM((2, rows, width), BF16)],
        compiler_params=pltpu.CompilerParams(vmem_limit_bytes=20 << 20),
        cost_estimate=pl.CostEstimate(flops=100_000_000_000, bytes_accessed=8_000_000, transcendentals=100_000),
        name="home",
    )(core, far.reshape(heads, 2, rows, LANES), fresh_own, fresh_other, weights, residual, modulation, picks)
    return hidden, buffer, picks, gates


def split_heads(block_rows):
    return block_rows.reshape(block_rows.shape[0], block_rows.shape[1] // HEAD_DIM, HEAD_DIM)


def head_scores(query_heads, key_rows):
    products = jnp.einsum("qhd,khd->qhk", query_heads, split_heads(key_rows), preferred_element_type=F32)
    return products * SCALE


def weighted_values(weights, value_rows):
    return jnp.einsum(
        "qhk,khd->qhd", weights.astype(BF16), split_heads(value_rows), preferred_element_type=F32
    )


def attention_by_gather(queries, fresh_keys, fresh_values, stale_keys, stale_values, out_weight, residual, modulation, routes, gates):
    row_count = queries.shape[0]
    own_start = lax.axis_index("patch") * row_count
    query_heads = split_heads(queries)
    scores = head_scores(query_heads, fresh_keys)
    running_max = scores.max(-1)
    weights = jnp.exp(scores - running_max[..., None])
    denominator, numerator = weights.sum(-1), weighted_values(weights, fresh_values)
    piece_keys = lax.all_gather(stale_keys, "patch", axis=0, tiled=True)
    piece_values = lax.all_gather(stale_values, "patch", axis=0, tiled=True)
    scores = head_scores(query_heads, piece_keys)
    positions = jnp.arange(piece_keys.shape[0], dtype=jnp.int32)
    own_rows = (positions >= own_start) & (positions < own_start + row_count)
    scores = jnp.where(own_rows[None, None, :], -1e30, scores)
    newest = jnp.maximum(running_max, scores.max(-1))
    rescale = jnp.exp(running_max - newest)
    weights = jnp.where(own_rows[None, None, :], 0.0, jnp.exp(scores - newest[..., None]))
    denominator = denominator * rescale + weights.sum(-1)
    numerator = numerator * rescale[..., None] + weighted_values(weights, piece_values)
    attended = (numerator / denominator[..., None]).reshape(queries.shape).astype(BF16)
    hidden = residual.astype(F32) + lax.psum_scatter(
        jnp.dot(attended, out_weight, preferred_element_type=F32).astype(BF16),
        "expert",
        scatter_dimension=0,
        tiled=True,
    ).astype(F32)
    centered = hidden - hidden.mean(-1, keepdims=True)
    variance = (centered * centered).mean(-1, keepdims=True)
    normed = (centered / jnp.sqrt(variance + 1e-06) * (1.0 + modulation[1]) + modulation[0]).astype(BF16)
    capacity = residual.shape[0] // 4
    picks = [chosen(slot, EXPERTS * capacity) for slot in slots_of(routes, capacity)]
    return hidden, contract(picks[0] + picks[1], normed, 0, 0).astype(BF16), jnp.stack(picks), gates


def expert_kernel(x_ref, up_ref, down_ref, out_ref, units_ref):
    for part in chunks(up_ref.shape[2]):
        units_ref[:, part] = jax.nn.gelu(
            jnp.dot(x_ref[...], up_ref[0, :, part], preferred_element_type=F32), approximate=True
        ).astype(BF16)
    for part in chunks(out_ref.shape[1]):
        out_ref[:, part] = jnp.dot(
            units_ref[...], down_ref[0, :, part], preferred_element_type=F32
        ).astype(BF16)


def chunks(width):
    step = next(c for c in (1792, 896, LANES) if width % c == 0)
    return [slice(i, i + step) for i in range(0, width, step)]


def expert_slice(inputs, up_weight, down_weight):
    rows, features = inputs.shape
    return pl.pallas_call(
        expert_kernel,
        out_shape=jax.ShapeDtypeStruct((rows, features), BF16),
        in_specs=[VMEM] * 3,
        out_specs=VMEM,
        scratch_shapes=[pltpu.VMEM((rows, up_weight.shape[2]), BF16)],
        compiler_params=pltpu.CompilerParams(vmem_limit_bytes=16 << 20),
        name="experts",
    )(inputs, up_weight, down_weight)


def combine_kernel(hidden_ref, picks_ref, gates_ref, returned_ref, out_ref):
    slices = returned_ref.shape[1]
    slots = returned_ref.shape[0] * returned_ref.shape[2]
    mixed = hidden_ref[...]
    for s in range(slices):
        rows = returned_ref[:, s].reshape(slots, returned_ref.shape[3])
        for k in range(TOPK):
            mixed += gates_ref[:, k : k + 1] * jnp.dot(picks_ref[k], rows, preferred_element_type=F32)
    out_ref[...] = mixed.astype(BF16)


def body(
    queries, fresh_keys, fresh_values, stale_keys, stale_values, residual, out_weight, modulation,
    up_weight, down_weight, routes, gates,
):
    rows, features = residual.shape
    patch_count = lax.axis_size("patch")
    device_count = patch_count * lax.axis_size("expert")
    by_heads = queries.shape[1] // HEAD_DIM == patch_count and patch_count % 2 == 0 and lax.axis_size("expert") == 2
    attention = attention_by_heads if by_heads else attention_by_gather
    hidden, buffer, picks, gates = attention(
        queries, fresh_keys, fresh_values, stale_keys, stale_values, out_weight, residual, modulation, routes, gates
    )
    capacity = rows // 4
    slice_count = device_count // EXPERTS
    outgoing = jnp.broadcast_to(
        buffer.reshape(EXPERTS, 1, capacity, features), (EXPERTS, slice_count, capacity, features)
    ).reshape(device_count, capacity, features)
    arrived = lax.all_to_all(outgoing, ("patch", "expert"), split_axis=0, concat_axis=0, tiled=True)
    outputs = expert_slice(arrived.reshape(device_count * capacity, features), up_weight, down_weight)
    returned = lax.all_to_all(
        outputs.reshape(device_count, capacity, features),
        ("patch", "expert"),
        split_axis=0,
        concat_axis=0,
        tiled=True,
    )
    return pl.pallas_call(
        combine_kernel,
        out_shape=jax.ShapeDtypeStruct((rows, features), BF16),
        in_specs=[VMEM] * 4,
        out_specs=VMEM,
        compiler_params=pltpu.CompilerParams(vmem_limit_bytes=20 << 20),
        name="combine",
    )(hidden, picks, gates, returned.reshape(EXPERTS, slice_count, capacity, features))


def solution(mesh):
    tokens = P(("group", "patch"), "expert")
    rows = P(("group", "patch", "expert"), None)
    weight = P(("patch", "expert"), None, None)
    placed = (
        tokens, tokens, tokens, tokens, tokens, rows, P("expert", None), P("group", None), weight, weight, rows, rows,
    )
    return jax.shard_map(body, mesh=mesh, in_specs=placed, out_specs=rows, check_vma=False)
```

```python
import functools
import math

import jax
import jax.numpy as jnp
from jax import lax
from jax.experimental import pallas as pl
from jax.experimental.pallas import tpu as pltpu
from jax.sharding import PartitionSpec as P

HEAD_DIM = 112
EXPERTS = 16
TOPK = 2
LANES = 128
SCALE = 1.0 / math.sqrt(HEAD_DIM)
BF16 = jnp.bfloat16
F32 = jnp.float32
VMEM = pl.BlockSpec(memory_space=pltpu.VMEM)
SMEM = pl.BlockSpec(memory_space=pltpu.SMEM)
ANY = pl.BlockSpec(memory_space=pl.ANY)


def contract(a, b, dim_a, dim_b):
    return lax.dot_general(a, b, (((dim_a,), (dim_b,)), ((), ())), preferred_element_type=F32)


def pack_kernel(q_ref, k_ref, v_ref, out_ref, rows_ref, turned_ref, in_sem, out_sem):
    loads = [
        pltpu.make_async_copy(ref, rows_ref.at[i], in_sem.at[i]) for i, ref in enumerate((q_ref, k_ref, v_ref))
    ]
    stores = [
        pltpu.make_async_copy(
            turned_ref.at[:, pl.ds(i * HEAD_DIM, HEAD_DIM)],
            out_ref.at[:, pl.ds(i * HEAD_DIM, HEAD_DIM)],
            out_sem.at[i],
        )
        for i in range(3)
    ]
    for load in loads:
        load.start()
    for i in range(3):
        loads[i].wait()
        turned = rows_ref[i].T
        for h in range(turned_ref.shape[0]):
            turned_ref[h, i * HEAD_DIM : (i + 1) * HEAD_DIM, :] = turned[h * HEAD_DIM : (h + 1) * HEAD_DIM]
        stores[i].start()
    for store in stores:
        store.wait()


def with_ones(values):
    return jnp.concatenate([values, jnp.ones((LANES - HEAD_DIM, values.shape[1]), BF16)], axis=0)


def partial_softmax(query, keys, values):
    scores = contract(query, keys, 0, 0)
    top = scores.max(-1, keepdims=True)
    weights = jnp.exp((scores - top) * SCALE).astype(BF16)
    return contract(weights, with_ones(values), 1, 1), top * SCALE


def fresh_kernel(
    core_ref, q_ref, k_ref, v_ref, routes_ref, gates_ref, w_own_ref, w_other_ref,
    own_ref, other_ref, picks_ref, gates_out_ref, w_ref, done_ref,
):
    share = w_own_ref.shape[0] // 2
    copies = [
        pltpu.make_async_copy(
            source.at[pl.ds(j * share, share)], w_ref.at[i, pl.ds(j * share, share)], done_ref.at[i, j]
        )
        for i, source in enumerate((w_own_ref, w_other_ref))
        for j in range(2)
    ]
    for copy in copies:
        copy.start()
    q, k, v = q_ref[...].T, k_ref[...].T, v_ref[...].T
    half = q.shape[1] // 2
    first = core_ref[0] == 0
    lane = lax.broadcasted_iota(jnp.int32, (2 * half, LANES), 1)
    for h in range(q.shape[0] // HEAD_DIM):
        rows = slice(h * HEAD_DIM, (h + 1) * HEAD_DIM)
        sums, top = partial_softmax(q[rows], k[rows], v[rows])
        total = sums[:, HEAD_DIM : HEAD_DIM + 1]
        sums = jnp.where(lane == HEAD_DIM, top + jnp.log(total), sums * (1.0 / total))
        lanes = slice(h * LANES, (h + 1) * LANES)
        own_ref[:, lanes] = jnp.where(first, sums[:half], sums[half:])
        other_ref[:, lanes] = jnp.where(first, sums[half:], sums[:half])
    slots = picks_ref.shape[2]
    for k, slot in enumerate(slots_of(routes_ref[...], slots // EXPERTS)):
        picks_ref[k] = chosen(slot, slots)
    gates_out_ref[...] = gates_ref[...]
    for copy in copies:
        copy.wait()


def attend_kernel(in_ref, fresh_ref, out_ref):
    patches, tokens = in_ref.shape[0], in_ref.shape[2]
    half, rows, steps = tokens // 2, 2 * tokens, patches // 2
    keys = jnp.concatenate([in_ref[j, HEAD_DIM : 2 * HEAD_DIM] for j in range(patches)], axis=1)
    values = with_ones(jnp.concatenate([in_ref[j, 2 * HEAD_DIM :] for j in range(patches)], axis=1))
    lane = lax.broadcasted_iota(jnp.int32, (rows, LANES), 1)
    own = (lax.broadcasted_iota(jnp.int32, (rows, rows), 0) < tokens) == (
        lax.broadcasted_iota(jnp.int32, (rows, rows), 1) < tokens
    )

    def scores_of(step):
        query = jnp.concatenate([in_ref[2 * step + i, :HEAD_DIM] for i in range(2)], axis=1)
        scores = contract(query, keys, 0, 0)
        first, last = step * rows, (step + 1) * rows
        parts = [jnp.where(own, -1e30, scores[:, first:last])]
        if step > 0:
            parts.insert(0, scores[:, :first])
        if step < steps - 1:
            parts.append(scores[:, last:])
        return jnp.concatenate(parts, axis=1)

    scores = scores_of(0)
    for step in range(steps):
        following = scores_of(step + 1) if step < steps - 1 else None
        top = scores.max(-1, keepdims=True)
        weights = jnp.exp2((scores - top) * (SCALE * math.log2(math.e))).astype(BF16)
        sums = contract(weights, values, 1, 1)
        total = sums[:, HEAD_DIM : HEAD_DIM + 1]
        log_total = top * SCALE + jnp.log(total)
        high = log_total.astype(BF16).astype(F32)
        rest = log_total - high
        middle = rest.astype(BF16).astype(F32)
        result = sums * (1.0 / total)
        result = jnp.where(lane == HEAD_DIM, high, result)
        result = jnp.where(lane == HEAD_DIM + 1, middle, result)
        result = jnp.where(lane == HEAD_DIM + 2, rest - middle, result)
        result = result.astype(BF16)
        for i in range(4):
            out_ref[4 * step + i] = result[i * half : (i + 1) * half]
        scores = following


def slots_of(routes, capacity):
    rows = routes.shape[0]
    expert = lax.broadcasted_iota(jnp.int32, (rows, EXPERTS), 1)
    names = [expert == routes[:, k : k + 1] for k in range(TOPK)]
    named = sum(n.astype(F32) for n in names).astype(BF16)
    earlier = (
        lax.broadcasted_iota(jnp.int32, (rows, rows), 1)
        < lax.broadcasted_iota(jnp.int32, (rows, rows), 0)
    ).astype(F32).astype(BF16)
    count = jnp.dot(earlier, named, preferred_element_type=F32)
    return [
        routes[:, k : k + 1] * capacity
        + jnp.where(names[k], count, 0.0).sum(-1, keepdims=True).astype(jnp.int32)
        for k in range(TOPK)
    ]


def chosen(slot, slots):
    return (
        (lax.broadcasted_iota(jnp.int32, (slot.shape[0], slots), 1) == slot).astype(F32).astype(BF16)
    )


def home_kernel(
    core_ref, far_ref, own_ref, other_ref, w_ref, residual_ref, modulation_ref,
    picks_ref, hidden_ref, buffer_ref, attended_ref,
):
    heads = far_ref.shape[0]
    core = core_ref[0]
    projected = None
    for side, near_ref in enumerate((own_ref, other_ref)):
        which = core if side == 0 else 1 - core
        for h in range(heads):
            far = far_ref[h, which].astype(F32)
            near = near_ref[:, h * LANES : (h + 1) * LANES]
            far_log = (
                far[:, HEAD_DIM : HEAD_DIM + 1]
                + far[:, HEAD_DIM + 1 : HEAD_DIM + 2]
                + far[:, HEAD_DIM + 2 : HEAD_DIM + 3]
            )
            near_log = near[:, HEAD_DIM : HEAD_DIM + 1]
            near_share = 1.0 / (1.0 + jnp.exp(jnp.minimum(far_log - near_log, 80.0)))
            merged = far + (near - far) * near_share
            attended_ref[side, :, h * HEAD_DIM : (h + 1) * HEAD_DIM] = merged[:, :HEAD_DIM].astype(BF16)
    for side in range(2):
        part = jnp.dot(attended_ref[side], w_ref[side], preferred_element_type=F32)
        projected = part if projected is None else projected + part
    hidden = residual_ref[...].astype(F32) + projected
    hidden_ref[...] = hidden
    centered = hidden - hidden.mean(-1, keepdims=True)
    variance = (centered * centered).mean(-1, keepdims=True)
    normed = (
        centered / jnp.sqrt(variance + 1e-06) * (1.0 + modulation_ref[1:2]) + modulation_ref[0:1]
    ).astype(BF16)
    buffer_ref[...] = contract(picks_ref[0] + picks_ref[1], normed, 0, 0).astype(BF16)


def attention_by_heads(queries, fresh_keys, fresh_values, stale_keys, stale_values, out_weight, residual, modulation, routes, gates):
    tokens, width = queries.shape
    heads = width // HEAD_DIM
    rows, features = residual.shape
    core = lax.axis_index("expert").astype(jnp.int32).reshape(1)
    swap = [(0, 1), (1, 0)]
    packed = pl.pallas_call(
        pack_kernel,
        out_shape=jax.ShapeDtypeStruct((heads, 3 * HEAD_DIM, tokens), BF16),
        in_specs=[ANY] * 3,
        out_specs=ANY,
        scratch_shapes=[
            pltpu.VMEM((3, tokens, width), BF16),
            pltpu.VMEM((heads, 3 * HEAD_DIM, tokens), BF16),
            pltpu.SemaphoreType.DMA((3,)),
            pltpu.SemaphoreType.DMA((3,)),
        ],
        compiler_params=pltpu.CompilerParams(vmem_limit_bytes=56 << 20),
        name="pack",
    )(queries, stale_keys, stale_values)
    w_other = lax.ppermute(out_weight, "expert", swap)
    gathered = lax.all_to_all(packed, "patch", split_axis=0, concat_axis=0, tiled=True)
    fresh_shape = jax.ShapeDtypeStruct((tokens // 2, heads * LANES), F32)
    slots = EXPERTS * (rows // 4)
    fresh_own, fresh_away, picks, gates, weights = pl.pallas_call(
        fresh_kernel,
        out_shape=(
            fresh_shape,
            fresh_shape,
            jax.ShapeDtypeStruct((TOPK, rows, slots), BF16),
            jax.ShapeDtypeStruct(gates.shape, F32),
            jax.ShapeDtypeStruct((2,) + out_weight.shape, BF16),
        ),
        in_specs=[SMEM] + [VMEM] * 5 + [ANY] * 2,
        out_specs=(VMEM,) * 4 + (ANY,),
        scratch_shapes=[pltpu.SemaphoreType.DMA((2, 2))],
        compiler_params=pltpu.CompilerParams(vmem_limit_bytes=16 << 20),
        cost_estimate=pl.CostEstimate(flops=5_000_000_000, bytes_accessed=2_000_000, transcendentals=200_000),
        name="fresh",
    )(core, queries, fresh_keys, fresh_values, routes, gates, out_weight, w_other)
    fresh_other = lax.ppermute(fresh_away, "expert", swap)
    stale = pl.pallas_call(
        attend_kernel,
        out_shape=jax.ShapeDtypeStruct((2 * heads, tokens // 2, LANES), BF16),
        in_specs=[VMEM, ANY],
        out_specs=VMEM,
        compiler_params=pltpu.CompilerParams(vmem_limit_bytes=16 << 20),
        cost_estimate=pl.CostEstimate(flops=100_000_000_000, bytes_accessed=2_000_000, transcendentals=1_000_000),
        name="attend",
    )(gathered, fresh_other)
    far = lax.all_to_all(stale, ("patch", "expert"), split_axis=0, concat_axis=0, tiled=True)
    hidden, buffer = pl.pallas_call(
        home_kernel,
        out_shape=(
            jax.ShapeDtypeStruct((rows, features), F32),
            jax.ShapeDtypeStruct((slots, features), BF16),
        ),
        in_specs=[SMEM] + [VMEM] * 7,
        out_specs=(VMEM, VMEM),
        scratch_shapes=[pltpu.VMEM((2, rows, width), BF16)],
        compiler_params=pltpu.CompilerParams(vmem_limit_bytes=20 << 20),
        cost_estimate=pl.CostEstimate(flops=100_000_000_000, bytes_accessed=8_000_000, transcendentals=100_000),
        name="home",
    )(core, far.reshape(heads, 2, rows, LANES), fresh_own, fresh_other, weights, residual, modulation, picks)
    return hidden, buffer, picks, gates


def split_heads(block_rows):
    return block_rows.reshape(block_rows.shape[0], block_rows.shape[1] // HEAD_DIM, HEAD_DIM)


def head_scores(query_heads, key_rows):
    products = jnp.einsum("qhd,khd->qhk", query_heads, split_heads(key_rows), preferred_element_type=F32)
    return products * SCALE


def weighted_values(weights, value_rows):
    return jnp.einsum(
        "qhk,khd->qhd", weights.astype(BF16), split_heads(value_rows), preferred_element_type=F32
    )


def attention_by_gather(queries, fresh_keys, fresh_values, stale_keys, stale_values, out_weight, residual, modulation, routes, gates):
    row_count = queries.shape[0]
    own_start = lax.axis_index("patch") * row_count
    query_heads = split_heads(queries)
    scores = head_scores(query_heads, fresh_keys)
    running_max = scores.max(-1)
    weights = jnp.exp(scores - running_max[..., None])
    denominator, numerator = weights.sum(-1), weighted_values(weights, fresh_values)
    piece_keys = lax.all_gather(stale_keys, "patch", axis=0, tiled=True)
    piece_values = lax.all_gather(stale_values, "patch", axis=0, tiled=True)
    scores = head_scores(query_heads, piece_keys)
    positions = jnp.arange(piece_keys.shape[0], dtype=jnp.int32)
    own_rows = (positions >= own_start) & (positions < own_start + row_count)
    scores = jnp.where(own_rows[None, None, :], -1e30, scores)
    newest = jnp.maximum(running_max, scores.max(-1))
    rescale = jnp.exp(running_max - newest)
    weights = jnp.where(own_rows[None, None, :], 0.0, jnp.exp(scores - newest[..., None]))
    denominator = denominator * rescale + weights.sum(-1)
    numerator = numerator * rescale[..., None] + weighted_values(weights, piece_values)
    attended = (numerator / denominator[..., None]).reshape(queries.shape).astype(BF16)
    hidden = residual.astype(F32) + lax.psum_scatter(
        jnp.dot(attended, out_weight, preferred_element_type=F32).astype(BF16),
        "expert",
        scatter_dimension=0,
        tiled=True,
    ).astype(F32)
    centered = hidden - hidden.mean(-1, keepdims=True)
    variance = (centered * centered).mean(-1, keepdims=True)
    normed = (centered / jnp.sqrt(variance + 1e-06) * (1.0 + modulation[1]) + modulation[0]).astype(BF16)
    capacity = residual.shape[0] // 4
    picks = [chosen(slot, EXPERTS * capacity) for slot in slots_of(routes, capacity)]
    return hidden, contract(picks[0] + picks[1], normed, 0, 0).astype(BF16), jnp.stack(picks), gates


def expert_kernel(x_ref, up_ref, down_ref, out_ref, units_ref):
    for part in chunks(up_ref.shape[2]):
        units_ref[:, part] = jax.nn.gelu(
            jnp.dot(x_ref[...], up_ref[0, :, part], preferred_element_type=F32), approximate=True
        ).astype(BF16)
    for part in chunks(out_ref.shape[1]):
        out_ref[:, part] = jnp.dot(
            units_ref[...], down_ref[0, :, part], preferred_element_type=F32
        ).astype(BF16)


def chunks(width):
    step = next(c for c in (1792, 896, LANES) if width % c == 0)
    return [slice(i, i + step) for i in range(0, width, step)]


def expert_slice(inputs, up_weight, down_weight):
    rows, features = inputs.shape
    return pl.pallas_call(
        expert_kernel,
        out_shape=jax.ShapeDtypeStruct((rows, features), BF16),
        in_specs=[VMEM] * 3,
        out_specs=VMEM,
        scratch_shapes=[pltpu.VMEM((rows, up_weight.shape[2]), BF16)],
        compiler_params=pltpu.CompilerParams(vmem_limit_bytes=16 << 20),
        name="experts",
    )(inputs, up_weight, down_weight)


def combine_kernel(hidden_ref, picks_ref, gates_ref, returned_ref, out_ref):
    slices = returned_ref.shape[1]
    slots = returned_ref.shape[0] * returned_ref.shape[2]
    mixed = hidden_ref[...]
    for s in range(slices):
        rows = returned_ref[:, s].reshape(slots, returned_ref.shape[3])
        picked = jnp.dot(picks_ref[...].reshape(-1, slots), rows, preferred_element_type=F32)
        for k in range(TOPK):
            mixed += gates_ref[:, k : k + 1] * picked[k * mixed.shape[0] : (k + 1) * mixed.shape[0]]
    out_ref[...] = mixed.astype(BF16)


def body(
    queries, fresh_keys, fresh_values, stale_keys, stale_values, residual, out_weight, modulation,
    up_weight, down_weight, routes, gates,
):
    rows, features = residual.shape
    patch_count = lax.axis_size("patch")
    device_count = patch_count * lax.axis_size("expert")
    by_heads = queries.shape[1] // HEAD_DIM == patch_count and patch_count % 2 == 0 and lax.axis_size("expert") == 2
    attention = attention_by_heads if by_heads else attention_by_gather
    hidden, buffer, picks, gates = attention(
        queries, fresh_keys, fresh_values, stale_keys, stale_values, out_weight, residual, modulation, routes, gates
    )
    capacity = rows // 4
    slice_count = device_count // EXPERTS
    outgoing = jnp.broadcast_to(
        buffer.reshape(EXPERTS, 1, capacity, features), (EXPERTS, slice_count, capacity, features)
    ).reshape(device_count, capacity, features)
    arrived = lax.all_to_all(outgoing, ("patch", "expert"), split_axis=0, concat_axis=0, tiled=True)
    outputs = expert_slice(arrived.reshape(device_count * capacity, features), up_weight, down_weight)
    returned = lax.all_to_all(
        outputs.reshape(device_count, capacity, features),
        ("patch", "expert"),
        split_axis=0,
        concat_axis=0,
        tiled=True,
    )
    return pl.pallas_call(
        combine_kernel,
        out_shape=jax.ShapeDtypeStruct((rows, features), BF16),
        in_specs=[VMEM] * 4,
        out_specs=VMEM,
        compiler_params=pltpu.CompilerParams(vmem_limit_bytes=20 << 20),
        name="combine",
    )(hidden, picks, gates, returned.reshape(EXPERTS, slice_count, capacity, features))


def solution(mesh):
    tokens = P(("group", "patch"), "expert")
    rows = P(("group", "patch", "expert"), None)
    weight = P(("patch", "expert"), None, None)
    placed = (
        tokens, tokens, tokens, tokens, tokens, rows, P("expert", None), P("group", None), weight, weight, rows, rows,
    )
    return jax.shard_map(body, mesh=mesh, in_specs=placed, out_specs=rows, check_vma=False)
```
